32 devices in a mesh: dp: 4 (over z), seq: 8 (over y, x, core).
Axes of the slice: x: 2, y: 2, z: 4, core: 2. Of those that a mesh axis runs over, the one named last changes fastest.
Arguments:
- tokens: bfloat16 [8, 1024, 1024], P('dp', 'seq'), may hold values from -6 to 6
- variate_ids: int32 [8, 1024], P('dp', 'seq'), may hold values from 0 to 3
- time_ids: int32 [8, 1024], P('dp', 'seq'), may hold values from 0 to 1023
- w_qkv: bfloat16 [2, 1024, 3072], P(None, ('dp', 'seq')), may hold values from -0.1875 to 0.1875
- w_out: bfloat16 [2, 1024, 1024], P(None, ('dp', 'seq')), may hold values from -3.5 to 3.5
- w_in: bfloat16 [2, 1024, 8192], P(None, ('dp', 'seq')), may hold values from -0.1875 to 0.1875
- w_down: bfloat16 [2, 4096, 1024], P(None, ('dp', 'seq')), may hold values from -0.09375 to 0.09375
- norm_gains: float32 [2, 2, 1024], replicated, may hold values from 0.5 to 1.5
- qk_gains: float32 [2, 2, 64], replicated, may hold values from 0.5 to 1.5
- head_bias: float32 [2, 2, 16], replicated, may hold values from -2 to 2
- cotangent: bfloat16 [8, 1024, 1024], P('dp', 'seq'), may hold values from -6 to 6
Outputs:
- layer_out: bfloat16 [8, 1024, 1024], P('dp', 'seq')
- input_grad: float32 [8, 1024, 1024], P('dp', 'seq')
- grad_qkv: float32 [2, 1024, 3072], P(None, ('dp', 'seq'))
- grad_out: float32 [2, 1024, 1024], P(None, ('dp', 'seq'))
- grad_in: float32 [2, 1024, 8192], P(None, ('dp', 'seq'))
- grad_down: float32 [2, 4096, 1024], P(None, ('dp', 'seq'))
- grad_norms: float32 [2, 2, 1024], replicated
- grad_qk: float32 [2, 2, 64], replicated
- grad_bias: float32 [2, 2, 16], replicated
- clipped_qkv: bfloat16 [2, 1024, 3072], P(None, ('dp', 'seq'))
- logit_max: float32 [2, 16], replicated
The draws below stay inside these ranges and needn't reach their ends.
All inputs are finite; a program needn't handle non-finite values.
Results may differ from the reference program's by a relative error of at most 0.022.
Values may be sent and summed in bfloat16 or wider, within the bound.
No kernel may reach another device: no remote copies, remote signals or barrier semaphores. Data moves between devices by JAX's collectives and lax.ppermute only.
A program may use at most 320 MiB of HBM per device.

```python
import math
import jax
import jax.numpy as jnp
from jax import lax

HEADS = 16
HEAD_WIDTH = 64
D = 1024
FF = 4096
LAYERS = 2
LENGTH = 1024
BATCH = 8


def place_ends(entries, key, least, largest):
    spot = [jax.random.randint(jax.random.fold_in(key, axis), (), 0, length) for axis, length in enumerate(entries.shape)]
    longest = entries.shape.index(max(entries.shape))
    next_to = spot[:longest] + [(spot[longest] + 1) % entries.shape[longest]] + spot[longest + 1:]
    return entries.at[tuple(spot)].set(least).at[tuple(next_to)].set(largest)


def levels(key, dims, shards, smallest, largest):
    def one(dim, shards_of):
        steps = jax.random.uniform(jax.random.fold_in(jax.random.fold_in(key, 6), dim), (shards_of,), jnp.float32, smallest / len(shards), largest / len(shards))
        return jnp.repeat(jnp.exp(steps), dims[dim] // shards_of).reshape((-1,) + (1,) * (len(dims) - dim - 1))

    level = one(*shards[0])
    for cut in shards[1:]:
        level = level * one(*cut)
    return level


def bell_draw(rng, extent, scale, bound, split=(), kind=jnp.bfloat16):
    values = jax.random.normal(rng, extent, jnp.float32) * scale
    if len(split) > 0:
        values = levels(rng, extent, split, -0.22, 0.18) * values
    return jnp.clip(values, min=-bound, max=bound).astype(kind)


def setup_inputs(seed: int = 0) -> dict:
    splits = jax.random.split(jax.random.key(seed), 12)
    tokens = bell_draw(splits[0], (BATCH, LENGTH, D), 1.0, 6.0, ((0, 4), (1, 8)))
    variate_ids = place_ends(jax.random.randint(splits[1], (BATCH, LENGTH), 0, 4), jax.random.fold_in(splits[1], 1), 0, 3).astype(jnp.int32)
    time_ids = place_ends(jax.random.randint(splits[2], (BATCH, LENGTH), 0, LENGTH), jax.random.fold_in(splits[2], 1), 0, LENGTH - 1).astype(jnp.int32)
    w_qkv = bell_draw(splits[3], (LAYERS, D, 3 * D), D ** -0.5, 0.1875, ((1, 32),))
    w_out = bell_draw(splits[4], (LAYERS, D, D), (max(1, 3 * D // LENGTH)) ** -0.5, 3.5, ((1, 32),))
    w_in = bell_draw(splits[5], (LAYERS, D, 2 * FF), D ** -0.5, 0.1875, ((1, 32),))
    w_down = bell_draw(splits[6], (LAYERS, FF, D), FF ** -0.5, 0.09375, ((1, 32),))
    norm_gains = jnp.clip(1.0 + 0.1 * jax.random.normal(splits[7], (LAYERS, 2, D), jnp.float32), 0.5, 1.5)
    qk_gains = jnp.clip(1.0 + 0.1 * jax.random.normal(splits[8], (LAYERS, 2, HEAD_WIDTH), jnp.float32), 0.5, 1.5)
    head_bias = jnp.clip(jax.random.uniform(splits[9], (LAYERS, 2, HEADS), jnp.float32, -2.0, 2.0), -2.0, 2.0)
    cotangent = bell_draw(splits[10], (BATCH, LENGTH, D), 1.0, 6.0, ((0, 4), (1, 8)))
    return {"tokens": tokens, "variate_ids": variate_ids, "time_ids": time_ids, "w_qkv": w_qkv, "w_out": w_out, "w_in": w_in, "w_down": w_down, "norm_gains": norm_gains, "qk_gains": qk_gains, "head_bias": head_bias, "cotangent": cotangent}


EPSILON = 1e-05
CLIP_LIMIT = 2.0
FLOOR_VALUE = -1e+30
HIGHEST_PRECISION = lax.Precision.HIGHEST

@jax.custom_vjp
def low(v):
    return lax.optimization_barrier(v.astype(jnp.bfloat16)).astype(jnp.float32)

@jax.custom_vjp
def low_back(v):
    return v

def low_keep(v):
    return (low(v), None)

def low_pass(kept, grad):
    return (grad,)

def back_keep(v):
    return (v, None)

def back_low(kept, grad):
    return (low(grad),)
low.defvjp(low_keep, low_pass)
low_back.defvjp(back_keep, back_low)

def rms_scale(values, gain):
    return values * lax.rsqrt(lax.optimization_barrier(jnp.mean(values * values, axis=-1, keepdims=True)) + EPSILON) * gain

def rotate(values, places):
    half_width = values.shape[-1] // 2
    frequency = jnp.exp(jnp.arange(half_width, dtype=jnp.float32) * (-2.0 * math.log(10000.0) / values.shape[-1]))
    angles = places.astype(jnp.float32)[..., None] * frequency
    cosine = jnp.cos(angles)
    sine = jnp.sin(angles)
    front_part = values[..., :half_width]
    back_part = values[..., half_width:]
    return jnp.concatenate([front_part * cosine - back_part * sine, back_part * cosine + front_part * sine], axis=-1)

def attend(query, key_rows, value_portion, key_ids, bias_pair):
    head_count, length, head_size = query.shape
    block_rows = min(512, length)
    score_scale = 1.0 / math.sqrt(head_size)

    def one_block(offset):
        block_queries = lax.dynamic_slice_in_dim(query, offset, block_rows, 1)
        block_ids = lax.dynamic_slice_in_dim(key_ids, offset, block_rows, 0)
        matches = block_ids[:, None] == key_ids[None, :]
        bias_terms = jnp.where(matches[None], bias_pair[0][:, None, None], bias_pair[1][:, None, None])
        scores = low_back(jnp.einsum('hqd,hkd->hqk', block_queries, key_rows, precision=HIGHEST_PRECISION) * score_scale + bias_terms)
        attention_probs = low(jax.nn.softmax(scores, axis=-1))
        attended = jnp.einsum('hqk,hkd->hqd', attention_probs, value_portion, precision=HIGHEST_PRECISION)
        return (attended, lax.optimization_barrier(jnp.max(scores, axis=(1, 2))))
    offsets = jnp.arange(length // block_rows, dtype=jnp.int32) * block_rows
    attended, block_tops = lax.map(jax.checkpoint(one_block), offsets)
    attended = jnp.transpose(attended, (1, 0, 2, 3)).reshape(head_count, length, head_size)
    return (attended, lax.optimization_barrier(jnp.max(block_tops, axis=0)))

def run_layer(state, key_ids, places, layer_params):
    matrix_qkv, matrix_out, matrix_in, matrix_down, norm_pair, qk_pair, bias_pair = layer_params
    length, model_width = state.shape
    head_count = bias_pair.shape[1]
    head_size = model_width // head_count
    hidden_units = matrix_down.shape[0]
    normed = low(rms_scale(state, norm_pair[0]))
    mixed = low_back(low(jnp.dot(normed, matrix_qkv, precision=HIGHEST_PRECISION)))
    mixed = mixed.reshape(length, 3, head_count, head_size).transpose(1, 2, 0, 3)
    query = low(rotate(rms_scale(mixed[0], qk_pair[0]), places))
    key_rows = low(rotate(rms_scale(mixed[1], qk_pair[1]), places))
    attended, head_tops = attend(query, key_rows, mixed[2], key_ids, bias_pair)
    attended = low_back(low(attended)).transpose(1, 0, 2).reshape(length, model_width)
    middle = state + low_back(jnp.dot(attended, matrix_out, precision=HIGHEST_PRECISION))
    second = low(rms_scale(middle, norm_pair[1]))
    joined = low_back(jnp.dot(second, matrix_in, precision=HIGHEST_PRECISION))
    gated = low(jax.nn.silu(joined[:, :hidden_units]) * joined[:, hidden_units:])
    state = middle + low_back(jnp.dot(gated, matrix_down, precision=HIGHEST_PRECISION))
    return (state, head_tops)

def reference(tokens, variate_ids, time_ids, w_qkv, w_out, w_in, w_down, norm_gains, qk_gains, head_bias, cotangent):
    params = (w_qkv.astype(jnp.float32), w_out.astype(jnp.float32), w_in.astype(jnp.float32), w_down.astype(jnp.float32), norm_gains, qk_gains, head_bias)
    layers = w_qkv.shape[0]
    head_count = head_bias.shape[2]
    model_width = w_qkv.shape[1]

    def forward(state, weights, key_ids, places):
        layer_tops = []
        for layer_index in range(layers):
            state, head_tops = run_layer(state, key_ids, places, tuple((part[layer_index] for part in weights)))
            layer_tops.append(head_tops)
        return (state, jnp.stack(layer_tops))

    def per_sequence(running, item):
        grads, best = running
        sequence, key_ids, places, seed_grad = item
        result, pull, seq_tops = jax.vjp(lambda state, weights: forward(state, weights, key_ids, places), sequence.astype(jnp.float32), params, has_aux=True)
        sequence_grad, weight_grads = pull(seed_grad.astype(jnp.float32))
        grads = jax.tree.map(jnp.add, grads, weight_grads)
        return ((grads, jnp.maximum(best, seq_tops)), (result.astype(jnp.bfloat16), sequence_grad))
    start_state = (jax.tree.map(jnp.zeros_like, params), jnp.full((layers, head_count), FLOOR_VALUE, jnp.float32))
    (grads, best), (outputs, input_grads) = lax.scan(per_sequence, start_state, (tokens, variate_ids, time_ids, cotangent))
    head_size = model_width // head_count
    factor = jnp.sqrt(CLIP_LIMIT / jnp.maximum(best, CLIP_LIMIT))
    spread = jnp.repeat(factor, head_size, axis=1)
    column_scale = jnp.concatenate([spread, spread, jnp.ones((layers, model_width), jnp.float32)], axis=1)
    clipped = (w_qkv.astype(jnp.float32) * column_scale[:, None, :]).astype(jnp.bfloat16)
    return (outputs, input_grads, grads[0], grads[1], grads[2], grads[3], grads[4], grads[5], grads[6], clipped, best)
```

```python
import math

import jax
import jax.numpy as jnp
from jax import lax
from jax.sharding import PartitionSpec as P

EPSILON = 1e-05
CLIP_LIMIT = 2.0
FLOOR_VALUE = -1e30
BF = jnp.bfloat16
F32 = jnp.float32


def rms_scale(values, gain):
    return values * lax.rsqrt(jnp.mean(values * values, axis=-1, keepdims=True) + EPSILON) * gain


def swiglu(joined):
    hidden_units = joined.shape[-1] // 2
    return jax.nn.silu(joined[:, :hidden_units]) * joined[:, hidden_units:]


def dot(a, b):
    return jnp.dot(a, b, preferred_element_type=F32)


def dot_nt(a, b):
    return lax.dot_general(a, b, (((1,), (1,)), ((), ())), preferred_element_type=F32)


def dot_tn(a, b):
    return lax.dot_general(a, b, (((0,), (0,)), ((), ())), preferred_element_type=F32)


def pick(array, index, axis=0):
    return lax.dynamic_index_in_dim(array, index, axis, keepdims=False)


class Net:
    def __init__(self, dp_n, seq_n, sequences):
        self.dp_n, self.seq_n = dp_n, seq_n
        self.hi_n = sequences
        self.lo_n = seq_n // sequences
        seq = lax.axis_index("seq")
        self.lo = seq % self.lo_n
        self.hi = seq // self.lo_n
        self.dp = lax.axis_index("dp")
        self.lo_bits = [1 << b for b in range(self.lo_n.bit_length() - 1)]
        self.hi_bits = [1 << b for b in range(self.hi_n.bit_length() - 1)]

    def swap_lo(self, x, bit):
        return lax.ppermute(x, "seq", [(i, i ^ bit) for i in range(self.seq_n)])

    def swap_hi(self, x, bit):
        return self.swap_lo(x, bit * self.lo_n)

    def swap_dp(self, x, bit):
        return lax.ppermute(x, "dp", [(i, i ^ bit) for i in range(self.dp_n)])

    def next_dp(self, x):
        return lax.ppermute(x, "dp", [(i, (i + 1) % self.dp_n) for i in range(self.dp_n)])

    def gather_lo(self, block):
        blocks = {0: block}
        for bit in reversed(self.lo_bits):
            for r in list(blocks):
                blocks[r | bit] = self.swap_lo(blocks[r], bit)
        return [blocks[r] for r in range(self.lo_n)]

    def scatter_lo(self, blocks):
        blocks = dict(enumerate(blocks))
        for bit in self.lo_bits:
            blocks = {
                r: blocks[r].astype(F32) + self.swap_lo(blocks[r | bit].astype(BF), bit).astype(F32)
                for r in sorted(blocks, reverse=True)
                if not r & bit
            }
        return blocks[0]

    def trade(self, blocks, bits, swap):
        blocks = list(blocks)
        for bit in reversed(bits):
            for r in range(len(blocks)):
                if r & bit:
                    blocks[r] = swap(blocks[r], bit)
        return blocks

    def trade_lo(self, blocks):
        return self.trade(blocks, self.lo_bits, self.swap_lo)

    def trade_hi(self, blocks):
        return self.trade(blocks, self.hi_bits, self.swap_hi)

    def all_small(self, x, combine):
        for bit in self.lo_bits:
            x = combine(x, self.swap_lo(x, bit))
        for bit in self.hi_bits:
            x = combine(x, self.swap_hi(x, bit))
        bit = 1
        while bit < self.dp_n:
            x = combine(x, self.swap_dp(x, bit))
            bit *= 2
        return x

    def gather_rows(self, own):
        full = jnp.zeros((self.dp_n, self.hi_n) + own.shape, own.dtype)
        chunk = own
        for step in range(self.dp_n):
            if step:
                chunk = self.next_dp(chunk)
            source = (self.dp - step) % self.dp_n
            blocks = {0: chunk}
            for bit in self.hi_bits:
                for q in list(blocks):
                    blocks[q | bit] = self.swap_hi(blocks[q], bit)
            for q, block in blocks.items():
                start = (source, self.hi ^ q) + (0,) * own.ndim
                full = lax.dynamic_update_slice(full, block[None, None], start)
        return full

    def scatter_rows(self, full):
        blocks = {q: pick(full, self.hi ^ q, 1) for q in range(self.hi_n)}
        for bit in self.hi_bits:
            blocks = {
                q: blocks[q] + self.swap_hi(blocks[q | bit].astype(BF), bit).astype(F32)
                for q in blocks
                if not q & bit
            }
        mine = blocks[0]
        running = pick(mine, (self.dp - 1) % self.dp_n)
        for step in range(1, self.dp_n):
            running = self.next_dp(running.astype(BF)).astype(F32)
            running = running + pick(mine, (self.dp - 1 - step) % self.dp_n)
        return running


def fetch_columns(net, shard, width):
    rows, parts = shard.shape[:2]
    blocks = [pick(shard, net.lo ^ r, 2).reshape(rows, parts * width) for r in range(net.lo_n)]
    blocks = net.trade_lo(blocks)
    own = jnp.zeros((net.lo_n,) + blocks[0].shape, BF)
    for r, block in enumerate(blocks):
        own = lax.dynamic_update_slice(own, block[None], (net.lo ^ r, 0, 0))
    own = own.reshape(net.lo_n * rows, parts * width)
    full = net.gather_rows(own)
    return full.reshape(-1, parts * width)


def scatter_columns(net, grad, rows, parts, width):
    grad = grad.reshape(net.dp_n, net.hi_n, net.lo_n * rows, parts * width)
    own = net.scatter_rows(grad).reshape(net.lo_n, rows, parts * width).astype(BF)
    blocks = net.trade_lo([pick(own, net.lo ^ r) for r in range(net.lo_n)])
    shard = jnp.zeros((rows, parts, net.lo_n, width), F32)
    for r, block in enumerate(blocks):
        block = block.astype(F32).reshape(rows, parts, 1, width)
        shard = lax.dynamic_update_slice(shard, block, (0, 0, net.lo ^ r, 0))
    return shard.reshape(rows, parts * net.lo_n * width)


def fetch_hidden(net, shard):
    return net.gather_rows(shard).reshape(-1, shard.shape[-1])


def scatter_hidden(net, grad, rows):
    return net.scatter_rows(grad.reshape(net.dp_n, net.hi_n, rows, -1))


def fetch_whole(net, shard):
    own = net.gather_rows(shard)
    parts = net.gather_lo(own)
    full = jnp.zeros((net.dp_n, net.hi_n, net.lo_n) + shard.shape, BF)
    for r, part in enumerate(parts):
        full = lax.dynamic_update_slice(full, part[:, :, None], (0, 0, net.lo ^ r, 0, 0))
    return full.reshape(-1, shard.shape[-1])


def scatter_whole(net, grad, rows):
    grad = grad.reshape(net.dp_n, net.hi_n, net.lo_n, rows, -1)
    own = net.scatter_lo([pick(grad, net.lo ^ r, 2) for r in range(net.lo_n)])
    return net.scatter_rows(own)


def rotate(values, cosine, sine):
    half_width = values.shape[-1] // 2
    front_part = values[..., :half_width]
    back_part = values[..., half_width:]
    return jnp.concatenate(
        [front_part * cosine - back_part * sine, back_part * cosine + front_part * sine], axis=-1
    )


def layer_scores(block_queries, key_rows, block_ids, key_ids, bias_pair, score_scale):
    scores = (
        jnp.einsum("pgl,pfl->pgf", block_queries, key_rows, preferred_element_type=F32)
        * score_scale
    )
    matches = (block_ids[:, None] == key_ids[None, :])[None]
    bias_terms = jnp.where(matches, bias_pair[0][:, None, None], bias_pair[1][:, None, None])
    return (scores + bias_terms, matches)


def attend_forward(query, key_rows, value_portion, key_ids, bias_pair):
    heads, length, head_size = query.shape
    block_rows = min(512, length)
    score_scale = 1.0 / math.sqrt(head_size)

    def one_block(offset):
        block_queries = lax.dynamic_slice_in_dim(query, offset, block_rows, 1)
        block_ids = lax.dynamic_slice_in_dim(key_ids, offset, block_rows, 0)
        scores, matches = layer_scores(
            block_queries, key_rows, block_ids, key_ids, bias_pair, score_scale
        )
        row_top = jnp.max(scores, axis=-1)
        exponent = jnp.exp(scores - row_top[..., None])
        row_total = jnp.sum(exponent, axis=-1)
        attention_probs = (exponent / row_total[..., None]).astype(BF)
        attended = jnp.einsum(
            "gpm,gmv->gpv", attention_probs, value_portion, preferred_element_type=F32
        )
        return (
            attended.astype(BF),
            row_top + jnp.log(row_total),
            jnp.max(row_top, axis=-1),
        )

    offsets = jnp.arange(length // block_rows, dtype=jnp.int32) * block_rows
    attended, log_total, block_tops = lax.map(one_block, offsets)
    attended = jnp.transpose(attended, (1, 0, 2, 3)).reshape(heads, length, head_size)
    log_total = jnp.transpose(log_total, (1, 0, 2)).reshape(heads, length)
    return (attended, log_total, jnp.max(block_tops, axis=0))


def attend_backward(query, key_rows, value_portion, key_ids, bias_pair, log_total, grad_attended):
    heads, length, head_size = query.shape
    block_rows = min(512, length)
    score_scale = 1.0 / math.sqrt(head_size)

    def one_block(running, offset):
        grad_keys, grad_values, grad_match, grad_other = running
        block_queries = lax.dynamic_slice_in_dim(query, offset, block_rows, 1)
        block_ids = lax.dynamic_slice_in_dim(key_ids, offset, block_rows, 0)
        block_total = lax.dynamic_slice_in_dim(log_total, offset, block_rows, 1)
        block_gradient = lax.dynamic_slice_in_dim(grad_attended, offset, block_rows, 1)
        scores, matches = layer_scores(
            block_queries, key_rows, block_ids, key_ids, bias_pair, score_scale
        )
        attention_probs = jnp.exp(scores - block_total[..., None])
        grad_prob = jnp.einsum(
            "pgl,pfl->pgf", block_gradient, value_portion, preferred_element_type=F32
        )
        grad_scores = attention_probs * (
            grad_prob - jnp.sum(attention_probs * grad_prob, axis=-1, keepdims=True)
        )
        low_scores = grad_scores.astype(BF)
        grad_match = grad_match + jnp.sum(
            jnp.where(matches, low_scores, 0.0).astype(F32), axis=(1, 2)
        )
        grad_other = grad_other + jnp.sum(
            jnp.where(matches, 0.0, low_scores).astype(F32), axis=(1, 2)
        )
        grad_query = (
            jnp.einsum("gpm,gmv->gpv", low_scores, key_rows, preferred_element_type=F32)
            * score_scale
        )
        grad_keys = (
            grad_keys
            + jnp.einsum("sla,sle->sae", low_scores, block_queries, preferred_element_type=F32)
            * score_scale
        )
        grad_values = grad_values + jnp.einsum(
            "sla,sle->sae",
            attention_probs.astype(BF),
            block_gradient,
            preferred_element_type=F32,
        )
        return ((grad_keys, grad_values, grad_match, grad_other), grad_query)

    offsets = jnp.arange(length // block_rows, dtype=jnp.int32) * block_rows
    zero_field = jnp.zeros((heads, length, head_size), F32)
    zero_heads = jnp.zeros((heads,), F32)
    running, grad_query = lax.scan(
        one_block, (zero_field, zero_field, zero_heads, zero_heads), offsets
    )
    grad_query = jnp.transpose(grad_query, (1, 0, 2, 3)).reshape(heads, length, head_size)
    return (grad_query, running[0], running[1], running[2], running[3])


def halves(blocks):
    cut = max(1, len(blocks) // 2)
    parts = [blocks[:cut], blocks[cut:]]
    return [jnp.concatenate(part, axis=0) for part in parts if part]


def split_rows(parts, count):
    each = count // len(parts)
    blocks = []
    for part in parts:
        blocks += jnp.split(part, each, axis=0)
    return blocks


def shards(
    tokens,
    variate_ids,
    time_ids,
    w_qkv,
    w_out,
    w_in,
    w_down,
    norm_gains,
    qk_gains,
    head_bias,
    cotangent,
):
    sequences, tok_dev, width = tokens.shape
    layers = w_qkv.shape[0]
    heads = head_bias.shape[2]
    head_size = qk_gains.shape[2]
    hidden = w_in.shape[2] // 2
    net = Net(lax.axis_size("dp"), lax.axis_size("seq"), sequences)
    lo_n = net.lo_n
    rows = sequences * tok_dev
    local_heads = heads // lo_n
    local_width = local_heads * head_size
    length = rows * lo_n
    head_start = net.lo * local_heads
    unit = w_down.shape[1]

    def to_groups(x):
        return jnp.concatenate(
            net.trade_hi([pick(x, net.hi ^ q) for q in range(sequences)]), axis=0
        )

    def to_devices(x):
        blocks = net.trade_hi(jnp.split(x, sequences, axis=0))
        out = jnp.zeros((sequences, tok_dev) + x.shape[1:], x.dtype)
        for q, block in enumerate(blocks):
            out = lax.dynamic_update_slice(out, block[None], (net.hi ^ q,) + (0,) * x.ndim)
        return out

    state = to_groups(tokens).astype(F32)
    pair = to_groups(jnp.stack([variate_ids, time_ids], axis=-1))
    pair = jnp.concatenate(net.gather_lo(pair), axis=0)
    key_ids, places = pair[:, 0], pair[:, 1]
    frequency = jnp.exp(
        jnp.arange(head_size // 2, dtype=F32) * (-2.0 * math.log(10000.0) / head_size)
    )
    angles = places.astype(F32)[:, None] * frequency
    cosine, sine = jnp.cos(angles), jnp.sin(angles)

    def head_prep(raw, gain):
        return rotate(rms_scale(raw, gain), cosine, sine)

    weights = []
    for layer in range(layers):
        rows_w = w_qkv.shape[1]
        weights.append(
            (
                fetch_columns(
                    net, w_qkv[layer].reshape(rows_w, 3, lo_n, local_width), local_width
                ),
                fetch_whole(net, w_out[layer]),
                fetch_columns(
                    net,
                    w_in[layer]
                    .reshape(rows_w, 2 * net.dp_n * net.hi_n, lo_n, unit),
                    unit,
                ),
                fetch_hidden(net, w_down[layer]),
            )
        )

    saved = []
    best_scores = jnp.full((layers, heads), FLOOR_VALUE, F32)
    for layer in range(layers):
        m_qkv, m_out, m_in, m_down = weights[layer]
        layer_in = state
        normed = rms_scale(layer_in, norm_gains[layer, 0]).astype(BF)
        normed_halves = halves(net.gather_lo(normed))
        mixed = jnp.concatenate([dot(part, m_qkv).astype(BF) for part in normed_halves], axis=0)
        raw = mixed.reshape(length, 3, local_heads, head_size).transpose(1, 2, 0, 3)
        query, query_pull = jax.vjp(head_prep, raw[0].astype(F32), qk_gains[layer, 0])
        keys, key_pull = jax.vjp(head_prep, raw[1].astype(F32), qk_gains[layer, 1])
        query, keys, values = query.astype(BF), keys.astype(BF), raw[2]
        bias_pair = lax.dynamic_slice_in_dim(head_bias[layer], head_start, local_heads, 1)
        attended, log_total, head_tops = attend_forward(query, keys, values, key_ids, bias_pair)
        best_scores = lax.dynamic_update_slice(
            best_scores, head_tops[None, :], (jnp.int32(layer), head_start)
        )
        attended = attended.transpose(1, 0, 2).reshape(length, local_width)
        arrived = net.trade_lo(jnp.split(attended, lo_n, axis=0))
        returned = jnp.zeros((rows, width), BF)
        for r, block in enumerate(arrived):
            returned = lax.dynamic_update_slice(returned, block, (0, (net.lo ^ r) * local_width))
        middle = layer_in + dot(returned, m_out)
        second = rms_scale(middle, norm_gains[layer, 1]).astype(BF)
        second_halves = halves(net.gather_lo(second))
        joined = [dot(part, m_in) for part in second_halves]
        gated = [swiglu(part).astype(BF) for part in joined]
        partial = [dot(part, m_down).astype(BF) for part in gated]
        state = middle + net.scatter_lo(split_rows(partial, lo_n))
        saved.append(
            (
                layer_in,
                normed_halves,
                query,
                keys,
                values,
                query_pull,
                key_pull,
                bias_pair,
                log_total,
                returned,
                middle,
                second_halves,
                joined,
                gated,
            )
        )
    best_scores = net.all_small(best_scores, jnp.maximum)
    layer_out = to_devices(state.astype(BF))

    gradient = to_groups(cotangent).astype(F32)
    qkv_parts = [None] * layers
    out_parts = [None] * layers
    in_parts = [None] * layers
    down_parts = [None] * layers
    norm_parts = [None] * layers
    qk_parts = [None] * layers
    bias_parts = [None] * layers
    for layer in reversed(range(layers)):
        m_qkv, m_out, m_in, m_down = weights[layer]
        (
            layer_in,
            normed_halves,
            query,
            keys,
            values,
            query_pull,
            key_pull,
            bias_pair,
            log_total,
            returned,
            middle,
            second_halves,
            joined,
            gated,
        ) = saved[layer]
        down_halves = halves(net.gather_lo(gradient.astype(BF)))
        grad_joined = []
        partial = []
        for part, joined_part in zip(down_halves, joined):
            grad_gated = dot_nt(part, m_down)
            unused, pull = jax.vjp(swiglu, joined_part)
            grad_joined.append(pull(grad_gated)[0].astype(BF))
            partial.append(dot_nt(grad_joined[-1], m_in).astype(BF))
        grad_second = net.scatter_lo(split_rows(partial, lo_n))
        grad_down = dot_tn(jnp.concatenate(gated, axis=0), jnp.concatenate(down_halves, axis=0))
        grad_in = dot_tn(
            jnp.concatenate(second_halves, axis=0), jnp.concatenate(grad_joined, axis=0)
        )
        down_parts[layer] = scatter_hidden(net, grad_down, unit)
        in_parts[layer] = scatter_columns(
            net, grad_in, w_in.shape[1], 2 * net.dp_n * net.hi_n, unit
        )
        unused, second_pull = jax.vjp(rms_scale, middle, norm_gains[layer, 1])
        grad_middle, gain_second = second_pull(grad_second)
        gradient = gradient + grad_middle
        branch = gradient.astype(BF)
        grad_returned = dot_nt(branch, m_out).astype(BF)
        grad_out = dot_tn(returned, branch)
        out_parts[layer] = scatter_whole(net, grad_out, w_out.shape[1])
        leaving = [
            lax.dynamic_slice_in_dim(grad_returned, (net.lo ^ r) * local_width, local_width, 1)
            for r in range(lo_n)
        ]
        grad_heads = jnp.concatenate(net.trade_lo(leaving), axis=0)
        grad_heads = grad_heads.reshape(length, local_heads, head_size).transpose(1, 0, 2)
        grad_query, grad_keys, grad_values, grad_match, grad_other = attend_backward(
            query, keys, values, key_ids, bias_pair, log_total, grad_heads
        )
        grad_qraw, gain_query = query_pull(grad_query)
        grad_kraw, gain_key = key_pull(grad_keys)
        grad_mixed = jnp.stack([grad_qraw, grad_kraw, grad_values]).astype(BF)
        grad_mixed = grad_mixed.transpose(2, 0, 1, 3).reshape(length, 3 * local_width)
        partial = [dot_nt(part, m_qkv).astype(BF) for part in jnp.split(grad_mixed, 2, axis=0)]
        grad_normed = net.scatter_lo(split_rows(partial, lo_n))
        grad_qkv = dot_tn(jnp.concatenate(normed_halves, axis=0), grad_mixed)
        qkv_parts[layer] = scatter_columns(net, grad_qkv, w_qkv.shape[1], 3, local_width)
        unused, first_pull = jax.vjp(rms_scale, layer_in, norm_gains[layer, 0])
        grad_layer_in, gain_first = first_pull(grad_normed)
        gradient = gradient + grad_layer_in
        norm_parts[layer] = jnp.stack([gain_first, gain_second])
        qk_parts[layer] = jnp.stack([gain_query, gain_key])
        bias_parts[layer] = lax.dynamic_update_slice(
            jnp.zeros((2, heads), F32),
            jnp.stack([grad_match, grad_other]),
            (jnp.int32(0), head_start),
        )
    input_grad = to_devices(gradient)
    small = jnp.concatenate(
        [jnp.stack(part).reshape(-1) for part in (norm_parts, qk_parts, bias_parts)]
    )
    small = net.all_small(small, jnp.add)
    cut_norm, cut_qk = norm_gains.size, norm_gains.size + qk_gains.size
    norm_sum = small[:cut_norm].reshape(norm_gains.shape)
    qk_sum = small[cut_norm:cut_qk].reshape(qk_gains.shape)
    bias_sum = small[cut_qk:].reshape(head_bias.shape)

    factor = jnp.sqrt(CLIP_LIMIT / jnp.maximum(best_scores, CLIP_LIMIT))
    spread = jnp.repeat(factor, head_size, axis=1)
    column_scale = jnp.concatenate([spread, spread, jnp.ones((layers, width), F32)], axis=1)
    clipped = (w_qkv.astype(F32) * column_scale[:, None, :]).astype(BF)
    return (
        layer_out,
        input_grad,
        jnp.stack(qkv_parts),
        jnp.stack(out_parts),
        jnp.stack(in_parts),
        jnp.stack(down_parts),
        norm_sum,
        qk_sum,
        bias_sum,
        clipped,
        best_scores,
    )


def solution(mesh):
    in_specs = (
        P("dp", "seq", None),
        P("dp", "seq"),
        P("dp", "seq"),
        P(None, ("dp", "seq"), None),
        P(None, ("dp", "seq"), None),
        P(None, ("dp", "seq"), None),
        P(None, ("dp", "seq"), None),
        P(),
        P(),
        P(),
        P("dp", "seq", None),
    )
    out_specs = (
        P("dp", "seq", None),
        P("dp", "seq", None),
        P(None, ("dp", "seq"), None),
        P(None, ("dp", "seq"), None),
        P(None, ("dp", "seq"), None),
        P(None, ("dp", "seq"), None),
        P(),
        P(),
        P(),
        P(None, ("dp", "seq"), None),
        P(),
    )
    return jax.shard_map(shards, mesh=mesh, in_specs=in_specs, out_specs=out_specs, check_vma=False)
```

```python
import functools
import math

import jax
import jax.numpy as jnp
from jax import lax
from jax.experimental import pallas as pl
from jax.experimental.pallas import tpu as pltpu
from jax.sharding import Mesh
from jax.sharding import PartitionSpec as P

EPSILON = 1e-05
CLIP_LIMIT = 2.0
FLOOR_VALUE = -1e30
BF = jnp.bfloat16
F32 = jnp.float32


def rms_scale(values, gain):
    return values * lax.rsqrt(jnp.mean(values * values, axis=-1, keepdims=True) + EPSILON) * gain


def dot(a, b):
    return jnp.dot(a, b, preferred_element_type=F32)


def pick(array, index, axis=0):
    return lax.dynamic_index_in_dim(array, index, axis, keepdims=False)


class Net:
    def __init__(self):
        self.dp_n, self.hi_n, self.lo_n = (lax.axis_size(name) for name in ("dp", "hi", "lo"))
        self.dp, self.hi, self.lo = (lax.axis_index(name) for name in ("dp", "hi", "lo"))
        self.seq_n = self.hi_n * self.lo_n
        self.seq = self.hi * self.lo_n + self.lo
        self.seq_bits = [1 << b for b in range(self.seq_n.bit_length() - 1)]
        self.lo_bits = [b for b in self.seq_bits if b < self.lo_n]
        self.hi_bits = [b // self.lo_n for b in self.seq_bits if b >= self.lo_n]
        self.chains = {"dp": [], "hi": []}

    def queued(self, name, send, x, depth=2):
        chain = self.chains[name]
        if len(chain) >= depth:
            x = after(x, chain[-depth])
        chain.append(send(x))
        return chain[-1]

    def swap(self, x, bit):
        if bit < self.lo_n:
            return lax.ppermute(x, "lo", [(i, i ^ bit) for i in range(self.lo_n)])
        bit //= self.lo_n
        return lax.ppermute(x, "hi", [(i, i ^ bit) for i in range(self.hi_n)])

    def swap_hi(self, x, bit):
        return self.swap(x, bit * self.lo_n)

    def swap_dp(self, x, bit):
        return lax.ppermute(x, "dp", [(i, i ^ bit) for i in range(self.dp_n)])

    def next_dp(self, x):
        return lax.ppermute(x, "dp", [(i, (i + 1) % self.dp_n) for i in range(self.dp_n)])

    def gather(self, block, bits):
        blocks = {0: block}
        if len(bits) == 3:
            core, first, second = bits
            half = block.shape[0] // 2
            blocks[first], blocks[second] = self.swap(block, first), self.swap(block, second)
            corner = (
                self.swap(blocks[first][:half], second),
                self.swap(blocks[second][half:], first),
            )
            blocks[first | second] = jnp.concatenate(corner, axis=0)
            for r in list(blocks):
                blocks[r | core] = self.swap(blocks[r], core)
        else:
            for bit in reversed(bits):
                for r in list(blocks):
                    blocks[r | bit] = self.swap(blocks[r], bit)
        return [blocks[r] for r in range(len(blocks))]

    def add_swapped(self, mine, sent, bit):
        return mine.astype(F32) + self.swap(sent.astype(BF), bit).astype(F32)

    def scatter(self, blocks, bits):
        if len(bits) == 3:
            core, first, second = bits
            half = blocks[0].shape[0] // 2
            order = (first | second, first, second, 0)
            sums = {r: self.add_swapped(blocks[r], blocks[r | core], core) for r in order}
            corner = sums[first | second]
            top = self.add_swapped(sums[second][:half], corner[:half], first)
            bottom = self.add_swapped(sums[first][half:], corner[half:], second)
            to_second = jnp.concatenate([top, sums[second][half:]], axis=0)
            to_first = jnp.concatenate([sums[first][:half], bottom], axis=0)
            total = self.add_swapped(sums[0], to_first, first)
            return self.add_swapped(total, to_second, second)
        blocks = dict(enumerate(blocks))
        for bit in bits:
            blocks = {
                r: self.add_swapped(blocks[r], blocks[r | bit], bit)
                for r in sorted(blocks, reverse=True)
                if not r & bit
            }
        return blocks[0]

    def trade(self, blocks, bits):
        blocks = dict(enumerate(blocks))
        rows = blocks[0].shape[0]
        for bit in reversed(bits):
            moving = [r for r in blocks if r & bit]
            if bit == 1:
                for r in moving:
                    blocks[r] = self.swap(blocks[r], bit)
            else:
                sent = self.swap(jnp.concatenate([blocks[r] for r in moving], axis=0), bit)
                for n, r in enumerate(moving):
                    blocks[r] = sent[n * rows : (n + 1) * rows]
        return [blocks[r] for r in range(len(blocks))]

    def trade_hi(self, blocks):
        blocks = list(blocks)
        for bit in self.hi_bits:
            blocks = [self.swap_hi(b, bit) if q & bit else b for q, b in enumerate(blocks)]
        return blocks

    def all_small(self, x, combine):
        for bit in self.seq_bits:
            x = combine(x, self.swap(x, bit))
        bit = 1
        while bit < self.dp_n:
            x = combine(x, self.swap_dp(x, bit))
            bit *= 2
        return x

    def gather_rows(self, own):
        full = place_first(own, self.dp_n * self.hi_n, self.dp * self.hi_n + self.hi)
        full = full.reshape((self.dp_n, self.hi_n) + own.shape)
        chunk = own
        for step in range(self.dp_n):
            if step:
                chunk = self.queued("dp", self.next_dp, chunk)
            source = (self.dp - step) % self.dp_n
            blocks = {0: chunk}
            for bit in self.hi_bits:
                for q in list(blocks):
                    blocks[q | bit] = self.queued(
                        "hi", lambda x, bit=bit: self.swap_hi(x, bit), blocks[q]
                    )
            for q, block in blocks.items():
                if step or q:
                    start = (source, self.hi ^ q) + (0,) * own.ndim
                    full = lax.dynamic_update_slice(full, block[None, None], start)
        return full

    def scatter_rows(self, mine, other):
        mine = self.add_swapped(mine, other, self.lo_n)
        running = pick(mine, (self.dp - 1) % self.dp_n)
        for step in range(1, self.dp_n):
            running = self.next_dp(running.astype(BF)).astype(F32)
            running = running + pick(mine, (self.dp - 1 - step) % self.dp_n)
        return running


def after(x, *earlier):
    return lax.optimization_barrier((x,) + earlier)[0]


def in_order(blocks, index):
    stacked = jnp.stack(blocks)
    return jnp.stack([pick(stacked, index ^ j) for j in range(len(blocks))])


def place_first(block, count, position):
    def kernel(at, block_ref, out_ref):
        out_ref[0] = block_ref[...]

    zeros = (0,) * block.ndim
    return pl.pallas_call(
        kernel,
        grid_spec=pltpu.PrefetchScalarGridSpec(
            num_scalar_prefetch=1,
            grid=(1,),
            in_specs=[pl.BlockSpec(block.shape, lambda i, at: zeros)],
            out_specs=pl.BlockSpec((1,) + block.shape, lambda i, at: (at[0],) + zeros),
        ),
        out_shape=jax.ShapeDtypeStruct((count,) + block.shape, block.dtype),
        name="place_first",
    )(position.astype(jnp.int32).reshape(1), block)


def split_columns(shard, index, count, width):
    rows = shard.shape[0]
    parts = shard.shape[1] // count // width
    if width % LANES:
        shard = shard.reshape(rows, parts, count, width)
        return [pick(shard, index ^ r, 2).reshape(rows, -1) for r in range(count)]

    def kernel(at, shard_ref, *outs):
        for r, out in enumerate(outs):
            for p in range(parts):
                start = pl.multiple_of((p * count + (at[0] ^ r)) * width, width)
                out[:, p * width : (p + 1) * width] = shard_ref[:, pl.ds(start, width)]

    return pl.pallas_call(
        kernel,
        in_specs=[pl.BlockSpec(memory_space=pltpu.SMEM), pl.BlockSpec(memory_space=pltpu.VMEM)],
        out_specs=[pl.BlockSpec(memory_space=pltpu.VMEM)] * count,
        out_shape=[jax.ShapeDtypeStruct((rows, parts * width), BF)] * count,
        name="split_columns",
    )(index.astype(jnp.int32).reshape(1), shard)


def merge_columns(blocks, index, width):
    rows, count = blocks[0].shape[0], len(blocks)
    parts = blocks[0].shape[1] // width
    if width % LANES:
        shard = in_order(blocks, index).reshape(count, rows, parts, width)
        return shard.transpose(1, 2, 0, 3).reshape(rows, -1).astype(F32)

    def kernel(at, *refs):
        out = refs[-1]
        for r, block in enumerate(refs[:-1]):
            for p in range(parts):
                start = pl.multiple_of((p * count + (at[0] ^ r)) * width, width)
                out[:, pl.ds(start, width)] = block[:, p * width : (p + 1) * width].astype(F32)

    return pl.pallas_call(
        kernel,
        in_specs=[pl.BlockSpec(memory_space=pltpu.SMEM)]
        + [pl.BlockSpec(memory_space=pltpu.VMEM)] * count,
        out_specs=pl.BlockSpec(memory_space=pltpu.VMEM),
        out_shape=jax.ShapeDtypeStruct((rows, parts * count * width), F32),
        name="merge_columns",
    )(index.astype(jnp.int32).reshape(1), *blocks)


def trade_columns(net, shard, bits, width):
    index, count = (net.seq, net.seq_n) if bits == net.seq_bits else (net.lo, net.lo_n)
    blocks = net.trade(split_columns(shard, index, count, width), bits)
    return join_rows(blocks, index)


def restore_columns(net, own, bits, width):
    index, count = (net.seq, net.seq_n) if bits == net.seq_bits else (net.lo, net.lo_n)
    own = own.astype(BF).reshape(count, -1, own.shape[1])
    blocks = net.trade([pick(own, index ^ r) for r in range(count)], bits)
    return merge_columns(blocks, index, width)


def fetch_attention(net, own_qkv, own_out):
    rows, cut = own_qkv.shape
    pieces = jnp.split(own_out, rows // own_out.shape[0], axis=1)
    own = jnp.concatenate([own_qkv, jnp.concatenate(pieces, axis=0)], axis=1)
    full = net.gather_rows(own).reshape(-1, rows, own.shape[1])
    blocks = net.gather(full[:, :, cut:], net.lo_bits)
    return full.reshape(-1, own.shape[1]), join_middle(blocks, net.lo, own_out.shape[0])


def fetch_hidden(net, own_in, own_down):
    columns = own_in.shape[1]
    pieces = jnp.split(own_down, own_down.shape[1] // columns, axis=1)
    own = jnp.concatenate([own_in] + pieces, axis=0)
    return lax.all_gather(own, "dp", axis=0)


def scatter_hidden(net, grads, rows_in):
    own = lax.psum_scatter(grads, "dp", scatter_dimension=0)
    own_in, own_down = own[:rows_in], own[rows_in:]
    pieces = rows_in * net.dp_n // grads.shape[2]
    return own_in, jnp.concatenate(jnp.split(own_down, pieces, axis=0), axis=1).astype(F32)


LANES = 128
NT = (((1,), (1,)), ((), ()))
TN = (((0,), (0,)), ((), ()))
VMEM = pl.BlockSpec(memory_space=pltpu.VMEM)
SMEM = pl.BlockSpec(memory_space=pltpu.SMEM)
LIMIT = 24 * 2**20


def on_chip(kernel, outs, *arrays, at=None, scratch=(), flops=0, name=None):
    outs = [jax.ShapeDtypeStruct(*out) for out in outs]
    moved = sum(math.prod(x.shape) * x.dtype.itemsize for x in list(arrays) + outs)
    first = [] if at is None else [at.astype(jnp.int32).reshape(1)]
    return pl.pallas_call(
        kernel,
        in_specs=[SMEM] * len(first) + [VMEM] * len(arrays),
        out_specs=[VMEM] * len(outs),
        out_shape=outs,
        scratch_shapes=list(scratch),
        compiler_params=pltpu.CompilerParams(vmem_limit_bytes=LIMIT),
        cost_estimate=pl.CostEstimate(flops=flops, bytes_accessed=moved, transcendentals=0),
        name=name,
    )(*first, *arrays)


def project(blocks, matrix, columns):
    rows = blocks[0].shape[0]

    def kernel(*refs):
        *ins, m, out = refs
        for n, x in enumerate(ins):
            out[n * rows : (n + 1) * rows, :] = dot(x[...], m[:, :columns]).astype(BF)

    return on_chip(
        kernel,
        [((rows * len(blocks), columns), BF)],
        *blocks,
        matrix,
        flops=2 * rows * len(blocks) * matrix.size,
        name="project",
    )[0]


def out_project(state, arrived, matrix, gain, at):
    rows, width = state.shape
    heads = arrived[0].shape[1]

    def kernel(index, x, m, g, *refs):
        *ins, middle, second = refs
        total = x[...]
        for r, block in enumerate(ins):
            start = pl.multiple_of((index[0] ^ r) * heads, heads)
            total = total + dot(block[...], m[pl.ds(start, heads), :])
        middle[...] = total
        second[...] = rms_scale(total, g[...]).astype(BF)

    return on_chip(
        kernel,
        [((rows, width), F32), ((rows, width), BF)],
        state,
        matrix,
        gain.reshape(1, width),
        *arrived,
        at=at,
        flops=2 * rows * matrix.size,
        name="out_project",
    )


def hidden_matrices(pack, width):
    rows = width // pack.shape[0]
    columns = pack.shape[2]
    down = (pack.shape[1] - rows) * columns // width
    m_in = jnp.concatenate([pack[n, :rows, :] for n in range(pack.shape[0])], axis=0)
    m_down = []
    for n in range(pack.shape[0]):
        starts = range(rows, pack.shape[1], down)
        m_down.append(jnp.concatenate([pack[n, p : p + down, :] for p in starts], axis=1))
    return m_in, jnp.concatenate(m_down, axis=0)


def feed_forward(blocks, pack):
    rows, width = blocks[0].shape
    count, hidden = len(blocks), pack.shape[2] // 2

    def kernel(*refs):
        ins, (m, joined), outs = refs[:count], refs[count : count + 2], refs[count + 2 :]
        m_in, m_down = hidden_matrices(m, width)
        for n, (x, out) in enumerate(zip(ins, outs)):
            both = dot(x[...], m_in)
            joined[n * rows : (n + 1) * rows, :] = both.astype(BF)
            gate, up = both[:, :hidden], both[:, hidden:]
            gated = gate / (1.0 + jnp.exp(-gate)) * up
            out[...] = dot(gated.astype(BF), m_down).astype(BF)

    joined, *parts = on_chip(
        kernel,
        [((rows * count, 2 * hidden), BF)] + [((rows, width), BF)] * count,
        *blocks,
        pack,
        flops=2 * rows * count * pack.size,
        name="feed_forward",
    )
    return joined, parts


def feed_backward(blocks, joined, pack):
    rows, width = blocks[0].shape
    count, hidden = len(blocks), pack.shape[2] // 2

    def kernel(*refs):
        ins, (j, m, grad_joined, gated) = refs[:count], refs[count : count + 4]
        m_in, m_down = hidden_matrices(m, width)
        for n, (x, out) in enumerate(zip(ins, refs[count + 4 :])):
            part = slice(n * rows, (n + 1) * rows)
            gate = j[part, :hidden].astype(F32)
            up = j[part, hidden:].astype(F32)
            grad = lax.dot_general(x[...], m_down, NT, preferred_element_type=F32)
            sigmoid = 1.0 / (1.0 + jnp.exp(-gate))
            silu = gate * sigmoid
            gated[part, :] = (silu * up).astype(BF)
            grad_gate = grad * up * (sigmoid + silu * (1.0 - sigmoid))
            grad_joined[part, :hidden] = grad_gate.astype(BF)
            grad_joined[part, hidden:] = (grad * silu).astype(BF)
            total = lax.dot_general(grad_joined[part, :], m_in, NT, preferred_element_type=F32)
            out[...] = total.astype(BF)

    grad_joined, gated, *parts = on_chip(
        kernel,
        [((rows * count, 2 * hidden), BF), ((rows * count, hidden), BF)]
        + [((rows, width), BF)] * count,
        *blocks,
        joined,
        pack,
        flops=2 * rows * count * pack.size,
        name="feed_backward",
    )
    return grad_joined, gated, parts


def side_by_side(refs, scratch, sems, start=0):
    copies, column = [], 0
    for group in refs:
        row = 0
        for x in group:
            place = scratch.at[pl.ds(row, x.shape[0]), pl.ds(column, x.shape[1])]
            copies.append(pltpu.make_async_copy(x, place, sems.at[start + len(copies)]))
            row += x.shape[0]
        column += group[0].shape[1]
    return copies


def weight_call(kernel, outs, groups, shapes, at, flops, name):
    flat = [x for group in groups for column in group for x in column]
    outs = [jax.ShapeDtypeStruct(*out) for out in outs]
    moved = sum(math.prod(x.shape) * x.dtype.itemsize for x in flat + outs)

    def body(index, *refs):
        ins, refs = list(refs[: len(flat)]), refs[len(flat) :]
        results, scratch, sems = refs[: len(outs)], refs[len(outs) : -1], refs[-1]
        copies = []
        for group, target in zip(groups, scratch):
            taken = [[ins.pop(0) for x in column] for column in group]
            copies += side_by_side(taken, target, sems, len(copies))
        for copy in copies:
            copy.start()
        for copy in copies:
            copy.wait()
        kernel(index, *scratch, *results)

    return pl.pallas_call(
        body,
        in_specs=[SMEM] + [pl.BlockSpec(memory_space=pl.ANY)] * len(flat),
        out_specs=[VMEM] * len(outs),
        out_shape=outs,
        scratch_shapes=[pltpu.VMEM(shape, BF) for shape in shapes]
        + [pltpu.SemaphoreType.DMA((len(flat),))],
        compiler_params=pltpu.CompilerParams(vmem_limit_bytes=2 * LIMIT),
        cost_estimate=pl.CostEstimate(flops=flops, bytes_accessed=moved, transcendentals=0),
        name=name,
    )(at.astype(jnp.int32).reshape(1), *flat)


def hidden_weights(net, second, grad_joined, gated, grads):
    length = sum(x.shape[0] for x in second)
    width, columns, hidden = second[0].shape[1], grad_joined[0].shape[1], gated[0].shape[1]
    rows, down = width // net.dp_n, hidden // net.dp_n
    pieces = width // columns

    def kernel(index, a, b, c, d, out):
        for n in range(net.dp_n):
            left = a[:, n * rows : (n + 1) * rows]
            out[n, :rows, :] = lax.dot_general(
                left, b[...], TN, preferred_element_type=F32
            ).astype(BF)
            left = c[:, n * down : (n + 1) * down]
            total = lax.dot_general(left, d[...], TN, preferred_element_type=F32).astype(BF)
            for p in range(pieces):
                start = rows + p * down
                out[n, start : start + down, :] = total[:, p * columns : (p + 1) * columns]

    return weight_call(
        kernel,
        [((net.dp_n, rows + pieces * down, columns), BF)],
        [[second], [grad_joined], [gated], [grads]],
        [(length, width), (length, columns), (length, hidden), (length, width)],
        net.dp,
        2 * length * width * (columns + hidden),
        "hidden_weights",
    )[0]


def mixed_weights(net, normed, grads):
    length, width = sum(x.shape[0] for x in normed), normed[0].shape[1]
    columns = sum(g.shape[1] for g in grads)
    chunk = width // net.dp_n // net.hi_n

    def kernel(index, a, b, mine, other):
        for n in range(net.dp_n * net.hi_n):
            left = a[:, n * chunk : (n + 1) * chunk]
            total = lax.dot_general(left, b[...], TN, preferred_element_type=F32)
            here = index[0] == n % net.hi_n

            @pl.when(here)
            def keep(n=n, total=total):
                mine[n // net.hi_n] = total

            @pl.when(jnp.logical_not(here))
            def send(n=n, total=total):
                other[n // net.hi_n] = total.astype(BF)

    shape = (net.dp_n, chunk, columns)
    return weight_call(
        kernel,
        [(shape, F32), (shape, BF)],
        [[normed], [[g] for g in grads]],
        [(length, width), (length, columns)],
        net.hi,
        2 * length * width * columns,
        "mixed_weights",
    )


def out_backward(net, gradient, total, middle, gain, matrix, arrived, rows_out):
    rows, width = gradient.shape
    count, heads = len(arrived), arrived[0].shape[1]
    groups = width // rows_out // count

    def kernel(index, g, t, mid, gn, m, *refs):
        ins, (new, gain_out), refs = refs[:count], refs[count : count + 2], refs[count + 2 :]
        leaving, shares, scratch = refs[:count], refs[count : 2 * count], refs[2 * count]
        x = mid[...]
        inverse = lax.rsqrt(jnp.mean(x * x, axis=-1, keepdims=True) + EPSILON)
        normal = x * inverse
        grad = t[...]
        gain_out[...] = jnp.sum(grad * normal, axis=0, keepdims=True)
        grad = grad * gn[...]
        grad = (grad - normal * jnp.mean(grad * normal, axis=-1, keepdims=True)) * inverse
        grad = g[...] + grad
        new[...] = grad
        branch = grad.astype(BF)
        for r in range(count):
            start = pl.multiple_of((index[0] ^ r) * heads, heads)
            leaving[r][...] = lax.dot_general(
                branch, m[pl.ds(start, heads), :], NT, preferred_element_type=F32
            ).astype(BF)
            block = lax.dot_general(ins[r][...], branch, TN, preferred_element_type=F32)
            scratch[pl.ds(pl.multiple_of(start // rows_out, heads // rows_out), heads // rows_out)] = (
                block.reshape(heads // rows_out, rows_out, width)
            )
        for r in range(count):
            for n in range(groups):
                shares[r][n] = scratch[n * count + (index[0] ^ r)].astype(BF)

    outs = on_chip(
        kernel,
        [((rows, width), F32), ((1, width), F32)]
        + [((rows, heads), BF)] * count
        + [((groups, rows_out, width), BF)] * count,
        gradient,
        total,
        middle,
        gain.reshape(1, width),
        matrix,
        *arrived,
        at=net.lo,
        scratch=[pltpu.VMEM((width // rows_out, rows_out, width), F32)],
        flops=4 * rows * matrix.size,
        name="out_backward",
    )
    return outs[0], outs[1][0], outs[2 : 2 + count], outs[2 + count :]


def mixed_backward(grads, matrix, rows):
    length = grads[0].shape[0]
    count = length // rows
    width = grads[0].shape[1]

    def kernel(q, k, v, m, *outs):
        for n, out in enumerate(outs):
            part = slice(n * rows, (n + 1) * rows)
            x = jnp.concatenate([q[part, :], k[part, :], v[part, :]], axis=1)
            out[...] = lax.dot_general(
                x, m[:, : 3 * width], NT, preferred_element_type=F32
            ).astype(BF)

    return on_chip(
        kernel,
        [((rows, matrix.shape[0]), BF)] * count,
        *grads,
        matrix,
        flops=2 * length * matrix.size,
        name="mixed_backward",
    )


def join_rows(blocks, index):
    rows = blocks[0].shape[0]
    if rows % 16:
        return in_order(blocks, index).reshape(-1, blocks[0].shape[1])

    def kernel(at, *refs):
        for r, block in enumerate(refs[:-1]):
            start = pl.multiple_of((at[0] ^ r) * rows, rows)
            refs[-1][pl.ds(start, rows), :] = block[...]

    shape = (rows * len(blocks), blocks[0].shape[1])
    return on_chip(kernel, [(shape, BF)], *blocks, at=index, name="join_rows")[0]


def join_middle(blocks, index, rows):
    n, stacked, c = blocks[0].shape
    count, pieces = len(blocks), stacked // rows
    if rows % 16:
        full = in_order(blocks, index).reshape(count, n, pieces, rows, c)
        return full.transpose(1, 0, 3, 2, 4).reshape(-1, pieces * c)

    def kernel(at, *refs):
        for r, block in enumerate(refs[:-1]):
            for i in range(n):
                start = pl.multiple_of((i * count + (at[0] ^ r)) * rows, rows)
                for p in range(pieces):
                    refs[-1][pl.ds(start, rows), p * c : (p + 1) * c] = block[
                        i, p * rows : (p + 1) * rows, :
                    ]

    shape = (n * count * rows, pieces * c)
    return on_chip(kernel, [(shape, BF)], *blocks, at=index, name="join_middle")[0]


def lane_ids():
    return lax.broadcasted_iota(jnp.int32, (1, LANES), 1)


def three_parts(x):
    hi = x.astype(BF).astype(F32)
    mid = (x - hi).astype(BF).astype(F32)
    return hi, mid, x - hi - mid


def group_sum(x, width):
    rows = lax.broadcasted_iota(jnp.int32, (LANES, LANES), 0) // width
    columns = lax.broadcasted_iota(jnp.int32, (LANES, LANES), 1) // width
    ones = jnp.where(rows == columns, 1.0, 0.0).astype(BF)
    return sum(dot(part.astype(BF), ones) for part in three_parts(x))


def swap_halves(x, half):
    front = (lane_ids() // half) % 2 == 0
    return jnp.where(front, pltpu.roll(x, LANES - half, 1), pltpu.roll(x, half, 1))


def head_prep(raw, gain, cosine, sine, width):
    raw = raw.astype(F32)
    inverse = lax.rsqrt(group_sum(raw * raw, width) * (1.0 / width) + EPSILON)
    scaled = raw * inverse * gain
    return scaled * cosine + swap_halves(scaled, width // 2) * sine, inverse


def attend_kernel(
    rows, query_in, key_in, value_in, cosine, sine, marks, gains, bias, attended, kept, tops
):
    length = query_in.shape[0]
    width = LANES // 2
    low = lane_ids() < width
    query, unused = head_prep(query_in[...], gains[0:1, :], cosine[...], sine[...], width)
    keys, unused = head_prep(key_in[...], gains[1:2, :], cosine[...], sine[...], width)
    query = query * (1.0 / math.sqrt(width))
    mark = marks[...].astype(F32)
    value = value_in[...].astype(F32)
    heads = []
    for h in range(2):
        shift = (lambda x: pltpu.roll(x, width, 1)) if h else (lambda x: x)
        heads.append(
            (
                jnp.where(low, shift(query), mark * bias[0, h : h + 1, :]).astype(BF),
                jnp.where(low, shift(keys), mark).astype(BF),
                jnp.where(low, shift(value), 1.0).astype(BF),
            )
        )
    best = [None, None]
    for start in range(0, length, rows):
        part = slice(start, start + rows)
        outs = []
        for h, (head_query, head_keys, head_value) in enumerate(heads):
            scores = lax.dot_general(head_query[part], head_keys, NT, preferred_element_type=F32)
            top = jnp.max(scores, axis=0, keepdims=True)
            best[h] = top if best[h] is None else jnp.maximum(best[h], top)
            mixed = dot(jnp.exp(scores).astype(BF), head_value)
            out = jnp.where(low, mixed / pltpu.roll(mixed, width, 1), jnp.log(mixed))
            kept[h, part, :] = out
            outs.append(out)
        attended[part, :] = jnp.where(low, outs[0], pltpu.roll(outs[1], width, 1)).astype(BF)
    for h in range(2):
        tops[h, :, :] = jnp.broadcast_to(jnp.max(best[h], axis=1, keepdims=True), (8, LANES))


def attend_backward_kernel(
    columns,
    query_in,
    key_in,
    value_in,
    grad_in,
    cosine,
    sine,
    marks,
    gains,
    bias,
    kept,
    grad_query,
    grad_key,
    grad_value,
    grad_gains,
    grad_bias,
    keys_turned,
    sum_keys,
    sum_values,
):
    length = query_in.shape[0]
    width = LANES // 2
    lane = lane_ids()
    low = lane < width
    scale = 1.0 / math.sqrt(width)
    query, query_inverse = head_prep(query_in[...], gains[0:1, :], cosine[...], sine[...], width)
    keys, key_inverse = head_prep(key_in[...], gains[1:2, :], cosine[...], sine[...], width)
    query = query * scale
    mark = marks[...].astype(F32)
    value = value_in[...].astype(F32)
    grads = grad_in[...].astype(F32)

    def place(x, first, other):
        for offset, part in enumerate(three_parts(x)):
            other = jnp.where(lane == first + offset, part, other)
        return other

    all_query, all_keys, all_values = [], [], []
    for h in range(2):
        shift = (lambda x: pltpu.roll(x, width, 1)) if h else (lambda x: x)
        out = kept[h]
        query_marks = place(-out, width + 12, mark * bias[0, h : h + 1, :])
        head_query = jnp.where(low, shift(query), query_marks).astype(BF)
        head_keys = jnp.where(low, shift(keys), mark).astype(BF)
        ones = jnp.where(lane < width + 3, 1.0, 0.0)
        head_value = jnp.where(low, shift(value), ones).astype(BF)
        head_grad = jnp.where(low, shift(grads), 0.0)
        inner = pltpu.roll(-group_sum(head_grad * out, width), width, 1)
        head_grad = place(inner, width, head_grad).astype(BF)
        keys_turned[...] = head_keys.astype(F32).T.astype(BF)
        turned = []
        for start in range(0, length, columns):
            part = slice(start, start + columns)
            scores = lax.dot_general(head_keys, head_query[part], NT, preferred_element_type=F32)
            probability = jnp.exp(scores)
            grad_prob = lax.dot_general(
                head_value, head_grad[part], NT, preferred_element_type=F32
            )
            grad_scores = (probability * grad_prob).astype(BF)
            part_values = dot(probability.astype(BF), head_grad[part])
            part_keys = dot(grad_scores, head_query[part])
            if start:
                sum_values[...] += part_values
                sum_keys[...] += part_keys
            else:
                sum_values[...] = part_values
                sum_keys[...] = part_keys
            turned.append(dot(keys_turned[...], grad_scores).T)
        head_sum = jnp.concatenate(turned, axis=0)
        equal = jnp.where((lane >= width) & (lane < width + 4), mark, 0.0)
        match = jnp.sum(jnp.sum(head_sum * equal, axis=0, keepdims=True), axis=1, keepdims=True)
        total = jnp.sum(
            jnp.where(lane == width + 12, jnp.sum(head_sum, axis=0, keepdims=True), 0.0),
            axis=1,
            keepdims=True,
        )
        both = jnp.where(lane == 0, match, total - match)
        grad_bias[h, :, :] = jnp.broadcast_to(both, (8, LANES))
        all_query.append(head_sum * scale)
        all_keys.append(sum_keys[...])
        all_values.append(sum_values[...])

    def join(pair):
        return jnp.where(low, pair[0], pltpu.roll(pair[1], width, 1))

    grad_value[...] = join(all_values).astype(BF)
    for n, (pair, raw, inverse, out) in enumerate(
        (
            (all_query, query_in, query_inverse, grad_query),
            (all_keys, key_in, key_inverse, grad_key),
        )
    ):
        grad = join(pair)
        grad = grad * cosine[...] - swap_halves(grad, width // 2) * sine[...]
        normal = raw[...].astype(F32) * inverse
        grad_gains[0, n : n + 1, :] = jnp.sum(grad * normal, axis=0, keepdims=True)
        grad = grad * gains[n : n + 1, :]
        mean = group_sum(grad * normal, width) * (1.0 / width)
        out[...] = ((grad - normal * mean) * inverse).astype(BF)


def lane_block(length, offset):
    return pl.BlockSpec((length, LANES), lambda i: (0, offset + i))


def whole_block(shape):
    return pl.BlockSpec(shape, lambda i: (0,) * len(shape))


def attend(mixed, tables, gains, bias):
    length, heads = mixed.shape[0], bias.shape[0]
    pairs = heads // 2
    block = lane_block
    return pl.pallas_call(
        functools.partial(attend_kernel, min(256, length)),
        grid=(pairs,),
        in_specs=[
            block(length, 0),
            block(length, pairs),
            block(length, 2 * pairs),
            whole_block((length, LANES)),
            whole_block((length, LANES)),
            whole_block((length, LANES)),
            whole_block((2, LANES)),
            pl.BlockSpec((1, 2, LANES), lambda i: (i, 0, 0)),
        ],
        out_specs=[
            block(length, 0),
            pl.BlockSpec((2, length, LANES), lambda i: (i, 0, 0)),
            pl.BlockSpec((2, 8, LANES), lambda i: (i, 0, 0)),
        ],
        out_shape=[
            jax.ShapeDtypeStruct((length, pairs * LANES), BF),
            jax.ShapeDtypeStruct((heads, length, LANES), F32),
            jax.ShapeDtypeStruct((heads, 8, LANES), F32),
        ],
        compiler_params=pltpu.CompilerParams(vmem_limit_bytes=48 * 2**20),
        cost_estimate=pl.CostEstimate(
            flops=8 * heads * length * length * LANES,
            bytes_accessed=16 * length * pairs * LANES,
            transcendentals=heads * length * length,
        ),
        name="attend",
    )(mixed, mixed, mixed, *tables, gains, bias.reshape(pairs, 2, LANES))


def attend_backward(mixed, grad, tables, gains, bias, kept):
    length, heads = mixed.shape[0], bias.shape[0]
    pairs = heads // 2
    block = lane_block
    flat = jax.ShapeDtypeStruct((length, pairs * LANES), BF)
    return pl.pallas_call(
        functools.partial(attend_backward_kernel, min(256, length)),
        grid=(pairs,),
        in_specs=[
            block(length, 0),
            block(length, pairs),
            block(length, 2 * pairs),
            block(length, 0),
            whole_block((length, LANES)),
            whole_block((length, LANES)),
            whole_block((length, LANES)),
            whole_block((2, LANES)),
            pl.BlockSpec((1, 2, LANES), lambda i: (i, 0, 0)),
            pl.BlockSpec((2, length, LANES), lambda i: (i, 0, 0)),
        ],
        out_specs=[
            block(length, 0),
            block(length, 0),
            block(length, 0),
            pl.BlockSpec((1, 2, LANES), lambda i: (i, 0, 0)),
            pl.BlockSpec((2, 8, LANES), lambda i: (i, 0, 0)),
        ],
        out_shape=[
            flat,
            flat,
            flat,
            jax.ShapeDtypeStruct((pairs, 2, LANES), F32),
            jax.ShapeDtypeStruct((heads, 8, LANES), F32),
        ],
        scratch_shapes=[
            pltpu.VMEM((LANES, length), BF),
            pltpu.VMEM((length, LANES), F32),
            pltpu.VMEM((length, LANES), F32),
        ],
        compiler_params=pltpu.CompilerParams(vmem_limit_bytes=56 * 2**20),
        cost_estimate=pl.CostEstimate(
            flops=20 * heads * length * length * LANES,
            bytes_accessed=24 * length * pairs * LANES,
            transcendentals=heads * length * length,
        ),
        name="attend_backward",
    )(mixed, mixed, mixed, grad, *tables, gains, bias.reshape(pairs, 2, LANES), kept)


def head_tables(ids, places, width):
    frequency = jnp.exp(jnp.arange(width // 2, dtype=F32) * (-2.0 * math.log(10000.0) / width))
    angles = places.astype(F32)[:, None] * frequency
    cosine, sine = jnp.cos(angles), jnp.sin(angles)
    lane = jnp.arange(LANES)[None, :]
    equal = (ids[:, None] == (lane - width) % 4) & (lane >= width) & (lane < width + 12)
    plain = (lane >= width + 12) & (lane < width + 15)
    return (
        jnp.concatenate([cosine] * 4, axis=1),
        jnp.concatenate([-sine, sine, -sine, sine], axis=1),
        (equal | plain).astype(BF),
    )


def bias_marks(pair, width):
    gap = pair[0] - pair[1]
    hi = lax.reduce_precision(gap, 8, 7)
    mid = lax.reduce_precision(gap - hi, 8, 7)
    lane = jnp.arange(LANES)[None, :]
    marks = jnp.zeros((pair.shape[1], LANES), F32)
    for n, part in enumerate((hi, mid, gap - hi - mid)):
        inside = (lane >= width + 4 * n) & (lane < width + 4 * n + 4)
        marks = jnp.where(inside, part[:, None], marks)
    return marks


def stages(blocks):
    count = len(blocks)
    cuts = [0, 2, 6, 8] if count == 8 else [0, count // 2, count]
    return [blocks[a:b] for a, b in zip(cuts, cuts[1:])]


def shards(
    tokens,
    variate_ids,
    time_ids,
    w_qkv,
    w_out,
    w_in,
    w_down,
    norm_gains,
    qk_gains,
    head_bias,
    cotangent,
):
    sequences, tok_dev, width = tokens.shape
    layers = w_qkv.shape[0]
    heads = head_bias.shape[2]
    head_size = qk_gains.shape[2]
    net = Net()
    lo_n, lo_bits, seq_bits = net.lo_n, net.lo_bits, net.seq_bits
    rows = sequences * tok_dev
    local_heads = heads // lo_n
    local_width = local_heads * head_size
    head_start = net.lo * local_heads
    unit = w_down.shape[1]
    rows_out = w_out.shape[1]

    def to_groups(x):
        return jnp.concatenate(
            net.trade_hi([pick(x, net.hi ^ q) for q in range(sequences)]), axis=0
        )

    def to_devices(x):
        return in_order(net.trade_hi(jnp.split(x, sequences, axis=0)), net.hi)

    state = to_groups(tokens).astype(F32)
    own_qkv = trade_columns(net, w_qkv[0], lo_bits, local_width)
    own_in = trade_columns(net, after(w_in[0], own_qkv), seq_bits, unit)
    weights = []
    for layer in range(layers):
        m_qkv, m_out = fetch_attention(net, own_qkv, w_out[layer])
        weights.append((m_qkv, m_out, fetch_hidden(net, own_in, w_down[layer])))
        if layer + 1 < layers:
            own_qkv = trade_columns(net, after(w_qkv[layer + 1], own_in), lo_bits, local_width)
            own_in = trade_columns(net, after(w_in[layer + 1], own_qkv), seq_bits, unit)

    pair = to_groups(jnp.stack([variate_ids, time_ids], axis=-1))
    pair = jnp.concatenate(net.gather(pair, lo_bits), axis=0)
    tables = head_tables(pair[:, 0], pair[:, 1], head_size)

    saved = []
    best_scores = jnp.full((layers, heads), FLOOR_VALUE, F32)
    for layer in range(layers):
        m_qkv, m_out, pack = weights[layer]
        layer_in = state
        normed = rms_scale(layer_in, norm_gains[layer, 0]).astype(BF)
        normed = net.gather(normed, lo_bits)
        mixed = project(normed, m_qkv, 3 * local_width)
        bias_pair = lax.dynamic_slice_in_dim(head_bias[layer], head_start, local_heads, 1)
        gains = jnp.concatenate([qk_gains[layer]] * 2, axis=1)
        bias = bias_marks(bias_pair, head_size)
        attended, kept, head_tops = attend(mixed, tables, gains, bias)
        head_tops = head_tops[:, 0, 0] + bias_pair[1]
        best_scores = lax.dynamic_update_slice(
            best_scores, head_tops[None, :], (jnp.int32(layer), head_start)
        )
        arrived = net.trade(jnp.split(attended, lo_n, axis=0), lo_bits)
        middle, second = out_project(layer_in, arrived, m_out, norm_gains[layer, 1], net.lo)
        second = net.gather(second, seq_bits)
        joined, partial = [], []
        for part in stages(second):
            joined_part, out = feed_forward(part, pack)
            joined.append(joined_part)
            partial += out
        state = middle + net.scatter(partial, seq_bits)
        saved.append((layer_in, normed, mixed, gains, bias, kept, arrived, middle, second, joined))
    layer_out = to_devices(state.astype(BF))

    gradient = to_groups(cotangent).astype(F32)
    qkv_parts = [None] * layers
    out_parts = [None] * layers
    in_parts = [None] * layers
    down_parts = [None] * layers
    norm_parts = [None] * layers
    qk_parts = [None] * layers
    bias_parts = [None] * layers
    for layer in reversed(range(layers)):
        m_qkv, m_out, pack = weights[layer]
        layer_in, normed, mixed, gains, bias, kept, arrived, middle, second, joined = saved[layer]
        down_in = net.gather(gradient.astype(BF), seq_bits)
        grad_joined, gated, partial = [], [], []
        for part, joined_part in zip(stages(down_in), joined):
            grad_part, gated_part, out = feed_backward(part, joined_part, pack)
            grad_joined.append(grad_part)
            gated.append(gated_part)
            partial += out
        grad_second = net.scatter(partial, seq_bits)
        grad_hidden = hidden_weights(net, second, grad_joined, gated, down_in)
        own_in, down_parts[layer] = scatter_hidden(net, grad_hidden, width // net.dp_n)
        in_parts[layer] = restore_columns(net, own_in, seq_bits, unit)
        gradient, gain_second, leaving, shares = out_backward(
            net, gradient, grad_second, middle, norm_gains[layer, 1], m_out, arrived, rows_out
        )
        grad_out = net.scatter(shares, lo_bits)
        grad_out = grad_out.reshape((net.dp_n, net.hi_n) + grad_out.shape[1:])
        out_parts[layer] = net.scatter_rows(pick(grad_out, net.hi, 1), pick(grad_out, 1 - net.hi, 1))
        grad_heads = jnp.concatenate(net.trade(leaving, lo_bits), axis=0)
        grad_query, grad_keys, grad_values, grad_gains, grad_pair = attend_backward(
            mixed, grad_heads, tables, gains, bias, kept
        )
        grads = [grad_query, grad_keys, grad_values]
        grad_normed = net.scatter(mixed_backward(grads, m_qkv, rows), lo_bits)
        own_qkv = net.scatter_rows(*mixed_weights(net, normed, grads))
        qkv_parts[layer] = restore_columns(net, own_qkv, lo_bits, local_width)
        unused, first_pull = jax.vjp(rms_scale, layer_in, norm_gains[layer, 0])
        grad_layer_in, gain_first = first_pull(grad_normed)
        gradient = gradient + grad_layer_in
        norm_parts[layer] = jnp.stack([gain_first, gain_second])
        qk_parts[layer] = grad_gains.reshape(-1, 2, 2, head_size).sum(axis=(0, 2))
        bias_parts[layer] = lax.dynamic_update_slice(
            jnp.zeros((2, heads), F32), grad_pair[:, 0, :2].T, (jnp.int32(0), head_start)
        )
    input_grad = to_devices(gradient.astype(BF)).astype(F32)
    tops = best_scores.size
    small = jnp.concatenate(
        [best_scores.reshape(-1)]
        + [jnp.stack(part).reshape(-1) for part in (norm_parts, qk_parts, bias_parts)]
    )
    is_top = jnp.arange(small.size) < tops
    small = net.all_small(small, lambda a, b: jnp.where(is_top, jnp.maximum(a, b), a + b))
    best_scores = small[:tops].reshape(best_scores.shape)
    small = small[tops:]
    cut_norm, cut_qk = norm_gains.size, norm_gains.size + qk_gains.size
    norm_sum = small[:cut_norm].reshape(norm_gains.shape)
    qk_sum = small[cut_norm:cut_qk].reshape(qk_gains.shape)
    bias_sum = small[cut_qk:].reshape(head_bias.shape)

    factor = jnp.sqrt(CLIP_LIMIT / jnp.maximum(best_scores, CLIP_LIMIT))
    spread = jnp.repeat(factor, head_size, axis=1)
    column_scale = jnp.concatenate([spread, spread, jnp.ones((layers, width), F32)], axis=1)
    clipped = (w_qkv.astype(F32) * column_scale[:, None, :]).astype(BF)
    return (
        layer_out,
        input_grad,
        jnp.stack(qkv_parts),
        jnp.stack(out_parts),
        jnp.stack(in_parts),
        jnp.stack(down_parts),
        norm_sum,
        qk_sum,
        bias_sum,
        clipped,
        best_scores,
    )


def solution(mesh):
    def program(*arrays):
        dp_n = mesh.shape["dp"]
        sequences = arrays[0].shape[0] // dp_n
        split = Mesh(mesh.devices.reshape(dp_n, sequences, -1), ("dp", "hi", "lo"))
        seq = ("hi", "lo")
        tokens_spec = P("dp", seq, None)
        rows_spec = P(None, ("dp",) + seq, None)
        ids_spec = P("dp", seq)
        in_specs = (tokens_spec, ids_spec, ids_spec) + (rows_spec,) * 4 + (P(),) * 3
        in_specs += (tokens_spec,)
        out_specs = (tokens_spec,) * 2 + (rows_spec,) * 4 + (P(),) * 3 + (rows_spec, P())
        run = jax.shard_map(
            shards, mesh=split, in_specs=in_specs, out_specs=out_specs, check_vma=False
        )
        return run(*arrays)

    return program
```

```python
import functools
import math

import jax
import jax.numpy as jnp
from jax import lax
from jax.experimental import pallas as pl
from jax.experimental.pallas import tpu as pltpu
from jax.sharding import Mesh
from jax.sharding import PartitionSpec as P

EPSILON = 1e-05
CLIP_LIMIT = 2.0
FLOOR_VALUE = -1e30
BF = jnp.bfloat16
F32 = jnp.float32


def rms_scale(values, gain):
    return values * lax.rsqrt(jnp.mean(values * values, axis=-1, keepdims=True) + EPSILON) * gain


def dot(a, b):
    return jnp.dot(a, b, preferred_element_type=F32)


def pick(array, index, axis=0):
    return lax.dynamic_index_in_dim(array, index, axis, keepdims=False)


class Net:
    def __init__(self):
        self.dp_n, self.hi_n, self.lo_n = (lax.axis_size(name) for name in ("dp", "hi", "lo"))
        self.dp, self.hi, self.lo = (lax.axis_index(name) for name in ("dp", "hi", "lo"))
        self.seq_n = self.hi_n * self.lo_n
        self.seq = self.hi * self.lo_n + self.lo
        self.seq_bits = [1 << b for b in range(self.seq_n.bit_length() - 1)]
        self.lo_bits = [b for b in self.seq_bits if b < self.lo_n]
        self.hi_bits = [b // self.lo_n for b in self.seq_bits if b >= self.lo_n]

    def swap(self, x, bit):
        if bit < self.lo_n:
            return lax.ppermute(x, "lo", [(i, i ^ bit) for i in range(self.lo_n)])
        bit //= self.lo_n
        return lax.ppermute(x, "hi", [(i, i ^ bit) for i in range(self.hi_n)])

    def swap_hi(self, x):
        return self.swap(x, self.lo_n)

    def swap_dp(self, x, bit):
        return lax.ppermute(x, "dp", [(i, i ^ bit) for i in range(self.dp_n)])

    def shift_dp(self, blocks):
        n = self.dp_n
        return [
            lax.ppermute(x, "dp", [(i, (i + k + 1) % n) for i in range(n)])
            for k, x in enumerate(blocks)
        ]

    def gather(self, block, bits, held=None):
        blocks = {0: block}
        if held is not None:
            blocks[bits[-1]] = held
        for bit in reversed(bits):
            for r in list(blocks):
                if r & bit:
                    continue
                if r | bit in blocks:
                    continue
                blocks[r | bit] = self.swap(blocks[r], bit)
        return [blocks[r] for r in range(len(blocks))]

    def add_swapped(self, mine, sent, bit):
        return mine.astype(F32) + self.swap(sent.astype(BF), bit).astype(F32)

    def scatter(self, blocks, bits):
        blocks = dict(enumerate(blocks))
        for bit in bits:
            blocks = self.halve(blocks, bit)
        return blocks[0]

    def halve(self, blocks, bit):
        return {
            r: self.add_swapped(blocks[r], blocks[r | bit], bit)
            for r in sorted(blocks, reverse=True)
            if not r & bit
        }

    def trade(self, blocks, bits):
        return Trade(self, blocks, bits).finish()

    def all_small(self, x, combine):
        for bit in self.seq_bits:
            x = combine(x, self.swap(x, bit))
        bit = 1
        while bit < self.dp_n:
            x = combine(x, self.swap_dp(x, bit))
            bit *= 2
        return x


class Trade:
    def __init__(self, net, blocks, bits):
        self.net, self.blocks, self.left, self.moving = net, list(blocks), list(bits), []

    def step(self, *earlier):
        bit = self.left.pop()
        moving = [r for r in range(len(self.blocks)) if r & bit]
        if bit == 1:
            self.moving = [self.net.swap(after(self.blocks[r], *earlier), bit) for r in moving]
            for r, x in zip(moving, self.moving):
                self.blocks[r] = x
            return
        rows = self.blocks[0].shape[0]
        sent = after(jnp.concatenate([self.blocks[r] for r in moving], axis=0), *earlier)
        self.moving = [self.net.swap(sent, bit)]
        for n, r in enumerate(moving):
            self.blocks[r] = self.moving[0][n * rows : (n + 1) * rows]

    def finish(self):
        while self.left:
            self.step()
        return self.blocks


class SumAll:
    def __init__(self, net, blocks):
        self.net, self.blocks, self.moving, self.step_n = net, blocks, [], 0

    def step(self, *earlier):
        net, bits = self.net, self.net.seq_bits
        self.step_n += 1
        if len(bits) != 3:
            if self.step_n == 1:
                self.blocks = [net.scatter(self.blocks, bits)]
            self.moving = []
            return
        core, first, second = bits
        half = self.blocks[0].shape[0] // 2
        if self.step_n == 1:
            order = (first | second, first, second, 0)
            self.moving = [net.swap(after(self.blocks[r | core], *earlier), core) for r in order]
            self.pairs = {r: [self.blocks[r], x] for r, x in zip(order, self.moving)}
        elif self.step_n == 2:
            top, bottom = add_low([self.pairs[first | second]], cut=half)
            self.moving = [
                net.swap(after(top, *earlier), first),
                net.swap(after(bottom, *earlier), second),
            ]
        else:
            top, bottom = self.moving
            to_first, to_second = add_low(
                [self.pairs[first], self.pairs[second]], [(half, bottom), (0, top)]
            )
            self.moving = [
                net.swap(after(to_first, *earlier), first),
                net.swap(after(to_second, *earlier), second),
            ]

    def parts(self):
        while self.step_n < 3:
            self.step()
        return self.pairs[0] + self.moving if self.moving else self.blocks


class SumLo:
    def __init__(self, net, blocks):
        self.net, self.blocks = net, blocks

    def step(self, *earlier):
        net = self.net
        if len(net.lo_bits) != 2:
            self.left = [net.scatter(self.blocks, net.lo_bits)]
            self.moving = []
            return
        self.moving = [net.swap(after(self.blocks[r | 1], *earlier), 1) for r in (2, 0)]
        self.left = [self.blocks[0], self.moving[1]]

    def parts(self, *earlier):
        if self.moving:
            (far,) = add_low([[self.blocks[2], self.moving[0]]])
            self.moving = [self.net.swap(after(far, *earlier), 2)]
        return self.left + self.moving


class GatherBoth:
    def __init__(self, net, own, *earlier):
        self.net, self.own = net, own
        own = after(own, *earlier)
        self.own_came = net.swap_hi(own)
        self.by_dp = net.shift_dp([own] * (net.dp_n - 1))
        self.moving = [self.own_came] + self.by_dp

    def step(self, *earlier):
        self.rest_came = self.net.swap_hi(after(jnp.concatenate(self.by_dp, axis=0), *earlier))
        self.moving = [self.rest_came]

    def finish(self):
        net = self.net
        rows, columns = self.own.shape
        n = net.dp_n

        def kernel(at, own, own_came, rest_came, *refs):
            *by_dp, out = refs
            dp, hi = at[0] // 2, at[0] % 2
            out[at[0]] = own[...]
            out[dp * 2 + 1 - hi] = own_came[...]
            for k in range(1, n):
                source = lax.rem(dp + n - k, n)
                out[source * 2 + hi] = by_dp[k - 1][...]
                out[source * 2 + 1 - hi] = rest_came[(k - 1) * rows : k * rows, :]

        return on_chip(
            kernel,
            [((2 * n, rows, columns), BF)],
            self.own,
            self.own_came,
            self.rest_came,
            *self.by_dp,
            at=net.dp * 2 + net.hi,
            name="join_gathered",
        )[0]


class SumBoth:
    def __init__(self, net, mine, came):
        n = net.dp_n

        def kernel(at, x, y, own, *outs):
            own[...] = x[at[0]] + y[at[0]].astype(F32)
            for k, out in enumerate(outs):
                to = lax.rem(at[0] + k + 1, n)
                out[...] = (x[to] + y[to].astype(F32)).astype(BF)

        shape = mine.shape[1:]
        self.own, *self.blocks = on_chip(
            kernel, [(shape, F32)] + [(shape, BF)] * (n - 1), mine, came, at=net.dp, name="sum_hi"
        )
        self.net = net

    def step(self, *earlier):
        self.blocks[0] = after(self.blocks[0], *earlier)
        self.moving = self.net.shift_dp(self.blocks)

    def total(self):
        return self.own + sum(x.astype(F32) for x in self.moving)


def after(x, *earlier):
    return lax.optimization_barrier((x,) + earlier)[0]


def in_order(blocks, index):
    stacked = jnp.stack(blocks)
    return jnp.stack([pick(stacked, index ^ j) for j in range(len(blocks))])


def split_columns(shard, count, width):
    rows = shard.shape[0]
    parts = shard.shape[1] // count // width
    if width % LANES:
        shard = shard.reshape(rows, parts, count, width).transpose(2, 0, 1, 3)
        return shard.reshape(count, rows, parts * width)

    def kernel(shard_ref, out):
        for r in range(count):
            for p in range(parts):
                start = (p * count + r) * width
                out[r, :, p * width : (p + 1) * width] = shard_ref[:, start : start + width]

    return on_chip(kernel, [((count, rows, parts * width), BF)], shard, name="split_columns")[0]


def merge_columns(blocks, layers, width):
    count, rows = blocks.shape[0], blocks.shape[1] // layers
    parts = blocks.shape[2] // width
    columns = parts * count * width
    if width % LANES:
        shards = blocks.reshape(count, layers, rows, parts, width).transpose(1, 2, 3, 0, 4)
        return shards.reshape(layers, rows, columns).astype(F32)

    def kernel(ref, out):
        for r in range(count):
            for layer in range(layers):
                for p in range(parts):
                    start = (p * count + r) * width
                    part = ref[r, layer * rows : (layer + 1) * rows, p * width : (p + 1) * width]
                    out[layer, :, start : start + width] = part.astype(F32)

    return on_chip(kernel, [((layers, rows, columns), F32)], blocks, name="merge_columns")[0]


def own_columns(blocks, layers):
    count, rows, columns = blocks.shape
    blocks = blocks.reshape(count, layers, rows // layers, columns)
    return [blocks[:, n].reshape(-1, columns) for n in range(layers)]


def return_rows(layers, axes, count):
    own = jnp.stack([x.astype(BF).reshape(count, -1, x.shape[1]) for x in layers], axis=1)
    own = own.reshape(count, -1, own.shape[-1])
    return lax.all_to_all(own, axes, 0, 0, tiled=True)


def join_pieces(own, other, axis):
    if axis == 1:
        pieces = jnp.split(other, own.shape[0] // other.shape[0], axis=1)
        return jnp.concatenate([own, jnp.concatenate(pieces, axis=0)], axis=1)
    return jnp.concatenate([own] + jnp.split(other, other.shape[1] // own.shape[1], axis=1))


def split_hidden(own, rows_in, width):
    pieces = width // own.shape[1]
    down = jnp.concatenate(jnp.split(own[rows_in:], pieces, axis=0), axis=1)
    return own[:rows_in], down.astype(F32)


LANES = 128
NT = (((1,), (1,)), ((), ()))
TN = (((0,), (0,)), ((), ()))
VMEM = pl.BlockSpec(memory_space=pltpu.VMEM)
SMEM = pl.BlockSpec(memory_space=pltpu.SMEM)
LIMIT = 16 * 2**20


def on_chip(kernel, outs, *arrays, at=None, scratch=(), flops=0, name=None):
    outs = [jax.ShapeDtypeStruct(*out) for out in outs]
    moved = sum(math.prod(x.shape) * x.dtype.itemsize for x in list(arrays) + outs)
    first = [] if at is None else [at.astype(jnp.int32).reshape(1)]
    return pl.pallas_call(
        kernel,
        in_specs=[SMEM] * len(first) + [VMEM] * len(arrays),
        out_specs=[VMEM] * len(outs),
        out_shape=outs,
        scratch_shapes=list(scratch),
        compiler_params=pltpu.CompilerParams(vmem_limit_bytes=LIMIT),
        cost_estimate=pl.CostEstimate(flops=flops, bytes_accessed=moved, transcendentals=0),
        name=name,
    )(*first, *arrays)


def add_low(groups, extras=None, cut=None):
    shape = groups[0][0].shape
    extras = extras or [None] * len(groups)
    flat, counts = [], []
    for group, extra in zip(groups, extras):
        members = group + ([extra[1]] if extra else [])
        counts.append(len(members))
        flat += members

    def kernel(*refs):
        ins, outs = list(refs[: len(flat)]), list(refs[len(flat) :])
        for count, extra in zip(counts, extras):
            members = [ins.pop(0) for _ in range(count)]
            last = members.pop() if extra else None
            total = sum(x[...].astype(F32) for x in members)
            if extra:
                rows = last.shape[0]
                part = total[extra[0] : extra[0] + rows] + last[...].astype(F32)
                pieces = [total[: extra[0]], part, total[extra[0] + rows :]]
                total = jnp.concatenate([p for p in pieces if p.shape[0]], axis=0)
            total = total.astype(BF)
            if cut is None:
                outs.pop(0)[...] = total
            else:
                outs.pop(0)[...] = total[:cut]
                outs.pop(0)[...] = total[cut:]

    if cut is None:
        shapes = [(shape, BF)] * len(groups)
    else:
        shapes = [((cut,) + shape[1:], BF), ((shape[0] - cut,) + shape[1:], BF)]
    return on_chip(kernel, shapes, *flat, name="add_low")


def finish_layer(middle, parts, gain):
    rows, width = middle.shape

    def kernel(x, g, *refs):
        *ins, state, normed = refs
        total = x[...] + sum(part[...].astype(F32) for part in ins)
        state[...] = total
        normed[...] = rms_scale(total, g[...]).astype(BF)

    outs = [((rows, width), F32), ((rows, width), BF)]
    return on_chip(kernel, outs, middle, gain.reshape(1, width), *parts, name="finish_layer")


def norm_backward(gradient, parts, values, gain):
    rows, width = gradient.shape

    def kernel(g, x, gn, *refs):
        *ins, new, low, gain_out = refs
        total = sum(part[...].astype(F32) for part in ins)
        grad, gain_part = norm_adjoint(x[...], gn[...], total)
        grad = g[...] + grad
        new[...] = grad
        low[...] = grad.astype(BF)
        gain_out[...] = gain_part

    outs = [((rows, width), F32), ((rows, width), BF), ((1, width), F32)]
    arrays = [gradient, values, gain.reshape(1, width)]
    new, low, gain_part = on_chip(kernel, outs, *arrays, *parts, name="norm_backward")
    return new, low, gain_part[0]


def norm_adjoint(values, gain, grad):
    inverse = lax.rsqrt(jnp.mean(values * values, axis=-1, keepdims=True) + EPSILON)
    normal = values * inverse
    gain_part = jnp.sum(grad * normal, axis=0, keepdims=True)
    grad = grad * gain
    grad = (grad - normal * jnp.mean(grad * normal, axis=-1, keepdims=True)) * inverse
    return grad, gain_part


def project(blocks, matrix, columns):
    rows = blocks[0].shape[0]

    def kernel(*refs):
        *ins, m, out = refs
        for n, x in enumerate(ins):
            out[n * rows : (n + 1) * rows, :] = dot(x[...], m[:, :columns]).astype(BF)

    return on_chip(
        kernel,
        [((rows * len(blocks), columns), BF)],
        *blocks,
        matrix,
        flops=2 * rows * len(blocks) * matrix.size,
        name="project",
    )[0]


def out_project(state, arrived, matrix, gain, at):
    rows, width = state.shape
    heads = arrived[0].shape[1]

    def kernel(index, x, m, g, *refs):
        *ins, middle, second = refs
        total = x[...]
        for r, block in enumerate(ins):
            start = pl.multiple_of((index[0] ^ r) * heads, heads)
            total = total + dot(block[...], m[pl.ds(start, heads), :])
        middle[...] = total
        second[...] = rms_scale(total, g[...]).astype(BF)

    return on_chip(
        kernel,
        [((rows, width), F32), ((rows, width), BF)],
        state,
        matrix,
        gain.reshape(1, width),
        *arrived,
        at=at,
        flops=2 * rows * matrix.size,
        name="out_project",
    )


def hidden_matrices(pack, width):
    rows = width // pack.shape[0]
    columns = pack.shape[2]
    down = (pack.shape[1] - rows) * columns // width
    m_in = jnp.concatenate([pack[n, :rows, :] for n in range(pack.shape[0])], axis=0)
    m_down = []
    for n in range(pack.shape[0]):
        starts = range(rows, pack.shape[1], down)
        m_down.append(jnp.concatenate([pack[n, p : p + down, :] for p in starts], axis=1))
    return m_in, jnp.concatenate(m_down, axis=0)


def feed_forward(blocks, pack):
    rows, width = blocks[0].shape
    count, hidden = len(blocks), pack.shape[2] // 2

    def kernel(*refs):
        m, ins, joined, outs = refs[0], refs[1 : count + 1], refs[count + 1], refs[count + 2 :]
        m_in, m_down = hidden_matrices(m, width)
        for n, (x, out) in enumerate(zip(ins, outs)):
            both = dot(x[...], m_in)
            joined[n * rows : (n + 1) * rows, :] = both.astype(BF)
            gate, up = both[:, :hidden], both[:, hidden:]
            gated = gate / (1.0 + jnp.exp(-gate)) * up
            out[...] = dot(gated.astype(BF), m_down).astype(BF)

    joined, *parts = on_chip(
        kernel,
        [((rows * count, 2 * hidden), BF)] + [((rows, width), BF)] * count,
        pack,
        *blocks,
        flops=2 * rows * count * pack.size,
        name="feed_forward",
    )
    return joined, parts


def feed_backward(blocks, joined, pack):
    rows, width = blocks[0].shape
    count, hidden = len(blocks), pack.shape[2] // 2

    def kernel(*refs):
        m, ins, (j, grad_joined, gated) = refs[0], refs[1 : count + 1], refs[count + 1 : count + 4]
        m_in, m_down = hidden_matrices(m, width)
        for n, (x, out) in enumerate(zip(ins, refs[count + 4 :])):
            part = slice(n * rows, (n + 1) * rows)
            gate = j[part, :hidden].astype(F32)
            up = j[part, hidden:].astype(F32)
            grad = lax.dot_general(x[...], m_down, NT, preferred_element_type=F32)
            sigmoid = 1.0 / (1.0 + jnp.exp(-gate))
            silu = gate * sigmoid
            gated[part, :] = (silu * up).astype(BF)
            grad_gate = grad * up * (sigmoid + silu * (1.0 - sigmoid))
            grad_joined[part, :hidden] = grad_gate.astype(BF)
            grad_joined[part, hidden:] = (grad * silu).astype(BF)
            total = lax.dot_general(grad_joined[part, :], m_in, NT, preferred_element_type=F32)
            out[...] = total.astype(BF)

    grad_joined, gated, *parts = on_chip(
        kernel,
        [((rows * count, 2 * hidden), BF), ((rows * count, hidden), BF)]
        + [((rows, width), BF)] * count,
        pack,
        *blocks,
        joined,
        flops=2 * rows * count * pack.size,
        name="feed_backward",
    )
    return grad_joined, gated, parts


def side_by_side(refs, scratch, sems, start=0):
    copies, column = [], 0
    for group in refs:
        row = 0
        for x in group:
            place = scratch.at[pl.ds(row, x.shape[0]), pl.ds(column, x.shape[1])]
            copies.append(pltpu.make_async_copy(x, place, sems.at[start + len(copies)]))
            row += x.shape[0]
        column += group[0].shape[1]
    return copies


def weight_call(kernel, outs, groups, shapes, at, flops, name):
    flat = [x for group in groups for column in group for x in column]
    outs = [jax.ShapeDtypeStruct(*out) for out in outs]
    moved = sum(math.prod(x.shape) * x.dtype.itemsize for x in flat + outs)

    def body(index, *refs):
        ins, refs = list(refs[: len(flat)]), refs[len(flat) :]
        results, scratch, sems = refs[: len(outs)], refs[len(outs) : -1], refs[-1]
        arrived, count = [], 0
        for group, target in zip(groups, scratch):
            taken = [[ins.pop(0) for x in column] for column in group]
            copies = side_by_side(taken, target, sems, count)
            count += len(copies)
            for copy in copies:
                copy.start()
            arrived.append(Arriving(copies, target))
        kernel(index, *arrived, *results)

    return pl.pallas_call(
        body,
        in_specs=[SMEM] + [pl.BlockSpec(memory_space=pl.ANY)] * len(flat),
        out_specs=[VMEM] * len(outs),
        out_shape=outs,
        scratch_shapes=[pltpu.VMEM(shape, BF) for shape in shapes]
        + [pltpu.SemaphoreType.DMA((len(flat),))],
        compiler_params=pltpu.CompilerParams(vmem_limit_bytes=2 * LIMIT),
        cost_estimate=pl.CostEstimate(flops=flops, bytes_accessed=moved, transcendentals=0),
        name=name,
    )(at.astype(jnp.int32).reshape(1), *flat)


class Arriving:
    def __init__(self, copies, ref):
        self.copies, self.ref = copies, ref

    def __getitem__(self, index):
        for copy in self.copies:
            copy.wait()
        self.copies = []
        return self.ref[index]


def hidden_weights(net, second, grad_joined, gated, grads):
    length = sum(x.shape[0] for x in second)
    width, columns, hidden = second[0].shape[1], grad_joined[0].shape[1], gated[0].shape[1]
    rows, down = width // net.dp_n, hidden // net.dp_n
    pieces = width // columns

    def kernel(index, a, b, c, d, out):
        for n in range(net.dp_n):
            left = a[:, n * rows : (n + 1) * rows]
            first = n * (rows + pieces * down)
            out[first : first + rows, :] = lax.dot_general(
                left, b[...], TN, preferred_element_type=F32
            ).astype(BF)
            left = c[:, n * down : (n + 1) * down]
            total = lax.dot_general(left, d[...], TN, preferred_element_type=F32).astype(BF)
            for p in range(pieces):
                start = first + rows + p * down
                out[start : start + down, :] = total[:, p * columns : (p + 1) * columns]

    return weight_call(
        kernel,
        [((net.dp_n * (rows + pieces * down), columns), BF)],
        [[second], [grad_joined], [gated], [grads]],
        [(length, width), (length, columns), (length, hidden), (length, width)],
        net.dp,
        2 * length * width * (columns + hidden),
        "hidden_weights",
    )[0]


def mixed_weights(net, normed, grads, shares, rows, kept):
    length, width = sum(x.shape[0] for x in normed), normed[0].shape[1]
    columns = sum(g.shape[1] for g in grads)
    chunk = width // net.dp_n // net.hi_n
    pieces = chunk // rows
    c = shares[0].shape[1] // pieces

    def kernel(index, a, b, *refs):
        *parts, mine, other = refs
        for n in range(net.dp_n * net.hi_n):
            left = a[:, n * chunk : (n + 1) * chunk]
            total = lax.dot_general(left, b[...], TN, preferred_element_type=F32)
            out = sum(part[n * rows : (n + 1) * rows, :].astype(F32) for part in parts)
            here = index[0] == n % net.hi_n

            def store(target, kind, n=n, total=total, out=out):
                target[n // net.hi_n, :, :columns] = total.astype(kind)
                for p in range(pieces):
                    cut = out[:, p * c : (p + 1) * c].astype(kind)
                    target[n // net.hi_n, p * rows : (p + 1) * rows, columns:] = cut

            pl.when(here)(lambda: store(mine, kept))
            pl.when(jnp.logical_not(here))(lambda: store(other, BF))

    shape = (net.dp_n, chunk, columns + c)
    flat = [x.astype(BF) for x in shares]
    return weight_call(
        kernel,
        [(shape, kept), (shape, BF)],
        [[normed], [[g] for g in grads]] + [[[x]] for x in flat],
        [(length, width), (length, columns)] + [x.shape for x in flat],
        net.hi,
        2 * length * width * columns,
        "mixed_weights",
    )


def split_pieces(own, columns, rows):
    pieces = own.shape[0] // rows
    return own[:, :columns], jnp.concatenate(jnp.split(own[:, columns:], pieces, axis=0), axis=1)


def out_backward(net, gradient, parts, middle, gain, matrix, arrived, rows_out):
    rows, width = gradient.shape
    count, heads = len(arrived), arrived[0].shape[1]
    groups = width // rows_out // count

    def kernel(index, g, mid, gn, *refs):
        sums, m, refs = refs[: len(parts)], refs[len(parts)], refs[len(parts) + 1 :]
        ins, (new, gain_out), refs = refs[:count], refs[count : count + 2], refs[count + 2 :]
        leaving, shares, scratch = refs[:count], refs[count : 2 * count], refs[2 * count]
        total = sum(part[...].astype(F32) for part in sums)
        grad, gain_out[...] = norm_adjoint(mid[...], gn[...], total)
        grad = g[...] + grad
        new[...] = grad
        branch = grad.astype(BF)
        for r in range(count):
            start = pl.multiple_of((index[0] ^ r) * heads, heads)
            leaving[r][...] = lax.dot_general(
                branch, m[pl.ds(start, heads), :], NT, preferred_element_type=F32
            ).astype(BF)
            block = lax.dot_general(ins[r][...], branch, TN, preferred_element_type=F32)
            scratch[pl.ds(pl.multiple_of(start // rows_out, heads // rows_out), heads // rows_out)] = (
                block.reshape(heads // rows_out, rows_out, width)
            )
        for r in range(count):
            for n in range(groups):
                shares[r][n] = scratch[n * count + (index[0] ^ r)].astype(BF)

    outs = on_chip(
        kernel,
        [((rows, width), F32), ((1, width), F32)]
        + [((rows, heads), BF)] * count
        + [((groups, rows_out, width), BF)] * count,
        gradient,
        middle,
        gain.reshape(1, width),
        *parts,
        matrix,
        *arrived,
        at=net.lo,
        scratch=[pltpu.VMEM((width // rows_out, rows_out, width), F32)],
        flops=4 * rows * matrix.size,
        name="out_backward",
    )
    return outs[0], outs[1][0], outs[2 : 2 + count], outs[2 + count :]


def mixed_backward(grads, matrix, rows):
    length = grads[0].shape[0]
    count = length // rows
    width = grads[0].shape[1]

    def kernel(q, k, v, m, *outs):
        for n, out in enumerate(outs):
            part = slice(n * rows, (n + 1) * rows)
            x = jnp.concatenate([q[part, :], k[part, :], v[part, :]], axis=1)
            out[...] = lax.dot_general(
                x, m[:, : 3 * width], NT, preferred_element_type=F32
            ).astype(BF)

    return on_chip(
        kernel,
        [((rows, matrix.shape[0]), BF)] * count,
        *grads,
        matrix,
        flops=2 * length * matrix.size,
        name="mixed_backward",
    )


def join_middle(blocks, index, rows):
    n, stacked, c = blocks[0].shape
    count, pieces = len(blocks), stacked // rows
    if rows % 16:
        full = in_order(blocks, index).reshape(count, n, pieces, rows, c)
        return full.transpose(1, 0, 3, 2, 4).reshape(-1, pieces * c)

    def kernel(at, *refs):
        for r, block in enumerate(refs[:-1]):
            for i in range(n):
                start = pl.multiple_of((i * count + (at[0] ^ r)) * rows, rows)
                for p in range(pieces):
                    refs[-1][pl.ds(start, rows), p * c : (p + 1) * c] = block[
                        i, p * rows : (p + 1) * rows, :
                    ]

    shape = (n * count * rows, pieces * c)
    return on_chip(kernel, [(shape, BF)], *blocks, at=index, name="join_middle")[0]


def lane_ids():
    return lax.broadcasted_iota(jnp.int32, (1, LANES), 1)


def three_parts(x):
    hi = x.astype(BF).astype(F32)
    mid = (x - hi).astype(BF).astype(F32)
    return hi, mid, x - hi - mid


def group_sum(x, width):
    rows = lax.broadcasted_iota(jnp.int32, (LANES, LANES), 0) // width
    columns = lax.broadcasted_iota(jnp.int32, (LANES, LANES), 1) // width
    ones = jnp.where(rows == columns, 1.0, 0.0).astype(BF)
    return sum(dot(part.astype(BF), ones) for part in three_parts(x))


def swap_halves(x, half):
    front = (lane_ids() // half) % 2 == 0
    return jnp.where(front, pltpu.roll(x, LANES - half, 1), pltpu.roll(x, half, 1))


def head_prep(raw, gain, cosine, sine, width):
    raw = raw.astype(F32)
    inverse = lax.rsqrt(group_sum(raw * raw, width) * (1.0 / width) + EPSILON)
    scaled = raw * inverse * gain
    return scaled * cosine + swap_halves(scaled, width // 2) * sine, inverse


def attend_kernel(
    rows, query_in, key_in, value_in, cosine, sine, marks, gains, bias, attended, kept, tops
):
    length = query_in.shape[0]
    width = LANES // 2
    low = lane_ids() < width
    query, unused = head_prep(query_in[...], gains[0:1, :], cosine[...], sine[...], width)
    keys, unused = head_prep(key_in[...], gains[1:2, :], cosine[...], sine[...], width)
    query = query * (1.0 / math.sqrt(width))
    mark = marks[...].astype(F32)
    value = value_in[...].astype(F32)
    heads = []
    for h in range(2):
        shift = (lambda x: pltpu.roll(x, width, 1)) if h else (lambda x: x)
        heads.append(
            (
                jnp.where(low, shift(query), mark * bias[0, h : h + 1, :]).astype(BF),
                jnp.where(low, shift(keys), mark).astype(BF),
                jnp.where(low, shift(value), 1.0).astype(BF),
            )
        )
    best = [None, None]
    for start in range(0, length, rows):
        part = slice(start, start + rows)
        outs = []
        for h, (head_query, head_keys, head_value) in enumerate(heads):
            scores = lax.dot_general(head_query[part], head_keys, NT, preferred_element_type=F32)
            top = jnp.max(scores, axis=0, keepdims=True)
            best[h] = top if best[h] is None else jnp.maximum(best[h], top)
            mixed = dot(jnp.exp(scores).astype(BF), head_value)
            out = jnp.where(low, mixed / pltpu.roll(mixed, width, 1), jnp.log(mixed))
            kept[h, part, :] = out
            outs.append(out)
        attended[part, :] = jnp.where(low, outs[0], pltpu.roll(outs[1], width, 1)).astype(BF)
    for h in range(2):
        tops[h, :, :] = jnp.broadcast_to(jnp.max(best[h], axis=1, keepdims=True), (8, LANES))


def attend_backward_kernel(
    columns,
    query_in,
    key_in,
    value_in,
    grad_in,
    cosine,
    sine,
    marks,
    gains,
    bias,
    kept,
    grad_query,
    grad_key,
    grad_value,
    grad_gains,
    grad_bias,
    keys_turned,
    sum_keys,
    sum_values,
):
    length = query_in.shape[0]
    width = LANES // 2
    lane = lane_ids()
    low = lane < width
    scale = 1.0 / math.sqrt(width)
    query, query_inverse = head_prep(query_in[...], gains[0:1, :], cosine[...], sine[...], width)
    keys, key_inverse = head_prep(key_in[...], gains[1:2, :], cosine[...], sine[...], width)
    query = query * scale
    mark = marks[...].astype(F32)
    value = value_in[...].astype(F32)
    grads = grad_in[...].astype(F32)

    def place(x, first, other):
        for offset, part in enumerate(three_parts(x)):
            other = jnp.where(lane == first + offset, part, other)
        return other

    all_query, all_keys, all_values = [], [], []
    for h in range(2):
        shift = (lambda x: pltpu.roll(x, width, 1)) if h else (lambda x: x)
        out = kept[h]
        query_marks = place(-out, width + 12, mark * bias[0, h : h + 1, :])
        head_query = jnp.where(low, shift(query), query_marks).astype(BF)
        head_keys = jnp.where(low, shift(keys), mark).astype(BF)
        ones = jnp.where(lane < width + 3, 1.0, 0.0)
        head_value = jnp.where(low, shift(value), ones).astype(BF)
        head_grad = jnp.where(low, shift(grads), 0.0)
        inner = pltpu.roll(-group_sum(head_grad * out, width), width, 1)
        head_grad = place(inner, width, head_grad).astype(BF)
        keys_turned[...] = head_keys.astype(F32).T.astype(BF)
        turned = []
        for start in range(0, length, columns):
            part = slice(start, start + columns)
            scores = lax.dot_general(head_keys, head_query[part], NT, preferred_element_type=F32)
            probability = jnp.exp(scores)
            grad_prob = lax.dot_general(
                head_value, head_grad[part], NT, preferred_element_type=F32
            )
            grad_scores = (probability * grad_prob).astype(BF)
            part_values = dot(probability.astype(BF), head_grad[part])
            part_keys = dot(grad_scores, head_query[part])
            if start:
                sum_values[...] += part_values
                sum_keys[...] += part_keys
            else:
                sum_values[...] = part_values
                sum_keys[...] = part_keys
            turned.append(dot(keys_turned[...], grad_scores).T)
        head_sum = jnp.concatenate(turned, axis=0)
        equal = jnp.where((lane >= width) & (lane < width + 4), mark, 0.0)
        match = jnp.sum(jnp.sum(head_sum * equal, axis=0, keepdims=True), axis=1, keepdims=True)
        total = jnp.sum(
            jnp.where(lane == width + 12, jnp.sum(head_sum, axis=0, keepdims=True), 0.0),
            axis=1,
            keepdims=True,
        )
        both = jnp.where(lane == 0, match, total - match)
        grad_bias[h, :, :] = jnp.broadcast_to(both, (8, LANES))
        all_query.append(head_sum * scale)
        all_keys.append(sum_keys[...])
        all_values.append(sum_values[...])

    def join(pair):
        return jnp.where(low, pair[0], pltpu.roll(pair[1], width, 1))

    grad_value[...] = join(all_values).astype(BF)
    for n, (pair, raw, inverse, out) in enumerate(
        (
            (all_query, query_in, query_inverse, grad_query),
            (all_keys, key_in, key_inverse, grad_key),
        )
    ):
        grad = join(pair)
        grad = grad * cosine[...] - swap_halves(grad, width // 2) * sine[...]
        normal = raw[...].astype(F32) * inverse
        grad_gains[0, n : n + 1, :] = jnp.sum(grad * normal, axis=0, keepdims=True)
        grad = grad * gains[n : n + 1, :]
        mean = group_sum(grad * normal, width) * (1.0 / width)
        out[...] = ((grad - normal * mean) * inverse).astype(BF)


def lane_block(length, offset):
    return pl.BlockSpec((length, LANES), lambda i: (0, offset + i))


def whole_block(shape):
    return pl.BlockSpec(shape, lambda i: (0,) * len(shape))


def attend(mixed, tables, gains, bias):
    length, heads = mixed.shape[0], bias.shape[0]
    pairs = heads // 2
    block = lane_block
    return pl.pallas_call(
        functools.partial(attend_kernel, min(256, length)),
        grid=(pairs,),
        in_specs=[
            block(length, 0),
            block(length, pairs),
            block(length, 2 * pairs),
            whole_block((length, LANES)),
            whole_block((length, LANES)),
            whole_block((length, LANES)),
            whole_block((2, LANES)),
            pl.BlockSpec((1, 2, LANES), lambda i: (i, 0, 0)),
        ],
        out_specs=[
            block(length, 0),
            pl.BlockSpec((2, length, LANES), lambda i: (i, 0, 0)),
            pl.BlockSpec((2, 8, LANES), lambda i: (i, 0, 0)),
        ],
        out_shape=[
            jax.ShapeDtypeStruct((length, pairs * LANES), BF),
            jax.ShapeDtypeStruct((heads, length, LANES), F32),
            jax.ShapeDtypeStruct((heads, 8, LANES), F32),
        ],
        compiler_params=pltpu.CompilerParams(vmem_limit_bytes=LIMIT * max(1, length // 1024)),
        cost_estimate=pl.CostEstimate(
            flops=8 * heads * length * length * LANES,
            bytes_accessed=16 * length * pairs * LANES,
            transcendentals=heads * length * length,
        ),
        name="attend",
    )(mixed, mixed, mixed, *tables, gains, bias.reshape(pairs, 2, LANES))


def attend_backward(mixed, grad, tables, gains, bias, kept):
    length, heads = mixed.shape[0], bias.shape[0]
    pairs = heads // 2
    block = lane_block
    flat = jax.ShapeDtypeStruct((length, pairs * LANES), BF)
    return pl.pallas_call(
        functools.partial(attend_backward_kernel, min(256, length)),
        grid=(pairs,),
        in_specs=[
            block(length, 0),
            block(length, pairs),
            block(length, 2 * pairs),
            block(length, 0),
            whole_block((length, LANES)),
            whole_block((length, LANES)),
            whole_block((length, LANES)),
            whole_block((2, LANES)),
            pl.BlockSpec((1, 2, LANES), lambda i: (i, 0, 0)),
            pl.BlockSpec((2, length, LANES), lambda i: (i, 0, 0)),
        ],
        out_specs=[
            block(length, 0),
            block(length, 0),
            block(length, 0),
            pl.BlockSpec((1, 2, LANES), lambda i: (i, 0, 0)),
            pl.BlockSpec((2, 8, LANES), lambda i: (i, 0, 0)),
        ],
        out_shape=[
            flat,
            flat,
            flat,
            jax.ShapeDtypeStruct((pairs, 2, LANES), F32),
            jax.ShapeDtypeStruct((heads, 8, LANES), F32),
        ],
        scratch_shapes=[
            pltpu.VMEM((LANES, length), BF),
            pltpu.VMEM((length, LANES), F32),
            pltpu.VMEM((length, LANES), F32),
        ],
        compiler_params=pltpu.CompilerParams(vmem_limit_bytes=LIMIT * max(1, length // 1024)),
        cost_estimate=pl.CostEstimate(
            flops=20 * heads * length * length * LANES,
            bytes_accessed=24 * length * pairs * LANES,
            transcendentals=heads * length * length,
        ),
        name="attend_backward",
    )(mixed, mixed, mixed, grad, *tables, gains, bias.reshape(pairs, 2, LANES), kept)


def head_tables(ids, places, width):
    frequency = jnp.exp(jnp.arange(width // 2, dtype=F32) * (-2.0 * math.log(10000.0) / width))
    angles = places.astype(F32)[:, None] * frequency
    cosine, sine = jnp.cos(angles), jnp.sin(angles)
    lane = jnp.arange(LANES)[None, :]
    equal = (ids[:, None] == (lane - width) % 4) & (lane >= width) & (lane < width + 12)
    plain = (lane >= width + 12) & (lane < width + 15)
    return (
        jnp.concatenate([cosine] * 4, axis=1),
        jnp.concatenate([-sine, sine, -sine, sine], axis=1),
        (equal | plain).astype(BF),
    )


def bias_marks(pair, width):
    gap = pair[0] - pair[1]
    hi = lax.reduce_precision(gap, 8, 7)
    mid = lax.reduce_precision(gap - hi, 8, 7)
    lane = jnp.arange(LANES)[None, :]
    marks = jnp.zeros((pair.shape[1], LANES), F32)
    for n, part in enumerate((hi, mid, gap - hi - mid)):
        inside = (lane >= width + 4 * n) & (lane < width + 4 * n + 4)
        marks = jnp.where(inside, part[:, None], marks)
    return marks


def wave(net, own, compute, held=None):
    bits = net.seq_bits
    if len(bits) != 3:
        blocks = net.gather(own, bits)
        cuts = (blocks[: len(blocks) // 2], blocks[len(blocks) // 2 :])
        return blocks, [compute(n, cut) for n, cut in enumerate(cuts)]
    core, first, second = bits
    half = own.shape[0] // 2
    if held is None:
        held = [net.swap(own, bit) for bit in (first, second)]
    by_core = net.swap(own, core)
    outs = [compute(0, [own, by_core])]
    by_first, by_second = (after(x, outs[0][0]) for x in held)
    corner = [net.swap(by_first[:half], second), net.swap(by_second[half:], first)]
    blocks = [own, by_core, by_first, net.swap(by_first, core)]
    blocks += [by_second, net.swap(by_second, core)]
    outs.append(compute(1, blocks[2:6]))
    corner = jnp.concatenate([after(x, outs[1][0]) for x in corner], axis=0)
    blocks += [corner, net.swap(corner, core)]
    outs.append(compute(2, blocks[6:]))
    return blocks, outs


def shards(
    tokens,
    variate_ids,
    time_ids,
    w_qkv,
    w_out,
    w_in,
    w_down,
    norm_gains,
    qk_gains,
    head_bias,
    cotangent,
):
    sequences, tok_dev, width = tokens.shape
    layers = w_qkv.shape[0]
    heads = head_bias.shape[2]
    head_size = qk_gains.shape[2]
    net = Net()
    lo_n, lo_bits, seq_bits = net.lo_n, net.lo_bits, net.seq_bits
    rows = sequences * tok_dev
    local_heads = heads // lo_n
    local_width = local_heads * head_size
    head_start = net.lo * local_heads
    unit = w_down.shape[1]
    rows_out = w_out.shape[1]

    def to_groups(x):
        return jnp.concatenate([pick(x, net.hi), net.swap_hi(pick(x, 1 - net.hi))], axis=0)

    def keep_own(x, came):
        return in_order([x[:tok_dev], came], net.hi)

    qkv_blocks = split_columns(w_qkv.reshape(-1, 3 * width), lo_n, local_width)
    qkv_came = lax.all_to_all(qkv_blocks, "lo", 0, 0, tiled=True)
    token_parts = after(tokens, qkv_blocks)
    tokens_came = net.swap_hi(pick(token_parts, 1 - net.hi))
    state = jnp.concatenate([pick(token_parts, net.hi), tokens_came], axis=0).astype(F32)
    flat_in = after(w_in.reshape(-1, w_in.shape[2]), qkv_blocks)
    in_blocks = split_columns(flat_in, net.seq_n, unit)
    in_came = lax.all_to_all(in_blocks, ("hi", "lo"), 0, 0, tiled=True)
    own_qkv = own_columns(qkv_came, layers)
    ring = GatherBoth(net, join_pieces(own_qkv[0], w_out[0], 1))
    normed = rms_scale(state, norm_gains[0, 0]).astype(BF)
    normed_held = net.swap(normed, lo_bits[-1])
    ring.step(tokens_came, ring.own_came)
    first_full = ring.finish()
    own_in = own_columns(in_came, layers)
    own_packs = [join_pieces(own_in[n], w_down[n], 0) for n in range(layers)]
    packs = [lax.all_gather(after(own_packs[0], *ring.by_dp), "dp", axis=0)]

    pair = to_groups(jnp.stack([variate_ids, time_ids], axis=-1))
    pair = jnp.concatenate(net.gather(pair, lo_bits), axis=0)
    tables = head_tables(pair[:, 0], pair[:, 1], head_size)

    def matrices(full):
        full = full.reshape((-1, own_qkv[0].shape[0]) + full.shape[2:])
        blocks = net.gather(full[:, :, 3 * local_width :], lo_bits)
        return full.reshape(-1, full.shape[2]), join_middle(blocks, net.lo, rows_out)

    saved, weights = [], []
    best_scores = jnp.full((layers, heads), FLOOR_VALUE, F32)
    for layer in range(layers):
        final = layer + 1 == layers
        weights.append(matrices(full_next if layer else first_full) + (packs[layer],))
        m_qkv, m_out, pack = weights[layer]
        ring = None
        layer_in = state
        blocks = net.gather(normed, lo_bits, None if layer else normed_held)
        mixed = project(blocks, m_qkv, 3 * local_width)
        if not final:
            own_next = join_pieces(own_qkv[layer + 1], w_out[layer + 1], 1)
            came_next = net.swap_hi(after(own_next, mixed))
        if final:
            seed_grad = to_groups(after(cotangent, blocks[-1]))
            seed_held = [net.swap(after(seed_grad, mixed), seq_bits[-1])]
        bias_pair = lax.dynamic_slice_in_dim(head_bias[layer], head_start, local_heads, 1)
        gains = jnp.concatenate([qk_gains[layer]] * 2, axis=1)
        bias = bias_marks(bias_pair, head_size)
        attended, kept, head_tops = attend(mixed, tables, gains, bias)
        head_tops = head_tops[:, 0, 0] + bias_pair[1]
        best_scores = lax.dynamic_update_slice(
            best_scores, head_tops[None, :], (jnp.int32(layer), head_start)
        )
        leaving = attended
        leaving = after(attended, *(seed_held if final else [came_next]))
        arrived = net.trade(jnp.split(leaving, lo_n, axis=0), lo_bits)
        if not final:
            own_next = in_order([own_next, came_next], net.hi).reshape(-1, own_next.shape[1])
            full_next = lax.all_gather(after(own_next, packs[-1]), "dp", axis=0, tiled=True)
            packs.append(lax.all_gather(after(own_packs[layer + 1], full_next), "dp", axis=0))
            full_next = full_next.reshape((net.dp_n * 2, -1) + full_next.shape[1:])
        middle, second = out_project(layer_in, arrived, m_out, norm_gains[layer, 1], net.lo)

        def forward(n, blocks, pack=pack):
            joined, parts = feed_forward(blocks, pack)
            return [joined] + parts

        second, outs = wave(net, second, forward)
        joined = [out[0] for out in outs]
        partial = [part for out in outs for part in out[1:]]
        if final:
            final_sum = SumAll(net, partial)
        else:
            parts = SumAll(net, partial).parts()
            state, normed = finish_layer(middle, parts, norm_gains[layer + 1, 0])
        saved.append((layer_in, blocks, mixed, gains, bias, kept, arrived, middle, second, joined))

    if len(seq_bits) == 3:
        seed_held = [net.swap(after(seed_grad, outs[0][0]), seq_bits[1])] + seed_held
    gradient = seed_grad.astype(F32)
    qkv_parts = [None] * layers
    out_parts = [None] * layers
    in_parts = [None] * layers
    down_parts = [None] * layers
    norm_parts = [None] * layers
    qk_parts = [None] * layers
    bias_parts = [None] * layers
    hidden_sums = [None] * layers
    attention_sums = [None] * layers
    sums, low = None, seed_grad
    for layer in reversed(range(layers)):
        final = layer + 1 == layers
        m_qkv, m_out, pack = weights[layer]
        layer_in, normed, mixed, gains, bias, kept, arrived, middle, second, joined = saved[layer]

        def backward(n, blocks, joined=joined, pack=pack, final=final, sums=sums):
            if n == 2 and not final:
                blocks = [after(blocks[0], hidden_sums[layer + 1])] + blocks[1:]
            grad_part, gated_part, parts = feed_backward(blocks, joined[n], pack)
            return [grad_part, gated_part] + parts

        held = seed_held if final and len(seq_bits) == 3 else None
        down_in, outs = wave(net, low, backward, held)
        grad_joined, gated = [out[0] for out in outs], [out[1] for out in outs]
        second_sum = SumAll(net, [part for out in outs for part in out[2:]])
        second_sum.step()
        moved = second_sum.moving
        second_sum.step()
        joined_first = after(grad_joined[0], *second_sum.moving)
        grad_hidden = hidden_weights(net, second, [joined_first] + grad_joined[1:], gated, down_in)
        hidden_sums[layer] = lax.psum_scatter(
            grad_hidden, "dp", scatter_dimension=0, tiled=True
        )
        if final:
            final_sum.step(*moved)
        parts = second_sum.parts()
        parts[0] = after(parts[0], grad_hidden, *(final_sum.moving if final else []))
        gradient, gain_second, leaving, shares = out_backward(
            net, gradient, parts, middle, norm_gains[layer, 1], m_out, arrived, rows_out
        )
        if final:
            final_sum.step(leaving[0])
        grad_heads = jnp.concatenate(net.trade(leaving, lo_bits), axis=0)
        share_sum = SumLo(net, [x.reshape(-1, width) for x in shares])
        share_sum.step()
        grad_heads = after(grad_heads, *share_sum.moving)
        out_sum = share_sum.parts()
        grad_query, grad_keys, grad_values, grad_gains, grad_pair = attend_backward(
            mixed, grad_heads, tables, gains, bias, kept
        )
        grads = [grad_query, after(grad_keys, *final_sum.moving) if final else grad_keys, grad_values]
        if not final:
            other_sums = attention_sums[layer + 1]
            other_came = net.swap_hi(after(other_sums[1], leaving[0]))
            grads[2] = after(grad_values, other_came)
            total = other_sums[0].astype(F32) + other_came.astype(F32)
            qkv_parts[layer + 1], out_parts[layer + 1] = split_pieces(
                total, 3 * local_width, rows_out
            )
        last = layer == 0
        mine, other = mixed_weights(net, normed, grads, out_sum, rows_out, F32 if last else BF)
        if last:
            sums = (mine, net.swap_hi(other))
        else:
            sent = [x.reshape(-1, x.shape[2]) for x in (mine, other)]
            attention_sums[layer] = [
                lax.psum_scatter(x, "dp", scatter_dimension=0, tiled=True) for x in sent
            ]
        grads[0] = after(grads[0], other)
        normed_sum = SumLo(net, mixed_backward(grads, m_qkv, rows))
        normed_sum.step()
        gradient, low, gain_first = norm_backward(
            gradient, normed_sum.parts(), layer_in, norm_gains[layer, 0]
        )
        norm_parts[layer] = jnp.stack([gain_first, gain_second])
        qk_parts[layer] = grad_gains.reshape(-1, 2, 2, head_size).sum(axis=(0, 2))
        bias_parts[layer] = lax.dynamic_update_slice(
            jnp.zeros((2, heads), F32), grad_pair[:, 0, :2].T, (jnp.int32(0), head_start)
        )
    both = SumBoth(net, *sums)
    both.step()
    final_sum.step(low)
    qkv_parts[0], out_parts[0] = split_pieces(both.total(), 3 * local_width, rows_out)
    for layer in range(layers):
        in_parts[layer], down_parts[layer] = split_hidden(
            hidden_sums[layer], width // net.dp_n, width
        )
    qkv_parts = return_rows(qkv_parts, "lo", lo_n)
    in_parts = return_rows(in_parts, ("hi", "lo"), net.seq_n)
    parts = final_sum.parts()
    low_state = (saved[-1][7] + sum(x.astype(F32) for x in parts)).astype(BF)
    layer_out = keep_own(low_state, net.swap_hi(low_state[tok_dev:]))
    input_grad = keep_own(low, net.swap_hi(low[tok_dev:])).astype(F32)
    tops = best_scores.size
    small = jnp.concatenate(
        [best_scores.reshape(-1)]
        + [jnp.stack(part).reshape(-1) for part in (norm_parts, qk_parts, bias_parts)]
    )
    small = after(small, both.own, hidden_sums[0])
    is_top = jnp.arange(small.size) < tops
    small = net.all_small(small, lambda a, b: jnp.where(is_top, jnp.maximum(a, b), a + b))
    best_scores = small[:tops].reshape(best_scores.shape)
    small = small[tops:]
    cut_norm, cut_qk = norm_gains.size, norm_gains.size + qk_gains.size
    norm_sum = small[:cut_norm].reshape(norm_gains.shape)
    qk_sum = small[cut_norm:cut_qk].reshape(qk_gains.shape)
    bias_sum = small[cut_qk:].reshape(head_bias.shape)

    factor = jnp.sqrt(CLIP_LIMIT / jnp.maximum(best_scores, CLIP_LIMIT))
    spread = jnp.repeat(factor, head_size, axis=1)
    column_scale = jnp.concatenate([spread, spread, jnp.ones((layers, width), F32)], axis=1)
    clipped = (w_qkv.astype(F32) * column_scale[:, None, :]).astype(BF)
    return (
        layer_out,
        input_grad,
        merge_columns(qkv_parts, layers, local_width),
        jnp.stack(out_parts),
        merge_columns(in_parts, layers, unit),
        jnp.stack(down_parts),
        norm_sum,
        qk_sum,
        bias_sum,
        clipped,
        best_scores,
    )


def solution(mesh):
    def program(*arrays):
        dp_n = mesh.shape["dp"]
        sequences = arrays[0].shape[0] // dp_n
        split = Mesh(mesh.devices.reshape(dp_n, sequences, -1), ("dp", "hi", "lo"))
        seq = ("hi", "lo")
        tokens_spec = P("dp", seq, None)
        rows_spec = P(None, ("dp",) + seq, None)
        ids_spec = P("dp", seq)
        in_specs = (tokens_spec, ids_spec, ids_spec) + (rows_spec,) * 4 + (P(),) * 3
        in_specs += (tokens_spec,)
        out_specs = (tokens_spec,) * 2 + (rows_spec,) * 4 + (P(),) * 3 + (rows_spec, P())
        run = jax.shard_map(
            shards, mesh=split, in_specs=in_specs, out_specs=out_specs, check_vma=False
        )
        return run(*arrays)

    return program
```

```python
import functools
import math

import jax
import jax.numpy as jnp
from jax import lax
from jax.experimental import pallas as pl
from jax.experimental.pallas import tpu as pltpu
from jax.sharding import Mesh
from jax.sharding import PartitionSpec as P

EPSILON = 1e-05
CLIP_LIMIT = 2.0
FLOOR_VALUE = -1e30
BF = jnp.bfloat16
F32 = jnp.float32


def rms_scale(values, gain):
    return values * lax.rsqrt(jnp.mean(values * values, axis=-1, keepdims=True) + EPSILON) * gain


def dot(a, b):
    return jnp.dot(a, b, preferred_element_type=F32)


def pick(array, index, axis=0):
    return lax.dynamic_index_in_dim(array, index, axis, keepdims=False)


class Net:
    def __init__(self):
        self.dp_n, self.hi_n, self.lo_n = (lax.axis_size(name) for name in ("dp", "hi", "lo"))
        self.dp, self.hi, self.lo = (lax.axis_index(name) for name in ("dp", "hi", "lo"))
        self.seq_n = self.hi_n * self.lo_n
        self.seq = self.hi * self.lo_n + self.lo
        self.seq_bits = [1 << b for b in range(self.seq_n.bit_length() - 1)]
        self.lo_bits = [b for b in self.seq_bits if b < self.lo_n]
        self.hi_bits = [b // self.lo_n for b in self.seq_bits if b >= self.lo_n]

    def swap(self, x, bit):
        if bit < self.lo_n:
            return lax.ppermute(x, "lo", [(i, i ^ bit) for i in range(self.lo_n)])
        bit //= self.lo_n
        return lax.ppermute(x, "hi", [(i, i ^ bit) for i in range(self.hi_n)])

    def swap_hi(self, x):
        return self.swap(x, self.lo_n)

    def swap_dp(self, x, bit):
        return lax.ppermute(x, "dp", [(i, i ^ bit) for i in range(self.dp_n)])

    def shift_dp(self, blocks):
        n = self.dp_n
        return [
            lax.ppermute(x, "dp", [(i, (i + k + 1) % n) for i in range(n)])
            for k, x in enumerate(blocks)
        ]

    def gather(self, block, bits, held=None):
        blocks = {0: block}
        if held is not None:
            blocks[bits[-1]] = held
        for bit in reversed(bits):
            for r in list(blocks):
                if r & bit:
                    continue
                if r | bit in blocks:
                    continue
                blocks[r | bit] = self.swap(blocks[r], bit)
        return [blocks[r] for r in range(len(blocks))]

    def add_swapped(self, mine, sent, bit):
        return mine.astype(F32) + self.swap(sent.astype(BF), bit).astype(F32)

    def scatter(self, blocks, bits):
        blocks = dict(enumerate(blocks))
        for bit in bits:
            blocks = self.halve(blocks, bit)
        return blocks[0]

    def halve(self, blocks, bit):
        return {
            r: self.add_swapped(blocks[r], blocks[r | bit], bit)
            for r in sorted(blocks, reverse=True)
            if not r & bit
        }

    def trade(self, blocks, bits):
        return Trade(self, blocks, bits).finish()

    def all_small(self, x, combine):
        for bit in self.seq_bits:
            x = combine(x, self.swap(x, bit))
        bit = 1
        while bit < self.dp_n:
            x = combine(x, self.swap_dp(x, bit))
            bit *= 2
        return x


class Trade:
    def __init__(self, net, blocks, bits):
        self.net, self.blocks, self.left, self.moving = net, list(blocks), list(bits), []

    def step(self, *earlier):
        bit = self.left.pop()
        moving = [r for r in range(len(self.blocks)) if r & bit]
        if bit == 1:
            self.moving = [self.net.swap(after(self.blocks[r], *earlier), bit) for r in moving]
            for r, x in zip(moving, self.moving):
                self.blocks[r] = x
            return
        rows = self.blocks[0].shape[0]
        sent = after(jnp.concatenate([self.blocks[r] for r in moving], axis=0), *earlier)
        self.moving = [self.net.swap(sent, bit)]
        for n, r in enumerate(moving):
            self.blocks[r] = self.moving[0][n * rows : (n + 1) * rows]

    def finish(self):
        while self.left:
            self.step()
        return self.blocks


class SumAll:
    def __init__(self, net, blocks):
        self.net, self.blocks, self.moving, self.step_n = net, blocks, [], 0
        self.low = []

    def step(self, *earlier):
        net, bits = self.net, self.net.seq_bits
        self.step_n += 1
        if len(bits) != 3:
            if self.step_n == 1:
                self.blocks = [net.scatter(self.blocks, bits)]
            self.moving = []
            return
        core, first, second = bits
        half = self.blocks[0].shape[0] // 2
        if self.step_n == 1:
            order = (first | second, first, second, 0)
            self.moving = [net.swap(after(self.blocks[r | core], *earlier), core) for r in order]
            self.pairs = {r: [self.blocks[r], x] for r, x in zip(order, self.moving)}
        elif self.step_n == 2:
            top, bottom = add_low([self.pairs[first | second]], cut=half)
            self.moving = [
                net.swap(after(top, *earlier), first),
                net.swap(after(bottom, *earlier), second),
            ]
        else:
            top, bottom = (after(x, *earlier) for x in self.moving)
            self.low = add_low(
                [self.pairs[first], self.pairs[second]], [(half, bottom), (0, top)]
            )
            self.moving = [net.swap(x, bit) for x, bit in zip(self.low, (first, second))]

    def parts(self):
        while self.step_n < 3:
            self.step()
        return self.pairs[0] + self.moving if self.moving else self.blocks


class SumLo:
    def __init__(self, net, blocks):
        self.net, self.blocks = net, blocks

    def step(self, *earlier):
        net = self.net
        if len(net.lo_bits) != 2:
            self.left = [net.scatter(self.blocks, net.lo_bits)]
            self.moving = []
            return
        self.moving = [net.swap(after(self.blocks[r | 1], *earlier), 1) for r in (2, 0)]
        self.left = [self.blocks[0], self.moving[1]]

    def parts(self, *earlier):
        if self.moving:
            (far,) = add_low([[self.blocks[2], self.moving[0]]])
            self.moving = [self.net.swap(after(far, *earlier), 2)]
        return self.left + self.moving


class GatherBoth:
    def __init__(self, net, own, *earlier):
        self.net, self.own = net, own
        own = after(own, *earlier)
        self.own_came = net.swap_hi(own)
        self.by_dp = net.shift_dp([own] * (net.dp_n - 1))
        self.moving = [self.own_came] + self.by_dp

    def step(self, *earlier):
        self.rest_came = self.net.swap_hi(after(jnp.concatenate(self.by_dp, axis=0), *earlier))
        self.moving = [self.rest_came]

    def finish(self):
        net = self.net
        rows, columns = self.own.shape
        n = net.dp_n

        def kernel(at, own, own_came, rest_came, *refs):
            *by_dp, out = refs
            dp, hi = at[0] // 2, at[0] % 2
            out[at[0]] = own[...]
            out[dp * 2 + 1 - hi] = own_came[...]
            for k in range(1, n):
                source = lax.rem(dp + n - k, n)
                out[source * 2 + hi] = by_dp[k - 1][...]
                out[source * 2 + 1 - hi] = rest_came[(k - 1) * rows : k * rows, :]

        return on_chip(
            kernel,
            [((2 * n, rows, columns), BF)],
            self.own,
            self.own_came,
            self.rest_came,
            *self.by_dp,
            at=net.dp * 2 + net.hi,
            name="join_gathered",
        )[0]


class SumBoth:
    def __init__(self, net, mine, came):
        n = net.dp_n

        def kernel(at, x, y, own, *outs):
            own[...] = x[at[0]] + y[at[0]].astype(F32)
            for k, out in enumerate(outs):
                to = lax.rem(at[0] + k + 1, n)
                out[...] = (x[to] + y[to].astype(F32)).astype(BF)

        shape = mine.shape[1:]
        self.own, *self.blocks = on_chip(
            kernel, [(shape, F32)] + [(shape, BF)] * (n - 1), mine, came, at=net.dp, name="sum_hi"
        )
        self.net = net

    def step(self, *earlier):
        self.blocks[0] = after(self.blocks[0], *earlier)
        self.moving = self.net.shift_dp(self.blocks)

    def total(self):
        return self.own + sum(x.astype(F32) for x in self.moving)


def after(x, *earlier):
    return lax.optimization_barrier((x,) + earlier)[0]


def in_order(blocks, index):
    stacked = jnp.stack(blocks)
    return jnp.stack([pick(stacked, index ^ j) for j in range(len(blocks))])


def split_columns(shard, count, width):
    rows = shard.shape[0]
    parts = shard.shape[1] // count // width
    if width % LANES:
        shard = shard.reshape(rows, parts, count, width).transpose(2, 0, 1, 3)
        return shard.reshape(count, rows, parts * width)

    def kernel(shard_ref, out):
        for r in range(count):
            for p in range(parts):
                start = (p * count + r) * width
                out[r, :, p * width : (p + 1) * width] = shard_ref[:, start : start + width]

    return on_chip(kernel, [((count, rows, parts * width), BF)], shard, name="split_columns")[0]


def merge_columns(blocks, layers, width):
    count, rows = blocks.shape[0], blocks.shape[1] // layers
    parts = blocks.shape[2] // width
    columns = parts * count * width
    if width % LANES:
        shards = blocks.reshape(count, layers, rows, parts, width).transpose(1, 2, 3, 0, 4)
        return shards.reshape(layers, rows, columns).astype(F32)

    def kernel(ref, out):
        for r in range(count):
            for layer in range(layers):
                for p in range(parts):
                    start = (p * count + r) * width
                    part = ref[r, layer * rows : (layer + 1) * rows, p * width : (p + 1) * width]
                    out[layer, :, start : start + width] = part.astype(F32)

    return on_chip(kernel, [((layers, rows, columns), F32)], blocks, name="merge_columns")[0]


def own_columns(blocks, layers):
    count, rows, columns = blocks.shape
    blocks = blocks.reshape(count, layers, rows // layers, columns)
    return [blocks[:, n].reshape(-1, columns) for n in range(layers)]


def return_rows(layers, axes, count, *earlier):
    own = jnp.stack([x.astype(BF).reshape(count, -1, x.shape[1]) for x in layers], axis=1)
    own = own.reshape(count, -1, own.shape[-1])
    return lax.all_to_all(after(own, *earlier), axes, 0, 0, tiled=True)


def join_pieces(own, other, axis):
    if axis == 1:
        pieces = jnp.split(other, own.shape[0] // other.shape[0], axis=1)
        return jnp.concatenate([own, jnp.concatenate(pieces, axis=0)], axis=1)
    return jnp.concatenate([own] + jnp.split(other, other.shape[1] // own.shape[1], axis=1))


def split_hidden(own, rows_in, width):
    pieces = width // own.shape[1]
    down = jnp.concatenate(jnp.split(own[rows_in:], pieces, axis=0), axis=1)
    return own[:rows_in], down.astype(F32)


LANES = 128
NT = (((1,), (1,)), ((), ()))
TN = (((0,), (0,)), ((), ()))
VMEM = pl.BlockSpec(memory_space=pltpu.VMEM)
SMEM = pl.BlockSpec(memory_space=pltpu.SMEM)
LIMIT = 16 * 2**20
WEIGHT_LIMIT = 32 * 2**20


def on_chip(kernel, outs, *arrays, at=None, scratch=(), flops=0, name=None):
    outs = [jax.ShapeDtypeStruct(*out) for out in outs]
    moved = sum(math.prod(x.shape) * x.dtype.itemsize for x in list(arrays) + outs)
    first = [] if at is None else [at.astype(jnp.int32).reshape(1)]
    return pl.pallas_call(
        kernel,
        in_specs=[SMEM] * len(first) + [VMEM] * len(arrays),
        out_specs=[VMEM] * len(outs),
        out_shape=outs,
        scratch_shapes=list(scratch),
        compiler_params=pltpu.CompilerParams(vmem_limit_bytes=LIMIT),
        cost_estimate=pl.CostEstimate(flops=flops, bytes_accessed=moved, transcendentals=0),
        name=name,
    )(*first, *arrays)


def add_low(groups, extras=None, cut=None):
    shape = groups[0][0].shape
    extras = extras or [None] * len(groups)
    flat, counts = [], []
    for group, extra in zip(groups, extras):
        members = group + ([extra[1]] if extra else [])
        counts.append(len(members))
        flat += members

    def kernel(*refs):
        ins, outs = list(refs[: len(flat)]), list(refs[len(flat) :])
        for count, extra in zip(counts, extras):
            members = [ins.pop(0) for _ in range(count)]
            last = members.pop() if extra else None
            total = sum(x[...].astype(F32) for x in members)
            if extra:
                rows = last.shape[0]
                part = total[extra[0] : extra[0] + rows] + last[...].astype(F32)
                pieces = [total[: extra[0]], part, total[extra[0] + rows :]]
                total = jnp.concatenate([p for p in pieces if p.shape[0]], axis=0)
            total = total.astype(BF)
            if cut is None:
                outs.pop(0)[...] = total
            else:
                outs.pop(0)[...] = total[:cut]
                outs.pop(0)[...] = total[cut:]

    if cut is None:
        shapes = [(shape, BF)] * len(groups)
    else:
        shapes = [((cut,) + shape[1:], BF), ((shape[0] - cut,) + shape[1:], BF)]
    return on_chip(kernel, shapes, *flat, name="add_low")


def finish_layer(middle, parts, gain):
    rows, width = middle.shape

    def kernel(x, g, *refs):
        *ins, state, normed = refs
        total = x[...] + sum(part[...].astype(F32) for part in ins)
        state[...] = total
        normed[...] = rms_scale(total, g[...]).astype(BF)

    outs = [((rows, width), F32), ((rows, width), BF)]
    return on_chip(kernel, outs, middle, gain.reshape(1, width), *parts, name="finish_layer")


def norm_backward(gradient, parts, values, gain):
    rows, width = gradient.shape

    def kernel(g, x, gn, *refs):
        *ins, new, low, gain_out = refs
        total = sum(part[...].astype(F32) for part in ins)
        grad, gain_part = norm_adjoint(x[...], gn[...], total)
        grad = g[...] + grad
        new[...] = grad
        low[...] = grad.astype(BF)
        gain_out[...] = gain_part

    outs = [((rows, width), F32), ((rows, width), BF), ((1, width), F32)]
    arrays = [gradient, values, gain.reshape(1, width)]
    new, low, gain_part = on_chip(kernel, outs, *arrays, *parts, name="norm_backward")
    return new, low, gain_part[0]


def norm_adjoint(values, gain, grad):
    inverse = lax.rsqrt(jnp.mean(values * values, axis=-1, keepdims=True) + EPSILON)
    normal = values * inverse
    gain_part = jnp.sum(grad * normal, axis=0, keepdims=True)
    grad = grad * gain
    grad = (grad - normal * jnp.mean(grad * normal, axis=-1, keepdims=True)) * inverse
    return grad, gain_part


def project(blocks, matrix, columns):
    rows = blocks[0].shape[0]

    def kernel(*refs):
        *ins, m, out = refs
        for n, x in enumerate(ins):
            out[n * rows : (n + 1) * rows, :] = dot(x[...], m[:, :columns]).astype(BF)

    return on_chip(
        kernel,
        [((rows * len(blocks), columns), BF)],
        *blocks,
        matrix,
        flops=2 * rows * len(blocks) * matrix.size,
        name="project",
    )[0]


def out_project(state, arrived, matrix, gain, at):
    rows, width = state.shape
    heads = arrived[0].shape[1]

    def kernel(index, x, m, g, *refs):
        *ins, middle, second = refs
        total = x[...]
        for r, block in enumerate(ins):
            start = pl.multiple_of((index[0] ^ r) * heads, heads)
            total = total + dot(block[...], m[pl.ds(start, heads), :])
        middle[...] = total
        second[...] = rms_scale(total, g[...]).astype(BF)

    return on_chip(
        kernel,
        [((rows, width), F32), ((rows, width), BF)],
        state,
        matrix,
        gain.reshape(1, width),
        *arrived,
        at=at,
        flops=2 * rows * matrix.size,
        name="out_project",
    )


def hidden_matrices(pack, width):
    rows = width // pack.shape[0]
    columns = pack.shape[2]
    down = (pack.shape[1] - rows) * columns // width
    m_in = jnp.concatenate([pack[n, :rows, :] for n in range(pack.shape[0])], axis=0)
    m_down = []
    for n in range(pack.shape[0]):
        starts = range(rows, pack.shape[1], down)
        m_down.append(jnp.concatenate([pack[n, p : p + down, :] for p in starts], axis=1))
    return m_in, jnp.concatenate(m_down, axis=0)


def feed_forward(blocks, pack):
    rows, width = blocks[0].shape
    count, hidden = len(blocks), pack.shape[2] // 2

    def kernel(*refs):
        m, ins, joined, outs = refs[0], refs[1 : count + 1], refs[count + 1], refs[count + 2 :]
        m_in, m_down = hidden_matrices(m, width)
        for n, (x, out) in enumerate(zip(ins, outs)):
            both = dot(x[...], m_in)
            joined[n * rows : (n + 1) * rows, :] = both.astype(BF)
            gate, up = both[:, :hidden], both[:, hidden:]
            gated = gate / (1.0 + jnp.exp(-gate)) * up
            out[...] = dot(gated.astype(BF), m_down).astype(BF)

    joined, *parts = on_chip(
        kernel,
        [((rows * count, 2 * hidden), BF)] + [((rows, width), BF)] * count,
        pack,
        *blocks,
        flops=2 * rows * count * pack.size,
        name="feed_forward",
    )
    return joined, parts


def feed_backward(blocks, joined, pack):
    rows, width = blocks[0].shape
    count, hidden = len(blocks), pack.shape[2] // 2

    def kernel(*refs):
        m, ins, (j, grad_joined, gated) = refs[0], refs[1 : count + 1], refs[count + 1 : count + 4]
        m_in, m_down = hidden_matrices(m, width)
        for n, (x, out) in enumerate(zip(ins, refs[count + 4 :])):
            part = slice(n * rows, (n + 1) * rows)
            gate = j[part, :hidden].astype(F32)
            up = j[part, hidden:].astype(F32)
            grad = lax.dot_general(x[...], m_down, NT, preferred_element_type=F32)
            sigmoid = 1.0 / (1.0 + jnp.exp(-gate))
            silu = gate * sigmoid
            gated[part, :] = (silu * up).astype(BF)
            grad_gate = grad * up * (sigmoid + silu * (1.0 - sigmoid))
            grad_joined[part, :hidden] = grad_gate.astype(BF)
            grad_joined[part, hidden:] = (grad * silu).astype(BF)
            total = lax.dot_general(grad_joined[part, :], m_in, NT, preferred_element_type=F32)
            out[...] = total.astype(BF)

    grad_joined, gated, *parts = on_chip(
        kernel,
        [((rows * count, 2 * hidden), BF), ((rows * count, hidden), BF)]
        + [((rows, width), BF)] * count,
        pack,
        *blocks,
        joined,
        flops=2 * rows * count * pack.size,
        name="feed_backward",
    )
    return grad_joined, gated, parts


def side_by_side(refs, scratch, sems, start=0):
    copies, column = [], 0
    for group in refs:
        row = 0
        for x in group:
            place = scratch.at[pl.ds(row, x.shape[0]), pl.ds(column, x.shape[1])]
            copies.append(pltpu.make_async_copy(x, place, sems.at[start + len(copies)]))
            row += x.shape[0]
        column += group[0].shape[1]
    return copies


def weight_call(kernel, outs, groups, shapes, at, flops, name):
    flat = [x for group in groups for column in group for x in column]
    outs = [jax.ShapeDtypeStruct(*out) for out in outs]
    moved = sum(math.prod(x.shape) * x.dtype.itemsize for x in flat + outs)

    def body(index, *refs):
        ins, refs = list(refs[: len(flat)]), refs[len(flat) :]
        results, scratch, sems = refs[: len(outs)], refs[len(outs) : -1], refs[-1]
        arrived, count = [], 0
        for group, target in zip(groups, scratch):
            taken = [[ins.pop(0) for x in column] for column in group]
            copies = side_by_side(taken, target, sems, count)
            count += len(copies)
            for copy in copies:
                copy.start()
            arrived.append(Arriving(copies, target))
        kernel(index, *arrived, *results)

    return pl.pallas_call(
        body,
        in_specs=[SMEM] + [pl.BlockSpec(memory_space=pl.ANY)] * len(flat),
        out_specs=[VMEM] * len(outs),
        out_shape=outs,
        scratch_shapes=[pltpu.VMEM(shape, BF) for shape in shapes]
        + [pltpu.SemaphoreType.DMA((len(flat),))],
        compiler_params=pltpu.CompilerParams(vmem_limit_bytes=WEIGHT_LIMIT),
        cost_estimate=pl.CostEstimate(flops=flops, bytes_accessed=moved, transcendentals=0),
        name=name,
    )(at.astype(jnp.int32).reshape(1), *flat)


class Arriving:
    def __init__(self, copies, ref):
        self.copies, self.ref = copies, ref

    def __getitem__(self, index):
        for copy in self.copies:
            copy.wait()
        self.copies = []
        return self.ref[index]


def hidden_weights(net, second, grad_joined, gated, grads):
    length = sum(x.shape[0] for x in second)
    width, columns, hidden = second[0].shape[1], grad_joined[0].shape[1], gated[0].shape[1]
    rows, down = width // net.dp_n, hidden // net.dp_n
    pieces = width // columns

    def kernel(index, a, b, c, d, out):
        for n in range(net.dp_n):
            left = a[:, n * rows : (n + 1) * rows]
            first = n * (rows + pieces * down)
            out[first : first + rows, :] = lax.dot_general(
                left, b[...], TN, preferred_element_type=F32
            ).astype(BF)
            left = c[:, n * down : (n + 1) * down]
            total = lax.dot_general(left, d[...], TN, preferred_element_type=F32).astype(BF)
            for p in range(pieces):
                start = first + rows + p * down
                out[start : start + down, :] = total[:, p * columns : (p + 1) * columns]

    return weight_call(
        kernel,
        [((net.dp_n * (rows + pieces * down), columns), BF)],
        [[second], [grad_joined], [gated], [grads]],
        [(length, width), (length, columns), (length, hidden), (length, width)],
        net.dp,
        2 * length * width * (columns + hidden),
        "hidden_weights",
    )[0]


def mixed_weights(net, normed, grads, shares, rows, kept):
    length, width = sum(x.shape[0] for x in normed), normed[0].shape[1]
    columns = sum(g.shape[1] for g in grads)
    chunk = width // net.dp_n // net.hi_n
    pieces = chunk // rows
    c = shares[0].shape[1] // pieces

    def kernel(index, a, b, *refs):
        *parts, mine, other = refs
        for n in range(net.dp_n * net.hi_n):
            left = a[:, n * chunk : (n + 1) * chunk]
            total = lax.dot_general(left, b[...], TN, preferred_element_type=F32)
            out = sum(part[n * rows : (n + 1) * rows, :].astype(F32) for part in parts)
            here = index[0] == n % net.hi_n

            def store(target, kind, n=n, total=total, out=out):
                target[n // net.hi_n, :, :columns] = total.astype(kind)
                for p in range(pieces):
                    cut = out[:, p * c : (p + 1) * c].astype(kind)
                    target[n // net.hi_n, p * rows : (p + 1) * rows, columns:] = cut

            pl.when(here)(lambda: store(mine, kept))
            pl.when(jnp.logical_not(here))(lambda: store(other, BF))

    shape = (net.dp_n, chunk, columns + c)
    flat = [x.astype(BF) for x in shares]
    return weight_call(
        kernel,
        [(shape, kept), (shape, BF)],
        [[normed], [[g] for g in grads]] + [[[x]] for x in flat],
        [(length, width), (length, columns)] + [x.shape for x in flat],
        net.hi,
        2 * length * width * columns,
        "mixed_weights",
    )


def split_pieces(own, columns, rows):
    pieces = own.shape[0] // rows
    return own[:, :columns], jnp.concatenate(jnp.split(own[:, columns:], pieces, axis=0), axis=1)


def out_backward(net, gradient, parts, middle, gain, matrix, arrived, rows_out):
    rows, width = gradient.shape
    count, heads = len(arrived), arrived[0].shape[1]
    groups = width // rows_out // count

    def kernel(index, g, mid, gn, *refs):
        sums, m, refs = refs[: len(parts)], refs[len(parts)], refs[len(parts) + 1 :]
        ins, (new, gain_out), refs = refs[:count], refs[count : count + 2], refs[count + 2 :]
        leaving, shares, scratch = refs[:count], refs[count : 2 * count], refs[2 * count]
        total = sum(part[...].astype(F32) for part in sums)
        grad, gain_out[...] = norm_adjoint(mid[...], gn[...], total)
        grad = g[...] + grad
        new[...] = grad
        branch = grad.astype(BF)
        for r in range(count):
            start = pl.multiple_of((index[0] ^ r) * heads, heads)
            leaving[r][...] = lax.dot_general(
                branch, m[pl.ds(start, heads), :], NT, preferred_element_type=F32
            ).astype(BF)
            block = lax.dot_general(ins[r][...], branch, TN, preferred_element_type=F32)
            scratch[pl.ds(pl.multiple_of(start // rows_out, heads // rows_out), heads // rows_out)] = (
                block.reshape(heads // rows_out, rows_out, width)
            )
        for r in range(count):
            for n in range(groups):
                shares[r][n] = scratch[n * count + (index[0] ^ r)].astype(BF)

    outs = on_chip(
        kernel,
        [((rows, width), F32), ((1, width), F32)]
        + [((rows, heads), BF)] * count
        + [((groups, rows_out, width), BF)] * count,
        gradient,
        middle,
        gain.reshape(1, width),
        *parts,
        matrix,
        *arrived,
        at=net.lo,
        scratch=[pltpu.VMEM((width // rows_out, rows_out, width), F32)],
        flops=4 * rows * matrix.size,
        name="out_backward",
    )
    return outs[0], outs[1][0], outs[2 : 2 + count], outs[2 + count :]


def mixed_backward(grads, matrix, rows):
    length = grads[0].shape[0]
    count = length // rows
    width = grads[0].shape[1]

    def kernel(q, k, v, m, *outs):
        for n, out in enumerate(outs):
            part = slice(n * rows, (n + 1) * rows)
            x = jnp.concatenate([q[part, :], k[part, :], v[part, :]], axis=1)
            out[...] = lax.dot_general(
                x, m[:, : 3 * width], NT, preferred_element_type=F32
            ).astype(BF)

    return on_chip(
        kernel,
        [((rows, matrix.shape[0]), BF)] * count,
        *grads,
        matrix,
        flops=2 * length * matrix.size,
        name="mixed_backward",
    )


def join_middle(blocks, index, rows):
    n, stacked, c = blocks[0].shape
    count, pieces = len(blocks), stacked // rows
    if rows % 16:
        full = in_order(blocks, index).reshape(count, n, pieces, rows, c)
        return full.transpose(1, 0, 3, 2, 4).reshape(-1, pieces * c)

    def kernel(at, *refs):
        for r, block in enumerate(refs[:-1]):
            for i in range(n):
                start = pl.multiple_of((i * count + (at[0] ^ r)) * rows, rows)
                for p in range(pieces):
                    refs[-1][pl.ds(start, rows), p * c : (p + 1) * c] = block[
                        i, p * rows : (p + 1) * rows, :
                    ]

    shape = (n * count * rows, pieces * c)
    return on_chip(kernel, [(shape, BF)], *blocks, at=index, name="join_middle")[0]


def lane_ids():
    return lax.broadcasted_iota(jnp.int32, (1, LANES), 1)


def three_parts(x):
    hi = x.astype(BF).astype(F32)
    mid = (x - hi).astype(BF).astype(F32)
    return hi, mid, x - hi - mid


def group_sum(x, width):
    rows = lax.broadcasted_iota(jnp.int32, (LANES, LANES), 0) // width
    columns = lax.broadcasted_iota(jnp.int32, (LANES, LANES), 1) // width
    ones = jnp.where(rows == columns, 1.0, 0.0).astype(BF)
    return sum(dot(part.astype(BF), ones) for part in three_parts(x))


def swap_halves(x, half):
    front = (lane_ids() // half) % 2 == 0
    return jnp.where(front, pltpu.roll(x, LANES - half, 1), pltpu.roll(x, half, 1))


def head_prep(raw, gain, cosine, sine, width):
    raw = raw.astype(F32)
    inverse = lax.rsqrt(group_sum(raw * raw, width) * (1.0 / width) + EPSILON)
    scaled = raw * inverse * gain
    return scaled * cosine + swap_halves(scaled, width // 2) * sine, inverse


def attend_kernel(
    rows, query_in, key_in, value_in, cosine, sine, marks, gains, bias, attended, kept, tops
):
    length = query_in.shape[0]
    width = LANES // 2
    low = lane_ids() < width
    query, unused = head_prep(query_in[...], gains[0:1, :], cosine[...], sine[...], width)
    keys, unused = head_prep(key_in[...], gains[1:2, :], cosine[...], sine[...], width)
    query = query * (1.0 / math.sqrt(width))
    mark = marks[...].astype(F32)
    value = value_in[...].astype(F32)
    heads = []
    for h in range(2):
        shift = (lambda x: pltpu.roll(x, width, 1)) if h else (lambda x: x)
        heads.append(
            (
                jnp.where(low, shift(query), mark * bias[0, h : h + 1, :]).astype(BF),
                jnp.where(low, shift(keys), mark).astype(BF),
                jnp.where(low, shift(value), 1.0).astype(BF),
            )
        )
    best = [None, None]
    for start in range(0, length, rows):
        part = slice(start, start + rows)
        outs = []
        for h, (head_query, head_keys, head_value) in enumerate(heads):
            scores = lax.dot_general(head_query[part], head_keys, NT, preferred_element_type=F32)
            top = jnp.max(scores, axis=0, keepdims=True)
            best[h] = top if best[h] is None else jnp.maximum(best[h], top)
            mixed = dot(jnp.exp(scores).astype(BF), head_value)
            out = jnp.where(low, mixed / pltpu.roll(mixed, width, 1), jnp.log(mixed))
            kept[h, part, :] = out
            outs.append(out)
        attended[part, :] = jnp.where(low, outs[0], pltpu.roll(outs[1], width, 1)).astype(BF)
    for h in range(2):
        tops[h, :, :] = jnp.broadcast_to(jnp.max(best[h], axis=1, keepdims=True), (8, LANES))


def attend_backward_kernel(
    columns,
    query_in,
    key_in,
    value_in,
    grad_in,
    cosine,
    sine,
    marks,
    gains,
    bias,
    kept,
    grad_query,
    grad_key,
    grad_value,
    grad_gains,
    grad_bias,
    keys_turned,
    sum_keys,
    sum_values,
):
    length = query_in.shape[0]
    width = LANES // 2
    lane = lane_ids()
    low = lane < width
    scale = 1.0 / math.sqrt(width)
    query, query_inverse = head_prep(query_in[...], gains[0:1, :], cosine[...], sine[...], width)
    keys, key_inverse = head_prep(key_in[...], gains[1:2, :], cosine[...], sine[...], width)
    query = query * scale
    mark = marks[...].astype(F32)
    value = value_in[...].astype(F32)
    grads = grad_in[...].astype(F32)

    def place(x, first, other):
        for offset, part in enumerate(three_parts(x)):
            other = jnp.where(lane == first + offset, part, other)
        return other

    all_query, all_keys, all_values = [], [], []
    for h in range(2):
        shift = (lambda x: pltpu.roll(x, width, 1)) if h else (lambda x: x)
        out = kept[h]
        query_marks = place(-out, width + 12, mark * bias[0, h : h + 1, :])
        head_query = jnp.where(low, shift(query), query_marks).astype(BF)
        head_keys = jnp.where(low, shift(keys), mark).astype(BF)
        ones = jnp.where(lane < width + 3, 1.0, 0.0)
        head_value = jnp.where(low, shift(value), ones).astype(BF)
        head_grad = jnp.where(low, shift(grads), 0.0)
        inner = pltpu.roll(-group_sum(head_grad * out, width), width, 1)
        head_grad = place(inner, width, head_grad).astype(BF)
        keys_turned[...] = head_keys.astype(F32).T.astype(BF)
        turned = []
        for start in range(0, length, columns):
            part = slice(start, start + columns)
            scores = lax.dot_general(head_keys, head_query[part], NT, preferred_element_type=F32)
            probability = jnp.exp(scores)
            grad_prob = lax.dot_general(
                head_value, head_grad[part], NT, preferred_element_type=F32
            )
            grad_scores = (probability * grad_prob).astype(BF)
            part_values = dot(probability.astype(BF), head_grad[part])
            part_keys = dot(grad_scores, head_query[part])
            if start:
                sum_values[...] += part_values
                sum_keys[...] += part_keys
            else:
                sum_values[...] = part_values
                sum_keys[...] = part_keys
            turned.append(dot(keys_turned[...], grad_scores).T)
        head_sum = jnp.concatenate(turned, axis=0)
        equal = jnp.where((lane >= width) & (lane < width + 4), mark, 0.0)
        match = jnp.sum(jnp.sum(head_sum * equal, axis=0, keepdims=True), axis=1, keepdims=True)
        total = jnp.sum(
            jnp.where(lane == width + 12, jnp.sum(head_sum, axis=0, keepdims=True), 0.0),
            axis=1,
            keepdims=True,
        )
        both = jnp.where(lane == 0, match, total - match)
        grad_bias[h, :, :] = jnp.broadcast_to(both, (8, LANES))
        all_query.append(head_sum * scale)
        all_keys.append(sum_keys[...])
        all_values.append(sum_values[...])

    def join(pair):
        return jnp.where(low, pair[0], pltpu.roll(pair[1], width, 1))

    grad_value[...] = join(all_values).astype(BF)
    for n, (pair, raw, inverse, out) in enumerate(
        (
            (all_query, query_in, query_inverse, grad_query),
            (all_keys, key_in, key_inverse, grad_key),
        )
    ):
        grad = join(pair)
        grad = grad * cosine[...] - swap_halves(grad, width // 2) * sine[...]
        normal = raw[...].astype(F32) * inverse
        grad_gains[0, n : n + 1, :] = jnp.sum(grad * normal, axis=0, keepdims=True)
        grad = grad * gains[n : n + 1, :]
        mean = group_sum(grad * normal, width) * (1.0 / width)
        out[...] = ((grad - normal * mean) * inverse).astype(BF)


def lane_block(length, offset):
    return pl.BlockSpec((length, LANES), lambda i: (0, offset + i))


def whole_block(shape):
    return pl.BlockSpec(shape, lambda i: (0,) * len(shape))


def attend(mixed, tables, gains, bias):
    length, heads = mixed.shape[0], bias.shape[0]
    pairs = heads // 2
    block = lane_block
    return pl.pallas_call(
        functools.partial(attend_kernel, min(256, length)),
        grid=(pairs,),
        in_specs=[
            block(length, 0),
            block(length, pairs),
            block(length, 2 * pairs),
            whole_block((length, LANES)),
            whole_block((length, LANES)),
            whole_block((length, LANES)),
            whole_block((2, LANES)),
            pl.BlockSpec((1, 2, LANES), lambda i: (i, 0, 0)),
        ],
        out_specs=[
            block(length, 0),
            pl.BlockSpec((2, length, LANES), lambda i: (i, 0, 0)),
            pl.BlockSpec((2, 8, LANES), lambda i: (i, 0, 0)),
        ],
        out_shape=[
            jax.ShapeDtypeStruct((length, pairs * LANES), BF),
            jax.ShapeDtypeStruct((heads, length, LANES), F32),
            jax.ShapeDtypeStruct((heads, 8, LANES), F32),
        ],
        compiler_params=pltpu.CompilerParams(vmem_limit_bytes=16 * 2**10 * max(1024, length)),
        cost_estimate=pl.CostEstimate(
            flops=8 * heads * length * length * LANES,
            bytes_accessed=16 * length * pairs * LANES,
            transcendentals=heads * length * length,
        ),
        name="attend",
    )(mixed, mixed, mixed, *tables, gains, bias.reshape(pairs, 2, LANES))


def attend_backward(mixed, grad, tables, gains, bias, kept):
    length, heads = mixed.shape[0], bias.shape[0]
    pairs = heads // 2
    block = lane_block
    flat = jax.ShapeDtypeStruct((length, pairs * LANES), BF)
    return pl.pallas_call(
        functools.partial(attend_backward_kernel, min(256, length)),
        grid=(pairs,),
        in_specs=[
            block(length, 0),
            block(length, pairs),
            block(length, 2 * pairs),
            block(length, 0),
            whole_block((length, LANES)),
            whole_block((length, LANES)),
            whole_block((length, LANES)),
            whole_block((2, LANES)),
            pl.BlockSpec((1, 2, LANES), lambda i: (i, 0, 0)),
            pl.BlockSpec((2, length, LANES), lambda i: (i, 0, 0)),
        ],
        out_specs=[
            block(length, 0),
            block(length, 0),
            block(length, 0),
            pl.BlockSpec((1, 2, LANES), lambda i: (i, 0, 0)),
            pl.BlockSpec((2, 8, LANES), lambda i: (i, 0, 0)),
        ],
        out_shape=[
            flat,
            flat,
            flat,
            jax.ShapeDtypeStruct((pairs, 2, LANES), F32),
            jax.ShapeDtypeStruct((heads, 8, LANES), F32),
        ],
        scratch_shapes=[
            pltpu.VMEM((LANES, length), BF),
            pltpu.VMEM((length, LANES), F32),
            pltpu.VMEM((length, LANES), F32),
        ],
        compiler_params=pltpu.CompilerParams(vmem_limit_bytes=16 * 2**10 * max(1024, length)),
        cost_estimate=pl.CostEstimate(
            flops=20 * heads * length * length * LANES,
            bytes_accessed=24 * length * pairs * LANES,
            transcendentals=heads * length * length,
        ),
        name="attend_backward",
    )(mixed, mixed, mixed, grad, *tables, gains, bias.reshape(pairs, 2, LANES), kept)


def head_tables(ids, places, width):
    frequency = jnp.exp(jnp.arange(width // 2, dtype=F32) * (-2.0 * math.log(10000.0) / width))
    angles = places.astype(F32)[:, None] * frequency
    cosine, sine = jnp.cos(angles), jnp.sin(angles)
    lane = jnp.arange(LANES)[None, :]
    equal = (ids[:, None] == (lane - width) % 4) & (lane >= width) & (lane < width + 12)
    plain = (lane >= width + 12) & (lane < width + 15)
    return (
        jnp.concatenate([cosine] * 4, axis=1),
        jnp.concatenate([-sine, sine, -sine, sine], axis=1),
        (equal | plain).astype(BF),
    )


def bias_marks(pair, width):
    gap = pair[0] - pair[1]
    hi = lax.reduce_precision(gap, 8, 7)
    mid = lax.reduce_precision(gap - hi, 8, 7)
    lane = jnp.arange(LANES)[None, :]
    marks = jnp.zeros((pair.shape[1], LANES), F32)
    for n, part in enumerate((hi, mid, gap - hi - mid)):
        inside = (lane >= width + 4 * n) & (lane < width + 4 * n + 4)
        marks = jnp.where(inside, part[:, None], marks)
    return marks


def wave(net, own, compute, held=None):
    bits = net.seq_bits
    if len(bits) != 3:
        blocks = net.gather(own, bits)
        cuts = (blocks[: len(blocks) // 2], blocks[len(blocks) // 2 :])
        return blocks, [compute(n, cut) for n, cut in enumerate(cuts)]
    core, first, second = bits
    half = own.shape[0] // 2
    if held is None:
        held = [net.swap(own, bit) for bit in (first, second)]
    by_core = net.swap(own, core)
    outs = [compute(0, [own, by_core])]
    by_first, by_second = (after(x, outs[0][0]) for x in held)
    corner = [net.swap(by_first[:half], second), net.swap(by_second[half:], first)]
    blocks = [own, by_core, by_first, net.swap(by_first, core)]
    blocks += [by_second, net.swap(by_second, core)]
    outs.append(compute(1, blocks[2:6]))
    corner = jnp.concatenate([after(x, outs[1][0]) for x in corner], axis=0)
    blocks += [corner, net.swap(corner, core)]
    outs.append(compute(2, blocks[6:]))
    return blocks, outs


def shards(
    tokens,
    variate_ids,
    time_ids,
    w_qkv,
    w_out,
    w_in,
    w_down,
    norm_gains,
    qk_gains,
    head_bias,
    cotangent,
):
    sequences, tok_dev, width = tokens.shape
    layers = w_qkv.shape[0]
    heads = head_bias.shape[2]
    head_size = qk_gains.shape[2]
    net = Net()
    lo_n, lo_bits, seq_bits = net.lo_n, net.lo_bits, net.seq_bits
    rows = sequences * tok_dev
    local_heads = heads // lo_n
    local_width = local_heads * head_size
    head_start = net.lo * local_heads
    unit = w_down.shape[1]
    rows_out = w_out.shape[1]

    def to_groups(x):
        return jnp.concatenate([pick(x, net.hi), net.swap_hi(pick(x, 1 - net.hi))], axis=0)

    def keep_own(x, came):
        return in_order([x[:tok_dev], came], net.hi)

    qkv_blocks = split_columns(w_qkv.reshape(-1, 3 * width), lo_n, local_width)
    qkv_came = lax.all_to_all(qkv_blocks, "lo", 0, 0, tiled=True)
    token_parts = after(tokens, qkv_blocks)
    tokens_came = net.swap_hi(pick(token_parts, 1 - net.hi))
    state = jnp.concatenate([pick(token_parts, net.hi), tokens_came], axis=0).astype(F32)
    flat_in = after(w_in.reshape(-1, w_in.shape[2]), qkv_blocks)
    in_blocks = split_columns(flat_in, net.seq_n, unit)
    in_came = lax.all_to_all(in_blocks, ("hi", "lo"), 0, 0, tiled=True)
    own_qkv = own_columns(qkv_came, layers)
    ring = GatherBoth(net, join_pieces(own_qkv[0], w_out[0], 1))
    normed = rms_scale(state, norm_gains[0, 0]).astype(BF)
    normed_held = net.swap(normed, lo_bits[-1])
    ring.step()
    first_full = ring.finish()
    own_in = own_columns(in_came, layers)
    own_packs = [join_pieces(own_in[n], w_down[n], 0) for n in range(layers)]
    early = (*ring.by_dp, ring.own_came, tokens_came, normed_held)
    packs = [lax.all_gather(after(own_packs[0], *early), "dp", axis=0)]

    pair = to_groups(jnp.stack([variate_ids, time_ids], axis=-1))
    pair = jnp.concatenate(net.gather(pair, lo_bits), axis=0)
    tables = head_tables(pair[:, 0], pair[:, 1], head_size)

    def matrices(full):
        full = full.reshape((-1, own_qkv[0].shape[0]) + full.shape[2:])
        blocks = net.gather(full[:, :, 3 * local_width :], lo_bits)
        return full.reshape(-1, full.shape[2]), join_middle(blocks, net.lo, rows_out)

    saved, weights = [], []
    best_scores = jnp.full((layers, heads), FLOOR_VALUE, F32)
    for layer in range(layers):
        final = layer + 1 == layers
        weights.append(matrices(full_next if layer else first_full) + (packs[layer],))
        m_qkv, m_out, pack = weights[layer]
        ring = None
        layer_in = state
        blocks = net.gather(normed, lo_bits, None if layer else normed_held)
        mixed = project(blocks, m_qkv, 3 * local_width)
        if not final:
            own_next = join_pieces(own_qkv[layer + 1], w_out[layer + 1], 1)
            came_next = net.swap_hi(after(own_next, mixed))
        if final:
            seed_grad = to_groups(after(cotangent, blocks[-1]))
            seed_held = [net.swap(after(seed_grad, mixed), seq_bits[-1])]
        bias_pair = lax.dynamic_slice_in_dim(head_bias[layer], head_start, local_heads, 1)
        gains = jnp.concatenate([qk_gains[layer]] * 2, axis=1)
        bias = bias_marks(bias_pair, head_size)
        attended, kept, head_tops = attend(mixed, tables, gains, bias)
        head_tops = head_tops[:, 0, 0] + bias_pair[1]
        best_scores = lax.dynamic_update_slice(
            best_scores, head_tops[None, :], (jnp.int32(layer), head_start)
        )
        leaving = attended
        leaving = after(attended, *(seed_held if final else [came_next]))
        arrived = net.trade(jnp.split(leaving, lo_n, axis=0), lo_bits)
        if not final:
            own_next = in_order([own_next, came_next], net.hi).reshape(-1, own_next.shape[1])
            full_next = lax.all_gather(own_next, "dp", axis=0, tiled=True)
            full_next = full_next.reshape((net.dp_n * 2, -1) + full_next.shape[1:])
        middle, second = out_project(layer_in, arrived, m_out, norm_gains[layer, 1], net.lo)
        if not final:
            packs.append(lax.all_gather(after(own_packs[layer + 1], second), "dp", axis=0))

        def forward(n, blocks, pack=pack):
            joined, parts = feed_forward(blocks, pack)
            return [joined] + parts

        second, outs = wave(net, second, forward)
        joined = [out[0] for out in outs]
        partial = [part for out in outs for part in out[1:]]
        if final:
            final_sum = SumAll(net, partial)
        else:
            parts = SumAll(net, partial).parts()
            state, normed = finish_layer(middle, parts, norm_gains[layer + 1, 0])
        saved.append((layer_in, blocks, mixed, gains, bias, kept, arrived, middle, second, joined))

    if len(seq_bits) == 3:
        seed_held = [net.swap(after(seed_grad, outs[0][0]), seq_bits[1])] + seed_held
    gradient = seed_grad.astype(F32)
    qkv_parts = [None] * layers
    out_parts = [None] * layers
    in_parts = [None] * layers
    down_parts = [None] * layers
    norm_parts = [None] * layers
    qk_parts = [None] * layers
    bias_parts = [None] * layers
    hidden_sums = [None] * layers
    attention_sums = [None] * layers
    sums, low = None, seed_grad
    for layer in reversed(range(layers)):
        final = layer + 1 == layers
        m_qkv, m_out, pack = weights[layer]
        layer_in, normed, mixed, gains, bias, kept, arrived, middle, second, joined = saved[layer]

        def backward(n, blocks, joined=joined, pack=pack, final=final, sums=sums):
            if n == 2 and not final:
                blocks = [after(blocks[0], hidden_sums[layer + 1])] + blocks[1:]
            grad_part, gated_part, parts = feed_backward(blocks, joined[n], pack)
            return [grad_part, gated_part] + parts

        held = seed_held if final and len(seq_bits) == 3 else None
        down_in, outs = wave(net, low, backward, held)
        grad_joined, gated = [out[0] for out in outs], [out[1] for out in outs]
        second_sum = SumAll(net, [part for out in outs for part in out[2:]])
        second_sum.step()
        moved = second_sum.moving
        second_sum.step()
        second_sum.step()
        joined_first = after(grad_joined[0], *second_sum.low)
        grad_hidden = hidden_weights(net, second, [joined_first] + grad_joined[1:], gated, down_in)
        hidden_sums[layer] = lax.psum_scatter(
            grad_hidden, "dp", scatter_dimension=0, tiled=True
        )
        if final:
            final_sum.step(*moved)
        parts = second_sum.parts()
        parts[0] = after(parts[0], grad_hidden, *(final_sum.moving if final else []))
        gradient, gain_second, leaving, shares = out_backward(
            net, gradient, parts, middle, norm_gains[layer, 1], m_out, arrived, rows_out
        )
        if final:
            final_sum.step(leaving[0])
        grad_heads = jnp.concatenate(net.trade(leaving, lo_bits), axis=0)
        share_sum = SumLo(net, [x.reshape(-1, width) for x in shares])
        share_sum.step()
        grad_heads = after(grad_heads, *share_sum.moving)
        out_sum = share_sum.parts()
        grad_query, grad_keys, grad_values, grad_gains, grad_pair = attend_backward(
            mixed, grad_heads, tables, gains, bias, kept
        )
        grads = [grad_query, after(grad_keys, *final_sum.moving) if final else grad_keys, grad_values]
        if not final:
            other_sums = attention_sums[layer + 1]
            other_came = net.swap_hi(after(other_sums[1], leaving[0]))
            grads[2] = after(grad_values, other_came)
            total = other_sums[0].astype(F32) + other_came.astype(F32)
            qkv_parts[layer + 1], out_parts[layer + 1] = split_pieces(
                total, 3 * local_width, rows_out
            )
        last = layer == 0
        mine, other = mixed_weights(net, normed, grads, out_sum, rows_out, F32 if last else BF)
        if last:
            sums = (mine, net.swap_hi(other))
        else:
            sent = [x.reshape(-1, x.shape[2]) for x in (mine, other)]
            attention_sums[layer] = [
                lax.psum_scatter(x, "dp", scatter_dimension=0, tiled=True) for x in sent
            ]
        grads[0] = after(grads[0], other)
        normed_sum = SumLo(net, mixed_backward(grads, m_qkv, rows))
        normed_sum.step()
        parts = normed_sum.parts()
        gradient, low, gain_first = norm_backward(
            gradient, parts, layer_in, norm_gains[layer, 0]
        )
        norm_parts[layer] = jnp.stack([gain_first, gain_second])
        qk_parts[layer] = grad_gains.reshape(-1, 2, 2, head_size).sum(axis=(0, 2))
        bias_parts[layer] = lax.dynamic_update_slice(
            jnp.zeros((2, heads), F32), grad_pair[:, 0, :2].T, (jnp.int32(0), head_start)
        )
    both = SumBoth(net, *sums)
    both.step()
    final_sum.step(low)
    qkv_parts[0], out_parts[0] = split_pieces(both.total(), 3 * local_width, rows_out)
    for layer in range(layers):
        in_parts[layer], down_parts[layer] = split_hidden(
            hidden_sums[layer], width // net.dp_n, width
        )
    in_parts = return_rows(in_parts, ("hi", "lo"), net.seq_n)
    qkv_parts = return_rows(qkv_parts, "lo", lo_n, in_parts)
    parts = final_sum.parts()
    low_state = (saved[-1][7] + sum(x.astype(F32) for x in parts)).astype(BF)
    layer_out = keep_own(low_state, net.swap_hi(low_state[tok_dev:]))
    input_grad = keep_own(low, net.swap_hi(low[tok_dev:])).astype(F32)
    tops = best_scores.size
    small = jnp.concatenate(
        [best_scores.reshape(-1)]
        + [jnp.stack(part).reshape(-1) for part in (norm_parts, qk_parts, bias_parts)]
    )
    small = after(small, *both.moving)
    is_top = jnp.arange(small.size) < tops
    small = net.all_small(small, lambda a, b: jnp.where(is_top, jnp.maximum(a, b), a + b))
    best_scores = small[:tops].reshape(best_scores.shape)
    small = small[tops:]
    cut_norm, cut_qk = norm_gains.size, norm_gains.size + qk_gains.size
    norm_sum = small[:cut_norm].reshape(norm_gains.shape)
    qk_sum = small[cut_norm:cut_qk].reshape(qk_gains.shape)
    bias_sum = small[cut_qk:].reshape(head_bias.shape)

    factor = jnp.sqrt(CLIP_LIMIT / jnp.maximum(best_scores, CLIP_LIMIT))
    spread = jnp.repeat(factor, head_size, axis=1)
    column_scale = jnp.concatenate([spread, spread, jnp.ones((layers, width), F32)], axis=1)
    clipped = (w_qkv.astype(F32) * column_scale[:, None, :]).astype(BF)
    return (
        layer_out,
        input_grad,
        merge_columns(qkv_parts, layers, local_width),
        jnp.stack(out_parts),
        merge_columns(in_parts, layers, unit),
        jnp.stack(down_parts),
        norm_sum,
        qk_sum,
        bias_sum,
        clipped,
        best_scores,
    )


def solution(mesh):
    def program(*arrays):
        dp_n = mesh.shape["dp"]
        sequences = arrays[0].shape[0] // dp_n
        split = Mesh(mesh.devices.reshape(dp_n, sequences, -1), ("dp", "hi", "lo"))
        seq = ("hi", "lo")
        tokens_spec = P("dp", seq, None)
        rows_spec = P(None, ("dp",) + seq, None)
        ids_spec = P("dp", seq)
        in_specs = (tokens_spec, ids_spec, ids_spec) + (rows_spec,) * 4 + (P(),) * 3
        in_specs += (tokens_spec,)
        out_specs = (tokens_spec,) * 2 + (rows_spec,) * 4 + (P(),) * 3 + (rows_spec, P())
        run = jax.shard_map(
            shards, mesh=split, in_specs=in_specs, out_specs=out_specs, check_vma=False
        )
        return run(*arrays)

    return program
```

```python
import functools
import math

import jax
import jax.numpy as jnp
from jax import lax
from jax.experimental import pallas as pl
from jax.experimental.pallas import tpu as pltpu
from jax.sharding import Mesh
from jax.sharding import PartitionSpec as P

EPSILON = 1e-05
CLIP_LIMIT = 2.0
FLOOR_VALUE = -1e30
BF = jnp.bfloat16
F32 = jnp.float32


def rms_scale(values, gain):
    return values * lax.rsqrt(jnp.mean(values * values, axis=-1, keepdims=True) + EPSILON) * gain


def dot(a, b):
    return jnp.dot(a, b, preferred_element_type=F32)


def pick(array, index, axis=0):
    return lax.dynamic_index_in_dim(array, index, axis, keepdims=False)


class Net:
    def __init__(self):
        self.dp_n, self.hi_n, self.lo_n = (lax.axis_size(name) for name in ("dp", "hi", "lo"))
        self.dp, self.hi, self.lo = (lax.axis_index(name) for name in ("dp", "hi", "lo"))
        self.seq_n = self.hi_n * self.lo_n
        self.seq = self.hi * self.lo_n + self.lo
        self.seq_bits = [1 << b for b in range(self.seq_n.bit_length() - 1)]
        self.lo_bits = [b for b in self.seq_bits if b < self.lo_n]
        self.hi_bits = [b // self.lo_n for b in self.seq_bits if b >= self.lo_n]

    def swap(self, x, bit):
        if bit < self.lo_n:
            return lax.ppermute(x, "lo", [(i, i ^ bit) for i in range(self.lo_n)])
        bit //= self.lo_n
        return lax.ppermute(x, "hi", [(i, i ^ bit) for i in range(self.hi_n)])

    def swap_hi(self, x):
        return self.swap(x, self.lo_n)

    def swap_dp(self, x, bit):
        return lax.ppermute(x, "dp", [(i, i ^ bit) for i in range(self.dp_n)])

    def shift_dp(self, blocks):
        n = self.dp_n
        return [
            lax.ppermute(x, "dp", [(i, (i + k + 1) % n) for i in range(n)])
            for k, x in enumerate(blocks)
        ]

    def gather(self, block, bits, held=None):
        blocks = {0: block}
        if held is not None:
            blocks[bits[-1]] = held
        for bit in reversed(bits):
            for r in list(blocks):
                if r & bit:
                    continue
                if r | bit in blocks:
                    continue
                blocks[r | bit] = self.swap(blocks[r], bit)
        return [blocks[r] for r in range(len(blocks))]

    def add_swapped(self, mine, sent, bit):
        return mine.astype(F32) + self.swap(sent.astype(BF), bit).astype(F32)

    def scatter(self, blocks, bits):
        blocks = dict(enumerate(blocks))
        for bit in bits:
            blocks = self.halve(blocks, bit)
        return blocks[0]

    def halve(self, blocks, bit):
        return {
            r: self.add_swapped(blocks[r], blocks[r | bit], bit)
            for r in sorted(blocks, reverse=True)
            if not r & bit
        }

    def trade(self, blocks, bits):
        return Trade(self, blocks, bits).finish()

    def all_small(self, x, combine):
        for bit in self.seq_bits:
            x = combine(x, self.swap(x, bit))
        bit = 1
        while bit < self.dp_n:
            x = combine(x, self.swap_dp(x, bit))
            bit *= 2
        return x


class Trade:
    def __init__(self, net, blocks, bits):
        self.net, self.blocks, self.left, self.moving = net, list(blocks), list(bits), []

    def step(self, *earlier):
        bit = self.left.pop()
        moving = [r for r in range(len(self.blocks)) if r & bit]
        if bit == 1:
            self.moving = [self.net.swap(after(self.blocks[r], *earlier), bit) for r in moving]
            for r, x in zip(moving, self.moving):
                self.blocks[r] = x
            return
        rows = self.blocks[0].shape[0]
        sent = after(jnp.concatenate([self.blocks[r] for r in moving], axis=0), *earlier)
        self.moving = [self.net.swap(sent, bit)]
        for n, r in enumerate(moving):
            self.blocks[r] = self.moving[0][n * rows : (n + 1) * rows]

    def finish(self):
        while self.left:
            self.step()
        return self.blocks


class SumAll:
    def __init__(self, net, blocks):
        self.net, self.blocks, self.moving, self.step_n = net, blocks, [], 0
        self.low = []

    def step(self, *earlier):
        net, bits = self.net, self.net.seq_bits
        self.step_n += 1
        if len(bits) != 3:
            if self.step_n == 1:
                self.blocks = [net.scatter(self.blocks, bits)]
            self.moving = []
            return
        core, first, second = bits
        half = self.blocks[0].shape[0] // 2
        if self.step_n == 1:
            order = (first | second, first, second, 0)
            self.moving = [net.swap(after(self.blocks[r | core], *earlier), core) for r in order]
            self.pairs = {r: [self.blocks[r], x] for r, x in zip(order, self.moving)}
        elif self.step_n == 2:
            top, bottom = add_low([self.pairs[first | second]], cut=half)
            self.moving = [
                net.swap(after(top, *earlier), first),
                net.swap(after(bottom, *earlier), second),
            ]
        else:
            top, bottom = (after(x, *earlier) for x in self.moving)
            self.low = add_low(
                [self.pairs[first], self.pairs[second]], [(half, bottom), (0, top)]
            )
            self.moving = [net.swap(x, bit) for x, bit in zip(self.low, (first, second))]

    def parts(self):
        while self.step_n < 3:
            self.step()
        return self.pairs[0] + self.moving if self.moving else self.blocks


class SumLo:
    def __init__(self, net, blocks):
        self.net, self.blocks = net, blocks

    def step(self, *earlier):
        net = self.net
        if len(net.lo_bits) != 2:
            self.left = [net.scatter(self.blocks, net.lo_bits)]
            self.moving, self.low = [], []
            return
        self.moving = [net.swap(after(self.blocks[r | 1], *earlier), 1) for r in (2, 0)]
        self.left = [self.blocks[0], self.moving[1]]

    def parts(self, *earlier):
        if self.moving:
            self.low = add_low([[self.blocks[2], self.moving[0]]])
            far = self.low[0]
            self.moving = [self.net.swap(after(far, *earlier), 2)]
        return self.left + self.moving


class GatherBoth:
    def __init__(self, net, own, *earlier):
        self.net, self.own = net, own
        own = after(own, *earlier)
        self.own_came = net.swap_hi(own)
        self.by_dp = net.shift_dp([own] * (net.dp_n - 1))
        self.moving = [self.own_came] + self.by_dp

    def step(self, *earlier):
        self.rest_came = self.net.swap_hi(after(jnp.concatenate(self.by_dp, axis=0), *earlier))
        self.moving = [self.rest_came]

    def finish(self):
        net = self.net
        rows, columns = self.own.shape
        n = net.dp_n

        def kernel(at, own, own_came, rest_came, *refs):
            *by_dp, out = refs
            dp, hi = at[0] // 2, at[0] % 2
            out[at[0]] = own[...]
            out[dp * 2 + 1 - hi] = own_came[...]
            for k in range(1, n):
                source = lax.rem(dp + n - k, n)
                out[source * 2 + hi] = by_dp[k - 1][...]
                out[source * 2 + 1 - hi] = rest_came[(k - 1) * rows : k * rows, :]

        return on_chip(
            kernel,
            [((2 * n, rows, columns), BF)],
            self.own,
            self.own_came,
            self.rest_came,
            *self.by_dp,
            at=net.dp * 2 + net.hi,
            name="join_gathered",
        )[0]


class SumBoth:
    def __init__(self, net, mine, came):
        n = net.dp_n

        def kernel(at, x, y, own, *outs):
            own[...] = x[at[0]] + y[at[0]].astype(F32)
            for k, out in enumerate(outs):
                to = lax.rem(at[0] + k + 1, n)
                out[...] = (x[to] + y[to].astype(F32)).astype(BF)

        shape = mine.shape[1:]
        self.own, *self.blocks = on_chip(
            kernel, [(shape, F32)] + [(shape, BF)] * (n - 1), mine, came, at=net.dp, name="sum_hi"
        )
        self.net = net

    def step(self, *earlier):
        self.blocks[0] = after(self.blocks[0], *earlier)
        self.moving = self.net.shift_dp(self.blocks)

    def total(self):
        return self.own + sum(x.astype(F32) for x in self.moving)


def after(x, *earlier):
    return lax.optimization_barrier((x,) + earlier)[0]


def in_order(blocks, index):
    stacked = jnp.stack(blocks)
    return jnp.stack([pick(stacked, index ^ j) for j in range(len(blocks))])


def split_columns(shard, count, width):
    rows = shard.shape[0]
    parts = shard.shape[1] // count // width
    if width % LANES:
        shard = shard.reshape(rows, parts, count, width).transpose(2, 0, 1, 3)
        return shard.reshape(count, rows, parts * width)

    def kernel(shard_ref, out):
        for r in range(count):
            for p in range(parts):
                start = (p * count + r) * width
                out[r, :, p * width : (p + 1) * width] = shard_ref[:, start : start + width]

    return on_chip(kernel, [((count, rows, parts * width), BF)], shard, name="split_columns")[0]


def merge_columns(blocks, layers, width):
    count, rows = blocks.shape[0], blocks.shape[1] // layers
    parts = blocks.shape[2] // width
    columns = parts * count * width
    if width % LANES:
        shards = blocks.reshape(count, layers, rows, parts, width).transpose(1, 2, 3, 0, 4)
        return shards.reshape(layers, rows, columns).astype(F32)

    def kernel(ref, out):
        for r in range(count):
            for layer in range(layers):
                for p in range(parts):
                    start = (p * count + r) * width
                    part = ref[r, layer * rows : (layer + 1) * rows, p * width : (p + 1) * width]
                    out[layer, :, start : start + width] = part.astype(F32)

    return on_chip(kernel, [((layers, rows, columns), F32)], blocks, name="merge_columns")[0]


def own_columns(blocks, layers):
    count, rows, columns = blocks.shape
    blocks = blocks.reshape(count, layers, rows // layers, columns)
    return [blocks[:, n].reshape(-1, columns) for n in range(layers)]


def return_rows(layers, axes, count, *earlier):
    own = jnp.stack([x.astype(BF).reshape(count, -1, x.shape[1]) for x in layers], axis=1)
    own = own.reshape(count, -1, own.shape[-1])
    return lax.all_to_all(after(own, *earlier), axes, 0, 0, tiled=True)


def join_pieces(own, other, axis):
    if axis == 1:
        pieces = jnp.split(other, own.shape[0] // other.shape[0], axis=1)
        return jnp.concatenate([own, jnp.concatenate(pieces, axis=0)], axis=1)
    return jnp.concatenate([own] + jnp.split(other, other.shape[1] // own.shape[1], axis=1))


def split_hidden(own, rows_in, width):
    pieces = width // own.shape[1]
    down = jnp.concatenate(jnp.split(own[rows_in:], pieces, axis=0), axis=1)
    return own[:rows_in], down.astype(F32)


LANES = 128
NT = (((1,), (1,)), ((), ()))
TN = (((0,), (0,)), ((), ()))
VMEM = pl.BlockSpec(memory_space=pltpu.VMEM)
SMEM = pl.BlockSpec(memory_space=pltpu.SMEM)
LIMIT = 16 * 2**20
WEIGHT_LIMIT = 32 * 2**20


def on_chip(kernel, outs, *arrays, at=None, scratch=(), flops=0, name=None):
    outs = [jax.ShapeDtypeStruct(*out) for out in outs]
    moved = sum(math.prod(x.shape) * x.dtype.itemsize for x in list(arrays) + outs)
    first = [] if at is None else [at.astype(jnp.int32).reshape(1)]
    return pl.pallas_call(
        kernel,
        in_specs=[SMEM] * len(first) + [VMEM] * len(arrays),
        out_specs=[VMEM] * len(outs),
        out_shape=outs,
        scratch_shapes=list(scratch),
        compiler_params=pltpu.CompilerParams(vmem_limit_bytes=LIMIT),
        cost_estimate=pl.CostEstimate(flops=flops, bytes_accessed=moved, transcendentals=0),
        name=name,
    )(*first, *arrays)


def add_low(groups, extras=None, cut=None):
    shape = groups[0][0].shape
    extras = extras or [None] * len(groups)
    flat, counts = [], []
    for group, extra in zip(groups, extras):
        members = group + ([extra[1]] if extra else [])
        counts.append(len(members))
        flat += members

    def kernel(*refs):
        ins, outs = list(refs[: len(flat)]), list(refs[len(flat) :])
        for count, extra in zip(counts, extras):
            members = [ins.pop(0) for _ in range(count)]
            last = members.pop() if extra else None
            total = sum(x[...].astype(F32) for x in members)
            if extra:
                rows = last.shape[0]
                part = total[extra[0] : extra[0] + rows] + last[...].astype(F32)
                pieces = [total[: extra[0]], part, total[extra[0] + rows :]]
                total = jnp.concatenate([p for p in pieces if p.shape[0]], axis=0)
            total = total.astype(BF)
            if cut is None:
                outs.pop(0)[...] = total
            else:
                outs.pop(0)[...] = total[:cut]
                outs.pop(0)[...] = total[cut:]

    if cut is None:
        shapes = [(shape, BF)] * len(groups)
    else:
        shapes = [((cut,) + shape[1:], BF), ((shape[0] - cut,) + shape[1:], BF)]
    return on_chip(kernel, shapes, *flat, name="add_low")


def finish_layer(middle, parts, gain):
    rows, width = middle.shape

    def kernel(x, g, *refs):
        *ins, state, normed = refs
        total = x[...] + sum(part[...].astype(F32) for part in ins)
        state[...] = total
        normed[...] = rms_scale(total, g[...]).astype(BF)

    outs = [((rows, width), F32), ((rows, width), BF)]
    return on_chip(kernel, outs, middle, gain.reshape(1, width), *parts, name="finish_layer")


def norm_backward(gradient, parts, values, gain):
    rows, width = gradient.shape

    def kernel(g, x, gn, *refs):
        *ins, new, low, gain_out = refs
        total = sum(part[...].astype(F32) for part in ins)
        grad, gain_part = norm_adjoint(x[...], gn[...], total)
        grad = g[...] + grad
        new[...] = grad
        low[...] = grad.astype(BF)
        gain_out[...] = gain_part

    outs = [((rows, width), F32), ((rows, width), BF), ((1, width), F32)]
    arrays = [gradient, values, gain.reshape(1, width)]
    new, low, gain_part = on_chip(kernel, outs, *arrays, *parts, name="norm_backward")
    return new, low, gain_part[0]


def norm_adjoint(values, gain, grad):
    inverse = lax.rsqrt(jnp.mean(values * values, axis=-1, keepdims=True) + EPSILON)
    normal = values * inverse
    gain_part = jnp.sum(grad * normal, axis=0, keepdims=True)
    grad = grad * gain
    grad = (grad - normal * jnp.mean(grad * normal, axis=-1, keepdims=True)) * inverse
    return grad, gain_part


def project(blocks, matrix, columns):
    rows = blocks[0].shape[0]

    def kernel(*refs):
        *ins, m, out = refs
        for n, x in enumerate(ins):
            out[n * rows : (n + 1) * rows, :] = dot(x[...], m[:, :columns]).astype(BF)

    return on_chip(
        kernel,
        [((rows * len(blocks), columns), BF)],
        *blocks,
        matrix,
        flops=2 * rows * len(blocks) * matrix.size,
        name="project",
    )[0]


def out_project(state, arrived, matrix, gain, at):
    rows, width = state.shape
    heads = arrived[0].shape[1]

    def kernel(index, x, m, g, *refs):
        *ins, middle, second = refs
        total = x[...]
        for r, block in enumerate(ins):
            start = pl.multiple_of((index[0] ^ r) * heads, heads)
            total = total + dot(block[...], m[pl.ds(start, heads), :])
        middle[...] = total
        second[...] = rms_scale(total, g[...]).astype(BF)

    return on_chip(
        kernel,
        [((rows, width), F32), ((rows, width), BF)],
        state,
        matrix,
        gain.reshape(1, width),
        *arrived,
        at=at,
        flops=2 * rows * matrix.size,
        name="out_project",
    )


def hidden_matrices(pack, width):
    rows = width // pack.shape[0]
    columns = pack.shape[2]
    down = (pack.shape[1] - rows) * columns // width
    m_in = jnp.concatenate([pack[n, :rows, :] for n in range(pack.shape[0])], axis=0)
    m_down = []
    for n in range(pack.shape[0]):
        starts = range(rows, pack.shape[1], down)
        m_down.append(jnp.concatenate([pack[n, p : p + down, :] for p in starts], axis=1))
    return m_in, jnp.concatenate(m_down, axis=0)


def feed_forward(blocks, pack):
    rows, width = blocks[0].shape
    count, hidden = len(blocks), pack.shape[2] // 2

    def kernel(*refs):
        m, ins, joined, outs = refs[0], refs[1 : count + 1], refs[count + 1], refs[count + 2 :]
        m_in, m_down = hidden_matrices(m, width)
        for n, (x, out) in enumerate(zip(ins, outs)):
            both = dot(x[...], m_in)
            joined[n * rows : (n + 1) * rows, :] = both.astype(BF)
            gate, up = both[:, :hidden], both[:, hidden:]
            gated = gate / (1.0 + jnp.exp(-gate)) * up
            out[...] = dot(gated.astype(BF), m_down).astype(BF)

    joined, *parts = on_chip(
        kernel,
        [((rows * count, 2 * hidden), BF)] + [((rows, width), BF)] * count,
        pack,
        *blocks,
        flops=2 * rows * count * pack.size,
        name="feed_forward",
    )
    return joined, parts


def feed_backward(blocks, joined, pack):
    rows, width = blocks[0].shape
    count, hidden = len(blocks), pack.shape[2] // 2

    def kernel(*refs):
        m, ins, (j, grad_joined, gated) = refs[0], refs[1 : count + 1], refs[count + 1 : count + 4]
        m_in, m_down = hidden_matrices(m, width)
        for n, (x, out) in enumerate(zip(ins, refs[count + 4 :])):
            part = slice(n * rows, (n + 1) * rows)
            gate = j[part, :hidden].astype(F32)
            up = j[part, hidden:].astype(F32)
            grad = lax.dot_general(x[...], m_down, NT, preferred_element_type=F32)
            sigmoid = 1.0 / (1.0 + jnp.exp(-gate))
            silu = gate * sigmoid
            gated[part, :] = (silu * up).astype(BF)
            grad_gate = grad * up * (sigmoid + silu * (1.0 - sigmoid))
            grad_joined[part, :hidden] = grad_gate.astype(BF)
            grad_joined[part, hidden:] = (grad * silu).astype(BF)
            total = lax.dot_general(grad_joined[part, :], m_in, NT, preferred_element_type=F32)
            out[...] = total.astype(BF)

    grad_joined, gated, *parts = on_chip(
        kernel,
        [((rows * count, 2 * hidden), BF), ((rows * count, hidden), BF)]
        + [((rows, width), BF)] * count,
        pack,
        *blocks,
        joined,
        flops=2 * rows * count * pack.size,
        name="feed_backward",
    )
    return grad_joined, gated, parts


def side_by_side(refs, scratch, sems, start=0):
    copies, column = [], 0
    for group in refs:
        row = 0
        for x in group:
            place = scratch.at[pl.ds(row, x.shape[0]), pl.ds(column, x.shape[1])]
            copies.append(pltpu.make_async_copy(x, place, sems.at[start + len(copies)]))
            row += x.shape[0]
        column += group[0].shape[1]
    return copies


def weight_call(kernel, outs, groups, shapes, at, flops, name):
    flat = [x for group in groups for column in group for x in column]
    outs = [jax.ShapeDtypeStruct(*out) for out in outs]
    moved = sum(math.prod(x.shape) * x.dtype.itemsize for x in flat + outs)

    def body(index, *refs):
        ins, refs = list(refs[: len(flat)]), refs[len(flat) :]
        results, scratch, sems = refs[: len(outs)], refs[len(outs) : -1], refs[-1]
        arrived, count = [], 0
        for group, target in zip(groups, scratch):
            taken = [[ins.pop(0) for x in column] for column in group]
            copies = side_by_side(taken, target, sems, count)
            count += len(copies)
            for copy in copies:
                copy.start()
            arrived.append(Arriving(copies, target))
        kernel(index, *arrived, *results)

    return pl.pallas_call(
        body,
        in_specs=[SMEM] + [pl.BlockSpec(memory_space=pl.ANY)] * len(flat),
        out_specs=[VMEM] * len(outs),
        out_shape=outs,
        scratch_shapes=[pltpu.VMEM(shape, BF) for shape in shapes]
        + [pltpu.SemaphoreType.DMA((len(flat),))],
        compiler_params=pltpu.CompilerParams(vmem_limit_bytes=WEIGHT_LIMIT),
        cost_estimate=pl.CostEstimate(flops=flops, bytes_accessed=moved, transcendentals=0),
        name=name,
    )(at.astype(jnp.int32).reshape(1), *flat)


class Arriving:
    def __init__(self, copies, ref):
        self.copies, self.ref = copies, ref

    def __getitem__(self, index):
        for copy in self.copies:
            copy.wait()
        self.copies = []
        return self.ref[index]


def hidden_weights(net, second, grad_joined, gated, grads):
    length = sum(x.shape[0] for x in second)
    width, columns, hidden = second[0].shape[1], grad_joined[0].shape[1], gated[0].shape[1]
    rows, down = width // net.dp_n, hidden // net.dp_n
    pieces = width // columns

    def kernel(index, a, b, c, d, out):
        for n in range(net.dp_n):
            left = a[:, n * rows : (n + 1) * rows]
            first = n * (rows + pieces * down)
            out[first : first + rows, :] = lax.dot_general(
                left, b[...], TN, preferred_element_type=F32
            ).astype(BF)
            left = c[:, n * down : (n + 1) * down]
            total = lax.dot_general(left, d[...], TN, preferred_element_type=F32).astype(BF)
            for p in range(pieces):
                start = first + rows + p * down
                out[start : start + down, :] = total[:, p * columns : (p + 1) * columns]

    return weight_call(
        kernel,
        [((net.dp_n * (rows + pieces * down), columns), BF)],
        [[second], [grad_joined], [gated], [grads]],
        [(length, width), (length, columns), (length, hidden), (length, width)],
        net.dp,
        2 * length * width * (columns + hidden),
        "hidden_weights",
    )[0]


def mixed_weights(net, normed, grads, shares, rows, kept):
    length, width = sum(x.shape[0] for x in normed), normed[0].shape[1]
    columns = sum(g.shape[1] for g in grads)
    chunk = width // net.dp_n // net.hi_n
    pieces = chunk // rows
    c = shares[0].shape[1] // pieces

    def kernel(index, a, b, *refs):
        *parts, mine, other = refs
        for n in range(net.dp_n * net.hi_n):
            left = a[:, n * chunk : (n + 1) * chunk]
            total = lax.dot_general(left, b[...], TN, preferred_element_type=F32)
            out = sum(part[n * rows : (n + 1) * rows, :].astype(F32) for part in parts)
            here = index[0] == n % net.hi_n

            def store(target, kind, n=n, total=total, out=out):
                target[n // net.hi_n, :, :columns] = total.astype(kind)
                for p in range(pieces):
                    cut = out[:, p * c : (p + 1) * c].astype(kind)
                    target[n // net.hi_n, p * rows : (p + 1) * rows, columns:] = cut

            pl.when(here)(lambda: store(mine, kept))
            pl.when(jnp.logical_not(here))(lambda: store(other, BF))

    shape = (net.dp_n, chunk, columns + c)
    flat = [x.astype(BF) for x in shares]
    return weight_call(
        kernel,
        [(shape, kept), (shape, BF)],
        [[normed], [[g] for g in grads]] + [[[x]] for x in flat],
        [(length, width), (length, columns)] + [x.shape for x in flat],
        net.hi,
        2 * length * width * columns,
        "mixed_weights",
    )


def split_pieces(own, columns, rows):
    pieces = own.shape[0] // rows
    return own[:, :columns], jnp.concatenate(jnp.split(own[:, columns:], pieces, axis=0), axis=1)


def out_backward(net, gradient, parts, middle, gain, matrix, arrived, rows_out):
    rows, width = gradient.shape
    count, heads = len(arrived), arrived[0].shape[1]
    groups = width // rows_out // count

    def kernel(index, g, mid, gn, *refs):
        sums, m, refs = refs[: len(parts)], refs[len(parts)], refs[len(parts) + 1 :]
        ins, (new, gain_out), refs = refs[:count], refs[count : count + 2], refs[count + 2 :]
        leaving, shares, scratch = refs[:count], refs[count : 2 * count], refs[2 * count]
        total = sum(part[...].astype(F32) for part in sums)
        grad, gain_out[...] = norm_adjoint(mid[...], gn[...], total)
        grad = g[...] + grad
        new[...] = grad
        branch = grad.astype(BF)
        for r in range(count):
            start = pl.multiple_of((index[0] ^ r) * heads, heads)
            leaving[r][...] = lax.dot_general(
                branch, m[pl.ds(start, heads), :], NT, preferred_element_type=F32
            ).astype(BF)
            block = lax.dot_general(ins[r][...], branch, TN, preferred_element_type=F32)
            scratch[pl.ds(pl.multiple_of(start // rows_out, heads // rows_out), heads // rows_out)] = (
                block.reshape(heads // rows_out, rows_out, width)
            )
        for r in range(count):
            for n in range(groups):
                shares[r][n] = scratch[n * count + (index[0] ^ r)].astype(BF)

    outs = on_chip(
        kernel,
        [((rows, width), F32), ((1, width), F32)]
        + [((rows, heads), BF)] * count
        + [((groups, rows_out, width), BF)] * count,
        gradient,
        middle,
        gain.reshape(1, width),
        *parts,
        matrix,
        *arrived,
        at=net.lo,
        scratch=[pltpu.VMEM((width // rows_out, rows_out, width), F32)],
        flops=4 * rows * matrix.size,
        name="out_backward",
    )
    return outs[0], outs[1][0], outs[2 : 2 + count], outs[2 + count :]


def mixed_backward(grads, matrix, rows):
    length = grads[0].shape[0]
    count = length // rows
    width = grads[0].shape[1]

    def kernel(q, k, v, m, *outs):
        for n, out in enumerate(outs):
            part = slice(n * rows, (n + 1) * rows)
            x = jnp.concatenate([q[part, :], k[part, :], v[part, :]], axis=1)
            out[...] = lax.dot_general(
                x, m[:, : 3 * width], NT, preferred_element_type=F32
            ).astype(BF)

    return on_chip(
        kernel,
        [((rows, matrix.shape[0]), BF)] * count,
        *grads,
        matrix,
        flops=2 * length * matrix.size,
        name="mixed_backward",
    )


def join_middle(blocks, index, rows):
    n, stacked, c = blocks[0].shape
    count, pieces = len(blocks), stacked // rows
    if rows % 16:
        full = in_order(blocks, index).reshape(count, n, pieces, rows, c)
        return full.transpose(1, 0, 3, 2, 4).reshape(-1, pieces * c)

    def kernel(at, *refs):
        for r, block in enumerate(refs[:-1]):
            for i in range(n):
                start = pl.multiple_of((i * count + (at[0] ^ r)) * rows, rows)
                for p in range(pieces):
                    refs[-1][pl.ds(start, rows), p * c : (p + 1) * c] = block[
                        i, p * rows : (p + 1) * rows, :
                    ]

    shape = (n * count * rows, pieces * c)
    return on_chip(kernel, [(shape, BF)], *blocks, at=index, name="join_middle")[0]


def lane_ids():
    return lax.broadcasted_iota(jnp.int32, (1, LANES), 1)


def three_parts(x):
    hi = x.astype(BF).astype(F32)
    mid = (x - hi).astype(BF).astype(F32)
    return hi, mid, x - hi - mid


def group_sum(x, width):
    rows = lax.broadcasted_iota(jnp.int32, (LANES, LANES), 0) // width
    columns = lax.broadcasted_iota(jnp.int32, (LANES, LANES), 1) // width
    ones = jnp.where(rows == columns, 1.0, 0.0).astype(BF)
    return sum(dot(part.astype(BF), ones) for part in three_parts(x))


def swap_halves(x, half):
    front = (lane_ids() // half) % 2 == 0
    return jnp.where(front, pltpu.roll(x, LANES - half, 1), pltpu.roll(x, half, 1))


def head_prep(raw, gain, cosine, sine, width):
    raw = raw.astype(F32)
    inverse = lax.rsqrt(group_sum(raw * raw, width) * (1.0 / width) + EPSILON)
    scaled = raw * inverse * gain
    return scaled * cosine + swap_halves(scaled, width // 2) * sine, inverse


def attend_kernel(
    rows, query_in, key_in, value_in, cosine, sine, marks, gains, bias, attended, kept, tops
):
    length = query_in.shape[0]
    width = LANES // 2
    low = lane_ids() < width
    query, unused = head_prep(query_in[...], gains[0:1, :], cosine[...], sine[...], width)
    keys, unused = head_prep(key_in[...], gains[1:2, :], cosine[...], sine[...], width)
    query = query * (1.0 / math.sqrt(width))
    mark = marks[...].astype(F32)
    value = value_in[...].astype(F32)
    heads = []
    for h in range(2):
        shift = (lambda x: pltpu.roll(x, width, 1)) if h else (lambda x: x)
        heads.append(
            (
                jnp.where(low, shift(query), mark * bias[0, h : h + 1, :]).astype(BF),
                jnp.where(low, shift(keys), mark).astype(BF),
                jnp.where(low, shift(value), 1.0).astype(BF),
            )
        )
    best = [None, None]
    for start in range(0, length, rows):
        part = slice(start, start + rows)
        outs = []
        for h, (head_query, head_keys, head_value) in enumerate(heads):
            scores = lax.dot_general(head_query[part], head_keys, NT, preferred_element_type=F32)
            top = jnp.max(scores, axis=0, keepdims=True)
            best[h] = top if best[h] is None else jnp.maximum(best[h], top)
            mixed = dot(jnp.exp(scores).astype(BF), head_value)
            out = jnp.where(low, mixed / pltpu.roll(mixed, width, 1), jnp.log(mixed))
            kept[h, part, :] = out
            outs.append(out)
        attended[part, :] = jnp.where(low, outs[0], pltpu.roll(outs[1], width, 1)).astype(BF)
    for h in range(2):
        tops[h, :, :] = jnp.broadcast_to(jnp.max(best[h], axis=1, keepdims=True), (8, LANES))


def attend_backward_kernel(
    columns,
    query_in,
    key_in,
    value_in,
    grad_in,
    cosine,
    sine,
    marks,
    gains,
    bias,
    kept,
    grad_query,
    grad_key,
    grad_value,
    grad_gains,
    grad_bias,
    keys_turned,
    sum_keys,
    sum_values,
):
    length = query_in.shape[0]
    width = LANES // 2
    lane = lane_ids()
    low = lane < width
    scale = 1.0 / math.sqrt(width)
    query, query_inverse = head_prep(query_in[...], gains[0:1, :], cosine[...], sine[...], width)
    keys, key_inverse = head_prep(key_in[...], gains[1:2, :], cosine[...], sine[...], width)
    query = query * scale
    mark = marks[...].astype(F32)
    value = value_in[...].astype(F32)
    grads = grad_in[...].astype(F32)

    def place(x, first, other):
        for offset, part in enumerate(three_parts(x)):
            other = jnp.where(lane == first + offset, part, other)
        return other

    all_query, all_keys, all_values = [], [], []
    for h in range(2):
        shift = (lambda x: pltpu.roll(x, width, 1)) if h else (lambda x: x)
        out = kept[h]
        query_marks = place(-out, width + 12, mark * bias[0, h : h + 1, :])
        head_query = jnp.where(low, shift(query), query_marks).astype(BF)
        head_keys = jnp.where(low, shift(keys), mark).astype(BF)
        ones = jnp.where(lane < width + 3, 1.0, 0.0)
        head_value = jnp.where(low, shift(value), ones).astype(BF)
        head_grad = jnp.where(low, shift(grads), 0.0)
        inner = pltpu.roll(-group_sum(head_grad * out, width), width, 1)
        head_grad = place(inner, width, head_grad).astype(BF)
        keys_turned[...] = head_keys.astype(F32).T.astype(BF)
        turned = []
        for start in range(0, length, columns):
            part = slice(start, start + columns)
            scores = lax.dot_general(head_keys, head_query[part], NT, preferred_element_type=F32)
            probability = jnp.exp(scores)
            grad_prob = lax.dot_general(
                head_value, head_grad[part], NT, preferred_element_type=F32
            )
            grad_scores = (probability * grad_prob).astype(BF)
            part_values = dot(probability.astype(BF), head_grad[part])
            part_keys = dot(grad_scores, head_query[part])
            if start:
                sum_values[...] += part_values
                sum_keys[...] += part_keys
            else:
                sum_values[...] = part_values
                sum_keys[...] = part_keys
            turned.append(dot(keys_turned[...], grad_scores).T)
        head_sum = jnp.concatenate(turned, axis=0)
        equal = jnp.where((lane >= width) & (lane < width + 4), mark, 0.0)
        match = jnp.sum(jnp.sum(head_sum * equal, axis=0, keepdims=True), axis=1, keepdims=True)
        total = jnp.sum(
            jnp.where(lane == width + 12, jnp.sum(head_sum, axis=0, keepdims=True), 0.0),
            axis=1,
            keepdims=True,
        )
        both = jnp.where(lane == 0, match, total - match)
        grad_bias[h, :, :] = jnp.broadcast_to(both, (8, LANES))
        all_query.append(head_sum * scale)
        all_keys.append(sum_keys[...])
        all_values.append(sum_values[...])

    def join(pair):
        return jnp.where(low, pair[0], pltpu.roll(pair[1], width, 1))

    grad_value[...] = join(all_values).astype(BF)
    for n, (pair, raw, inverse, out) in enumerate(
        (
            (all_query, query_in, query_inverse, grad_query),
            (all_keys, key_in, key_inverse, grad_key),
        )
    ):
        grad = join(pair)
        grad = grad * cosine[...] - swap_halves(grad, width // 2) * sine[...]
        normal = raw[...].astype(F32) * inverse
        grad_gains[0, n : n + 1, :] = jnp.sum(grad * normal, axis=0, keepdims=True)
        grad = grad * gains[n : n + 1, :]
        mean = group_sum(grad * normal, width) * (1.0 / width)
        out[...] = ((grad - normal * mean) * inverse).astype(BF)


def lane_block(length, offset):
    return pl.BlockSpec((length, LANES), lambda i: (0, offset + i))


def whole_block(shape):
    return pl.BlockSpec(shape, lambda i: (0,) * len(shape))


def attend(mixed, tables, gains, bias):
    length, heads = mixed.shape[0], bias.shape[0]
    pairs = heads // 2
    block = lane_block
    return pl.pallas_call(
        functools.partial(attend_kernel, min(256, length)),
        grid=(pairs,),
        in_specs=[
            block(length, 0),
            block(length, pairs),
            block(length, 2 * pairs),
            whole_block((length, LANES)),
            whole_block((length, LANES)),
            whole_block((length, LANES)),
            whole_block((2, LANES)),
            pl.BlockSpec((1, 2, LANES), lambda i: (i, 0, 0)),
        ],
        out_specs=[
            block(length, 0),
            pl.BlockSpec((2, length, LANES), lambda i: (i, 0, 0)),
            pl.BlockSpec((2, 8, LANES), lambda i: (i, 0, 0)),
        ],
        out_shape=[
            jax.ShapeDtypeStruct((length, pairs * LANES), BF),
            jax.ShapeDtypeStruct((heads, length, LANES), F32),
            jax.ShapeDtypeStruct((heads, 8, LANES), F32),
        ],
        compiler_params=pltpu.CompilerParams(vmem_limit_bytes=16 * 2**10 * max(1024, length)),
        cost_estimate=pl.CostEstimate(
            flops=8 * heads * length * length * LANES,
            bytes_accessed=16 * length * pairs * LANES,
            transcendentals=heads * length * length,
        ),
        name="attend",
    )(mixed, mixed, mixed, *tables, gains, bias.reshape(pairs, 2, LANES))


def attend_backward(mixed, grad, tables, gains, bias, kept):
    length, heads = mixed.shape[0], bias.shape[0]
    pairs = heads // 2
    block = lane_block
    flat = jax.ShapeDtypeStruct((length, pairs * LANES), BF)
    return pl.pallas_call(
        functools.partial(attend_backward_kernel, min(256, length)),
        grid=(pairs,),
        in_specs=[
            block(length, 0),
            block(length, pairs),
            block(length, 2 * pairs),
            block(length, 0),
            whole_block((length, LANES)),
            whole_block((length, LANES)),
            whole_block((length, LANES)),
            whole_block((2, LANES)),
            pl.BlockSpec((1, 2, LANES), lambda i: (i, 0, 0)),
            pl.BlockSpec((2, length, LANES), lambda i: (i, 0, 0)),
        ],
        out_specs=[
            block(length, 0),
            block(length, 0),
            block(length, 0),
            pl.BlockSpec((1, 2, LANES), lambda i: (i, 0, 0)),
            pl.BlockSpec((2, 8, LANES), lambda i: (i, 0, 0)),
        ],
        out_shape=[
            flat,
            flat,
            flat,
            jax.ShapeDtypeStruct((pairs, 2, LANES), F32),
            jax.ShapeDtypeStruct((heads, 8, LANES), F32),
        ],
        scratch_shapes=[
            pltpu.VMEM((LANES, length), BF),
            pltpu.VMEM((length, LANES), F32),
            pltpu.VMEM((length, LANES), F32),
        ],
        compiler_params=pltpu.CompilerParams(vmem_limit_bytes=16 * 2**10 * max(1024, length)),
        cost_estimate=pl.CostEstimate(
            flops=20 * heads * length * length * LANES,
            bytes_accessed=24 * length * pairs * LANES,
            transcendentals=heads * length * length,
        ),
        name="attend_backward",
    )(mixed, mixed, mixed, grad, *tables, gains, bias.reshape(pairs, 2, LANES), kept)


def head_tables(ids, places, width):
    frequency = jnp.exp(jnp.arange(width // 2, dtype=F32) * (-2.0 * math.log(10000.0) / width))
    angles = places.astype(F32)[:, None] * frequency
    cosine, sine = jnp.cos(angles), jnp.sin(angles)
    lane = jnp.arange(LANES)[None, :]
    equal = (ids[:, None] == (lane - width) % 4) & (lane >= width) & (lane < width + 12)
    plain = (lane >= width + 12) & (lane < width + 15)
    return (
        jnp.concatenate([cosine] * 4, axis=1),
        jnp.concatenate([-sine, sine, -sine, sine], axis=1),
        (equal | plain).astype(BF),
    )


def bias_marks(pair, width):
    gap = pair[0] - pair[1]
    hi = lax.reduce_precision(gap, 8, 7)
    mid = lax.reduce_precision(gap - hi, 8, 7)
    lane = jnp.arange(LANES)[None, :]
    marks = jnp.zeros((pair.shape[1], LANES), F32)
    for n, part in enumerate((hi, mid, gap - hi - mid)):
        inside = (lane >= width + 4 * n) & (lane < width + 4 * n + 4)
        marks = jnp.where(inside, part[:, None], marks)
    return marks


def wave(net, own, compute, held=None):
    bits = net.seq_bits
    if len(bits) != 3:
        blocks = net.gather(own, bits)
        cuts = (blocks[: len(blocks) // 2], blocks[len(blocks) // 2 :])
        return blocks, [compute(n, cut) for n, cut in enumerate(cuts)]
    core, first, second = bits
    half = own.shape[0] // 2
    if held is None:
        held = [net.swap(own, bit) for bit in (first, second)]
    by_core = net.swap(own, core)
    outs = [compute(0, [own, by_core])]
    by_first, by_second = (after(x, outs[0][0]) for x in held)
    corner = [net.swap(by_first[:half], second), net.swap(by_second[half:], first)]
    blocks = [own, by_core, by_first, net.swap(by_first, core)]
    blocks += [by_second, net.swap(by_second, core)]
    outs.append(compute(1, blocks[2:6]))
    corner = jnp.concatenate([after(x, outs[1][0]) for x in corner], axis=0)
    blocks += [corner, net.swap(corner, core)]
    outs.append(compute(2, blocks[6:]))
    return blocks, outs


def shards(
    tokens,
    variate_ids,
    time_ids,
    w_qkv,
    w_out,
    w_in,
    w_down,
    norm_gains,
    qk_gains,
    head_bias,
    cotangent,
):
    sequences, tok_dev, width = tokens.shape
    layers = w_qkv.shape[0]
    heads = head_bias.shape[2]
    head_size = qk_gains.shape[2]
    net = Net()
    lo_n, lo_bits, seq_bits = net.lo_n, net.lo_bits, net.seq_bits
    rows = sequences * tok_dev
    local_heads = heads // lo_n
    local_width = local_heads * head_size
    head_start = net.lo * local_heads
    unit = w_down.shape[1]
    rows_out = w_out.shape[1]

    def to_groups(x):
        return jnp.concatenate([pick(x, net.hi), net.swap_hi(pick(x, 1 - net.hi))], axis=0)

    def keep_own(x, came):
        return in_order([x[:tok_dev], came], net.hi)

    qkv_blocks = split_columns(w_qkv.reshape(-1, 3 * width), lo_n, local_width)
    qkv_came = lax.all_to_all(qkv_blocks, "lo", 0, 0, tiled=True)
    token_parts = after(tokens, qkv_blocks)
    tokens_came = net.swap_hi(pick(token_parts, 1 - net.hi))
    state = jnp.concatenate([pick(token_parts, net.hi), tokens_came], axis=0).astype(F32)
    flat_in = after(w_in.reshape(-1, w_in.shape[2]), qkv_blocks)
    in_blocks = split_columns(flat_in, net.seq_n, unit)
    in_came = lax.all_to_all(in_blocks, ("hi", "lo"), 0, 0, tiled=True)
    own_qkv = own_columns(qkv_came, layers)
    ring = GatherBoth(net, join_pieces(own_qkv[0], w_out[0], 1))
    normed = rms_scale(state, norm_gains[0, 0]).astype(BF)
    normed_held = net.swap(normed, lo_bits[-1])
    ring.step()
    first_full = ring.finish()
    own_in = own_columns(in_came, layers)
    own_packs = [join_pieces(own_in[n], w_down[n], 0) for n in range(layers)]
    pair = to_groups(jnp.stack([variate_ids, time_ids], axis=-1))
    pairs = net.gather(pair, lo_bits)
    early = (*ring.by_dp, ring.own_came, tokens_came, normed_held, pairs[-1])
    packs = [lax.all_gather(after(own_packs[0], *early), "dp", axis=0)]

    pair = jnp.concatenate(pairs, axis=0)
    tables = head_tables(pair[:, 0], pair[:, 1], head_size)

    def matrices(full):
        full = full.reshape((-1, own_qkv[0].shape[0]) + full.shape[2:])
        blocks = net.gather(full[:, :, 3 * local_width :], lo_bits)
        return full.reshape(-1, full.shape[2]), join_middle(blocks, net.lo, rows_out)

    saved, weights = [], []
    best_scores = jnp.full((layers, heads), FLOOR_VALUE, F32)
    for layer in range(layers):
        final = layer + 1 == layers
        weights.append(matrices(full_next if layer else first_full) + (packs[layer],))
        m_qkv, m_out, pack = weights[layer]
        ring = None
        layer_in = state
        blocks = net.gather(normed, lo_bits, None if layer else normed_held)
        taken = blocks
        if final:
            seed_grad = jnp.concatenate([pick(cotangent, net.hi), seed_came], axis=0)
            seed_held = [net.swap(after(seed_grad, blocks[0]), seq_bits[-1])]
            taken = [after(blocks[0], *seed_held)] + blocks[1:]
        mixed = project(taken, m_qkv, 3 * local_width)
        if not final:
            own_next = join_pieces(own_qkv[layer + 1], w_out[layer + 1], 1)
            came_next = net.swap_hi(after(own_next, mixed))
        if layer == 0:
            seed_came = net.swap_hi(pick(after(cotangent, came_next), 1 - net.hi))
        bias_pair = lax.dynamic_slice_in_dim(head_bias[layer], head_start, local_heads, 1)
        gains = jnp.concatenate([qk_gains[layer]] * 2, axis=1)
        bias = bias_marks(bias_pair, head_size)
        attended, kept, head_tops = attend(mixed, tables, gains, bias)
        head_tops = head_tops[:, 0, 0] + bias_pair[1]
        best_scores = lax.dynamic_update_slice(
            best_scores, head_tops[None, :], (jnp.int32(layer), head_start)
        )
        leaving = attended if final else after(attended, came_next)
        arrived = net.trade(jnp.split(leaving, lo_n, axis=0), lo_bits)
        if layer == 0:
            arrived[0] = after(arrived[0], seed_came)
        if not final:
            own_next = in_order([own_next, came_next], net.hi).reshape(-1, own_next.shape[1])
            full_next = lax.all_gather(own_next, "dp", axis=0, tiled=True)
            full_next = full_next.reshape((net.dp_n * 2, -1) + full_next.shape[1:])
        middle, second = out_project(layer_in, arrived, m_out, norm_gains[layer, 1], net.lo)
        if not final:
            packs.append(lax.all_gather(after(own_packs[layer + 1], second), "dp", axis=0))

        def forward(n, blocks, pack=pack):
            joined, parts = feed_forward(blocks, pack)
            return [joined] + parts

        second, outs = wave(net, second, forward)
        joined = [out[0] for out in outs]
        partial = [part for out in outs for part in out[1:]]
        if final:
            final_sum = SumAll(net, partial)
        else:
            parts = SumAll(net, partial).parts()
            state, normed = finish_layer(middle, parts, norm_gains[layer + 1, 0])
        saved.append((layer_in, blocks, mixed, gains, bias, kept, arrived, middle, second, joined))

    if len(seq_bits) == 3:
        seed_held = [net.swap(after(seed_grad, outs[0][0]), seq_bits[1])] + seed_held
    gradient = seed_grad.astype(F32)
    qkv_parts = [None] * layers
    out_parts = [None] * layers
    in_parts = [None] * layers
    down_parts = [None] * layers
    norm_parts = [None] * layers
    qk_parts = [None] * layers
    bias_parts = [None] * layers
    hidden_sums = [None] * layers
    attention_sums = [None] * layers
    sums, low = None, seed_grad
    for layer in reversed(range(layers)):
        final = layer + 1 == layers
        m_qkv, m_out, pack = weights[layer]
        layer_in, normed, mixed, gains, bias, kept, arrived, middle, second, joined = saved[layer]

        def backward(n, blocks, joined=joined, pack=pack, final=final, sums=sums):
            if n == 2 and not final:
                blocks = [after(blocks[0], hidden_sums[layer + 1])] + blocks[1:]
            grad_part, gated_part, parts = feed_backward(blocks, joined[n], pack)
            return [grad_part, gated_part] + parts

        held = seed_held if final and len(seq_bits) == 3 else None
        down_in, outs = wave(net, low, backward, held)
        grad_joined, gated = [out[0] for out in outs], [out[1] for out in outs]
        second_sum = SumAll(net, [part for out in outs for part in out[2:]])
        second_sum.step()
        moved = second_sum.moving
        second_sum.step()
        second_sum.step()
        parts = second_sum.parts()

        def weights_of(*earlier):
            first = after(grad_joined[0], *earlier)
            total = hidden_weights(net, second, [first] + grad_joined[1:], gated, down_in)
            hidden_sums[layer] = lax.psum_scatter(total, "dp", scatter_dimension=0, tiled=True)
            return total

        if final:
            final_sum.step(*moved)
            parts[0] = after(parts[0], *final_sum.moving)
        else:
            parts[0] = after(parts[0], weights_of(*second_sum.low))
        gradient, gain_second, leaving, shares = out_backward(
            net, gradient, parts, middle, norm_gains[layer, 1], m_out, arrived, rows_out
        )
        if final:
            final_sum.step(leaving[0])
        grad_heads = jnp.concatenate(net.trade(leaving, lo_bits), axis=0)
        share_sum = SumLo(net, [x.reshape(-1, width) for x in shares])
        share_sum.step()
        late = [weights_of(leaving[0])] if final else []
        grad_heads = after(grad_heads, *share_sum.moving, *late)
        out_sum = share_sum.parts()
        grad_query, grad_keys, grad_values, grad_gains, grad_pair = attend_backward(
            mixed, grad_heads, tables, gains, bias, kept
        )
        grad_query = after(grad_query, *share_sum.moving)
        grads = [grad_query, after(grad_keys, *final_sum.moving) if final else grad_keys, grad_values]
        if not final:
            other_sums = attention_sums[layer + 1]
            other_came = net.swap_hi(after(other_sums[1], leaving[0]))
            grads[2] = after(grad_values, other_came)
            total = other_sums[0].astype(F32) + other_came.astype(F32)
            qkv_parts[layer + 1], out_parts[layer + 1] = split_pieces(
                total, 3 * local_width, rows_out
            )
        last = layer == 0
        if not last:
            normed_sum = SumLo(net, mixed_backward(grads, m_qkv, rows))
            normed_sum.step()
            parts = normed_sum.parts()
            grads = [grads[0], after(grads[1], *normed_sum.low), grads[2]]
        mine, other = mixed_weights(net, normed, grads, out_sum, rows_out, F32 if last else BF)
        if last:
            sums = (mine, net.swap_hi(other))
        else:
            sent = [x.reshape(-1, x.shape[2]) for x in (mine, other)]
            attention_sums[layer] = [
                lax.psum_scatter(x, "dp", scatter_dimension=0, tiled=True) for x in sent
            ]
        if last:
            grads[0] = after(grads[0], other)
            normed_sum = SumLo(net, mixed_backward(grads, m_qkv, rows))
            normed_sum.step()
            parts = normed_sum.parts()
        else:
            parts[0] = after(parts[0], other)
        gradient, low, gain_first = norm_backward(
            gradient, parts, layer_in, norm_gains[layer, 0]
        )
        norm_parts[layer] = jnp.stack([gain_first, gain_second])
        qk_parts[layer] = grad_gains.reshape(-1, 2, 2, head_size).sum(axis=(0, 2))
        bias_parts[layer] = lax.dynamic_update_slice(
            jnp.zeros((2, heads), F32), grad_pair[:, 0, :2].T, (jnp.int32(0), head_start)
        )
    both = SumBoth(net, *sums)
    both.step()
    final_sum.step(low)
    qkv_parts[0], out_parts[0] = split_pieces(both.total(), 3 * local_width, rows_out)
    for layer in range(layers):
        in_parts[layer], down_parts[layer] = split_hidden(
            hidden_sums[layer], width // net.dp_n, width
        )
    qkv_parts = return_rows(qkv_parts, "lo", lo_n)
    in_parts = return_rows(in_parts, ("hi", "lo"), net.seq_n, qkv_parts)
    parts = final_sum.parts()
    low_state = (saved[-1][7] + sum(x.astype(F32) for x in parts)).astype(BF)
    layer_out = keep_own(low_state, net.swap_hi(low_state[tok_dev:]))
    input_grad = keep_own(low, net.swap_hi(low[tok_dev:])).astype(F32)
    tops = best_scores.size
    small = jnp.concatenate(
        [best_scores.reshape(-1)]
        + [jnp.stack(part).reshape(-1) for part in (norm_parts, qk_parts, bias_parts)]
    )
    small = after(small, *both.moving)
    is_top = jnp.arange(small.size) < tops
    small = net.all_small(small, lambda a, b: jnp.where(is_top, jnp.maximum(a, b), a + b))
    best_scores = small[:tops].reshape(best_scores.shape)
    small = small[tops:]
    cut_norm, cut_qk = norm_gains.size, norm_gains.size + qk_gains.size
    norm_sum = small[:cut_norm].reshape(norm_gains.shape)
    qk_sum = small[cut_norm:cut_qk].reshape(qk_gains.shape)
    bias_sum = small[cut_qk:].reshape(head_bias.shape)

    factor = jnp.sqrt(CLIP_LIMIT / jnp.maximum(best_scores, CLIP_LIMIT))
    spread = jnp.repeat(factor, head_size, axis=1)
    column_scale = jnp.concatenate([spread, spread, jnp.ones((layers, width), F32)], axis=1)
    clipped = (w_qkv.astype(F32) * column_scale[:, None, :]).astype(BF)
    return (
        layer_out,
        input_grad,
        merge_columns(qkv_parts, layers, local_width),
        jnp.stack(out_parts),
        merge_columns(in_parts, layers, unit),
        jnp.stack(down_parts),
        norm_sum,
        qk_sum,
        bias_sum,
        clipped,
        best_scores,
    )


def solution(mesh):
    def program(*arrays):
        dp_n = mesh.shape["dp"]
        sequences = arrays[0].shape[0] // dp_n
        split = Mesh(mesh.devices.reshape(dp_n, sequences, -1), ("dp", "hi", "lo"))
        seq = ("hi", "lo")
        tokens_spec = P("dp", seq, None)
        rows_spec = P(None, ("dp",) + seq, None)
        ids_spec = P("dp", seq)
        in_specs = (tokens_spec, ids_spec, ids_spec) + (rows_spec,) * 4 + (P(),) * 3
        in_specs += (tokens_spec,)
        out_specs = (tokens_spec,) * 2 + (rows_spec,) * 4 + (P(),) * 3 + (rows_spec, P())
        run = jax.shard_map(
            shards, mesh=split, in_specs=in_specs, out_specs=out_specs, check_vma=False
        )
        return run(*arrays)

    return program
```

```python
import functools
import math

import jax
import jax.numpy as jnp
from jax import lax
from jax.experimental import pallas as pl
from jax.experimental.pallas import tpu as pltpu
from jax.sharding import Mesh
from jax.sharding import PartitionSpec as P

EPSILON = 1e-05
CLIP_LIMIT = 2.0
FLOOR_VALUE = -1e30
BF = jnp.bfloat16
F32 = jnp.float32


def rms_scale(values, gain):
    return values * lax.rsqrt(jnp.mean(values * values, axis=-1, keepdims=True) + EPSILON) * gain


def dot(a, b):
    return jnp.dot(a, b, preferred_element_type=F32)


def pick(array, index, axis=0):
    return lax.dynamic_index_in_dim(array, index, axis, keepdims=False)


class Net:
    def __init__(self):
        self.dp_n, self.hi_n, self.lo_n = (lax.axis_size(name) for name in ("dp", "hi", "lo"))
        self.dp, self.hi, self.lo = (lax.axis_index(name) for name in ("dp", "hi", "lo"))
        self.seq_n = self.hi_n * self.lo_n
        self.seq = self.hi * self.lo_n + self.lo
        self.seq_bits = [1 << b for b in range(self.seq_n.bit_length() - 1)]
        self.lo_bits = [b for b in self.seq_bits if b < self.lo_n]
        self.hi_bits = [b // self.lo_n for b in self.seq_bits if b >= self.lo_n]

    def swap(self, x, bit):
        if bit < self.lo_n:
            return lax.ppermute(x, "lo", [(i, i ^ bit) for i in range(self.lo_n)])
        bit //= self.lo_n
        return lax.ppermute(x, "hi", [(i, i ^ bit) for i in range(self.hi_n)])

    def swap_hi(self, x):
        return self.swap(x, self.lo_n)

    def swap_dp(self, x, bit):
        return lax.ppermute(x, "dp", [(i, i ^ bit) for i in range(self.dp_n)])

    def shift_dp(self, blocks):
        n = self.dp_n
        return [
            lax.ppermute(x, "dp", [(i, (i + k + 1) % n) for i in range(n)])
            for k, x in enumerate(blocks)
        ]

    def gather(self, block, bits, held=None):
        blocks = {0: block}
        if held is not None:
            blocks[bits[-1]] = held
        for bit in reversed(bits):
            for r in list(blocks):
                if r & bit:
                    continue
                if r | bit in blocks:
                    continue
                blocks[r | bit] = self.swap(blocks[r], bit)
        return [blocks[r] for r in range(len(blocks))]

    def add_swapped(self, mine, sent, bit):
        return mine.astype(F32) + self.swap(sent.astype(BF), bit).astype(F32)

    def scatter(self, blocks, bits):
        blocks = dict(enumerate(blocks))
        for bit in bits:
            blocks = self.halve(blocks, bit)
        return blocks[0]

    def halve(self, blocks, bit):
        return {
            r: self.add_swapped(blocks[r], blocks[r | bit], bit)
            for r in sorted(blocks, reverse=True)
            if not r & bit
        }

    def trade(self, blocks, bits):
        return Trade(self, blocks, bits).finish()

    def all_small(self, x, combine):
        for bit in self.seq_bits:
            x = combine(x, self.swap(x, bit))
        bit = 1
        while bit < self.dp_n:
            x = combine(x, self.swap_dp(x, bit))
            bit *= 2
        return x


class Trade:
    def __init__(self, net, blocks, bits):
        self.net, self.blocks, self.left, self.moving = net, list(blocks), list(bits), []

    def step(self, *earlier):
        bit = self.left.pop()
        moving = [r for r in range(len(self.blocks)) if r & bit]
        if bit == 1:
            self.moving = [self.net.swap(after(self.blocks[r], *earlier), bit) for r in moving]
            for r, x in zip(moving, self.moving):
                self.blocks[r] = x
            return
        rows = self.blocks[0].shape[0]
        sent = after(jnp.concatenate([self.blocks[r] for r in moving], axis=0), *earlier)
        self.moving = [self.net.swap(sent, bit)]
        for n, r in enumerate(moving):
            self.blocks[r] = self.moving[0][n * rows : (n + 1) * rows]

    def finish(self):
        while self.left:
            self.step()
        return self.blocks


class SumAll:
    def __init__(self, net, blocks):
        self.net, self.blocks, self.moving, self.step_n = net, blocks, [], 0
        self.low = []

    def step(self, *earlier):
        net, bits = self.net, self.net.seq_bits
        self.step_n += 1
        if len(bits) != 3:
            if self.step_n == 1:
                self.blocks = [net.scatter(self.blocks, bits)]
            self.moving = []
            return
        core, first, second = bits
        half = self.blocks[0].shape[0] // 2
        if self.step_n == 1:
            order = (first | second, first, second, 0)
            self.moving = [net.swap(after(self.blocks[r | core], *earlier), core) for r in order]
            self.pairs = {r: [self.blocks[r], x] for r, x in zip(order, self.moving)}
        elif self.step_n == 2:
            top, bottom = add_low([self.pairs[first | second]], cut=half)
            self.moving = [
                net.swap(after(top, *earlier), first),
                net.swap(after(bottom, *earlier), second),
            ]
        else:
            top, bottom = (after(x, *earlier) for x in self.moving)
            self.low = add_low(
                [self.pairs[first], self.pairs[second]], [(half, bottom), (0, top)]
            )
            self.moving = [net.swap(x, bit) for x, bit in zip(self.low, (first, second))]

    def parts(self):
        while self.step_n < 3:
            self.step()
        return self.pairs[0] + self.moving if self.moving else self.blocks


class SumLo:
    def __init__(self, net, blocks):
        self.net, self.blocks = net, blocks

    def step(self, *earlier):
        net = self.net
        if len(net.lo_bits) != 2:
            self.left = [net.scatter(self.blocks, net.lo_bits)]
            self.moving, self.low = [], []
            return
        self.moving = [net.swap(after(self.blocks[r | 1], *earlier), 1) for r in (2, 0)]
        self.left = [self.blocks[0], self.moving[1]]

    def parts(self, *earlier):
        if self.moving:
            self.low = add_low([[self.blocks[2], self.moving[0]]])
            far = self.low[0]
            self.moving = [self.net.swap(after(far, *earlier), 2)]
        return self.left + self.moving


class GatherBoth:
    def __init__(self, net, own, *earlier):
        self.net, self.own = net, own
        own = after(own, *earlier)
        self.own_came = net.swap_hi(own)
        self.by_dp = net.shift_dp([own] * (net.dp_n - 1))
        self.moving = [self.own_came] + self.by_dp

    def step(self, *earlier):
        self.rest_came = self.net.swap_hi(after(jnp.concatenate(self.by_dp, axis=0), *earlier))
        self.moving = [self.rest_came]

    def finish(self):
        net = self.net
        rows, columns = self.own.shape
        n = net.dp_n

        def kernel(at, own, own_came, rest_came, *refs):
            *by_dp, out = refs
            dp, hi = at[0] // 2, at[0] % 2
            out[at[0]] = own[...]
            out[dp * 2 + 1 - hi] = own_came[...]
            for k in range(1, n):
                source = lax.rem(dp + n - k, n)
                out[source * 2 + hi] = by_dp[k - 1][...]
                out[source * 2 + 1 - hi] = rest_came[(k - 1) * rows : k * rows, :]

        return on_chip(
            kernel,
            [((2 * n, rows, columns), BF)],
            self.own,
            self.own_came,
            self.rest_came,
            *self.by_dp,
            at=net.dp * 2 + net.hi,
            name="join_gathered",
        )[0]


class SumBoth:
    def __init__(self, net, mine, came):
        n = net.dp_n

        def kernel(at, x, y, own, *outs):
            own[...] = x[at[0]] + y[at[0]].astype(F32)
            for k, out in enumerate(outs):
                to = lax.rem(at[0] + k + 1, n)
                out[...] = (x[to] + y[to].astype(F32)).astype(BF)

        shape = mine.shape[1:]
        self.own, *self.blocks = on_chip(
            kernel, [(shape, F32)] + [(shape, BF)] * (n - 1), mine, came, at=net.dp, name="sum_hi"
        )
        self.net = net

    def step(self, *earlier):
        self.blocks[0] = after(self.blocks[0], *earlier)
        self.moving = self.net.shift_dp(self.blocks)

    def total(self):
        return self.own + sum(x.astype(F32) for x in self.moving)


def after(x, *earlier):
    return lax.optimization_barrier((x,) + earlier)[0]


def in_order(blocks, index):
    stacked = jnp.stack(blocks)
    return jnp.stack([pick(stacked, index ^ j) for j in range(len(blocks))])


def split_columns(shard, count, width):
    rows = shard.shape[0]
    parts = shard.shape[1] // count // width
    if width % LANES:
        shard = shard.reshape(rows, parts, count, width).transpose(2, 0, 1, 3)
        return shard.reshape(count, rows, parts * width)

    def kernel(shard_ref, out):
        for r in range(count):
            for p in range(parts):
                start = (p * count + r) * width
                out[r, :, p * width : (p + 1) * width] = shard_ref[:, start : start + width]

    return on_chip(kernel, [((count, rows, parts * width), BF)], shard, name="split_columns")[0]


def merge_columns(blocks, layers, width):
    count, rows = blocks.shape[0], blocks.shape[1] // layers
    parts = blocks.shape[2] // width
    columns = parts * count * width
    if width % LANES:
        shards = blocks.reshape(count, layers, rows, parts, width).transpose(1, 2, 3, 0, 4)
        return shards.reshape(layers, rows, columns).astype(F32)

    def kernel(ref, out):
        for r in range(count):
            for layer in range(layers):
                for p in range(parts):
                    start = (p * count + r) * width
                    part = ref[r, layer * rows : (layer + 1) * rows, p * width : (p + 1) * width]
                    out[layer, :, start : start + width] = part.astype(F32)

    return on_chip(kernel, [((layers, rows, columns), F32)], blocks, name="merge_columns")[0]


def own_columns(blocks, layers):
    count, rows, columns = blocks.shape
    blocks = blocks.reshape(count, layers, rows // layers, columns)
    return [blocks[:, n].reshape(-1, columns) for n in range(layers)]


def return_rows(layers, axes, count, *earlier):
    own = jnp.stack([x.astype(BF).reshape(count, -1, x.shape[1]) for x in layers], axis=1)
    own = own.reshape(count, -1, own.shape[-1])
    return lax.all_to_all(after(own, *earlier), axes, 0, 0, tiled=True)


def join_pieces(own, other, axis):
    if axis == 1:
        pieces = jnp.split(other, own.shape[0] // other.shape[0], axis=1)
        return jnp.concatenate([own, jnp.concatenate(pieces, axis=0)], axis=1)
    return jnp.concatenate([own] + jnp.split(other, other.shape[1] // own.shape[1], axis=1))


def split_hidden(own, rows_in, width):
    pieces = width // own.shape[1]
    down = jnp.concatenate(jnp.split(own[rows_in:], pieces, axis=0), axis=1)
    return own[:rows_in], down.astype(F32)


LANES = 128
NT = (((1,), (1,)), ((), ()))
TN = (((0,), (0,)), ((), ()))
VMEM = pl.BlockSpec(memory_space=pltpu.VMEM)
SMEM = pl.BlockSpec(memory_space=pltpu.SMEM)
LIMIT = 16 * 2**20
WEIGHT_LIMIT = 32 * 2**20


def on_chip(kernel, outs, *arrays, at=None, scratch=(), flops=0, name=None):
    outs = [jax.ShapeDtypeStruct(*out) for out in outs]
    moved = sum(math.prod(x.shape) * x.dtype.itemsize for x in list(arrays) + outs)
    first = [] if at is None else [at.astype(jnp.int32).reshape(1)]
    return pl.pallas_call(
        kernel,
        in_specs=[SMEM] * len(first) + [VMEM] * len(arrays),
        out_specs=[VMEM] * len(outs),
        out_shape=outs,
        scratch_shapes=list(scratch),
        compiler_params=pltpu.CompilerParams(vmem_limit_bytes=LIMIT),
        cost_estimate=pl.CostEstimate(flops=flops, bytes_accessed=moved, transcendentals=0),
        name=name,
    )(*first, *arrays)


def add_low(groups, extras=None, cut=None):
    shape = groups[0][0].shape
    extras = extras or [None] * len(groups)
    flat, counts = [], []
    for group, extra in zip(groups, extras):
        members = group + ([extra[1]] if extra else [])
        counts.append(len(members))
        flat += members

    def kernel(*refs):
        ins, outs = list(refs[: len(flat)]), list(refs[len(flat) :])
        for count, extra in zip(counts, extras):
            members = [ins.pop(0) for _ in range(count)]
            last = members.pop() if extra else None
            total = sum(x[...].astype(F32) for x in members)
            if extra:
                rows = last.shape[0]
                part = total[extra[0] : extra[0] + rows] + last[...].astype(F32)
                pieces = [total[: extra[0]], part, total[extra[0] + rows :]]
                total = jnp.concatenate([p for p in pieces if p.shape[0]], axis=0)
            total = total.astype(BF)
            if cut is None:
                outs.pop(0)[...] = total
            else:
                outs.pop(0)[...] = total[:cut]
                outs.pop(0)[...] = total[cut:]

    if cut is None:
        shapes = [(shape, BF)] * len(groups)
    else:
        shapes = [((cut,) + shape[1:], BF), ((shape[0] - cut,) + shape[1:], BF)]
    return on_chip(kernel, shapes, *flat, name="add_low")


def finish_layer(middle, parts, gain):
    rows, width = middle.shape

    def kernel(x, g, *refs):
        *ins, state, normed = refs
        total = x[...] + sum(part[...].astype(F32) for part in ins)
        state[...] = total
        normed[...] = rms_scale(total, g[...]).astype(BF)

    outs = [((rows, width), F32), ((rows, width), BF)]
    return on_chip(kernel, outs, middle, gain.reshape(1, width), *parts, name="finish_layer")


def norm_backward(gradient, parts, values, gain):
    rows, width = gradient.shape

    def kernel(g, x, gn, *refs):
        *ins, new, low, gain_out = refs
        total = sum(part[...].astype(F32) for part in ins)
        grad, gain_part = norm_adjoint(x[...], gn[...], total)
        grad = g[...] + grad
        new[...] = grad
        low[...] = grad.astype(BF)
        gain_out[...] = gain_part

    outs = [((rows, width), F32), ((rows, width), BF), ((1, width), F32)]
    arrays = [gradient, values, gain.reshape(1, width)]
    new, low, gain_part = on_chip(kernel, outs, *arrays, *parts, name="norm_backward")
    return new, low, gain_part[0]


def norm_adjoint(values, gain, grad):
    inverse = lax.rsqrt(jnp.mean(values * values, axis=-1, keepdims=True) + EPSILON)
    normal = values * inverse
    gain_part = jnp.sum(grad * normal, axis=0, keepdims=True)
    grad = grad * gain
    grad = (grad - normal * jnp.mean(grad * normal, axis=-1, keepdims=True)) * inverse
    return grad, gain_part


def project(blocks, matrix, columns):
    rows = blocks[0].shape[0]

    def kernel(*refs):
        *ins, m, out = refs
        for n, x in enumerate(ins):
            out[n * rows : (n + 1) * rows, :] = dot(x[...], m[:, :columns]).astype(BF)

    return on_chip(
        kernel,
        [((rows * len(blocks), columns), BF)],
        *blocks,
        matrix,
        flops=2 * rows * len(blocks) * matrix.size,
        name="project",
    )[0]


def out_project(state, arrived, matrix, gain, at):
    rows, width = state.shape
    heads = arrived[0].shape[1]

    def kernel(index, x, m, g, *refs):
        *ins, middle, second = refs
        total = x[...]
        for r, block in enumerate(ins):
            start = pl.multiple_of((index[0] ^ r) * heads, heads)
            total = total + dot(block[...], m[pl.ds(start, heads), :])
        middle[...] = total
        second[...] = rms_scale(total, g[...]).astype(BF)

    return on_chip(
        kernel,
        [((rows, width), F32), ((rows, width), BF)],
        state,
        matrix,
        gain.reshape(1, width),
        *arrived,
        at=at,
        flops=2 * rows * matrix.size,
        name="out_project",
    )


def hidden_matrices(pack, width):
    rows = width // pack.shape[0]
    columns = pack.shape[2]
    down = (pack.shape[1] - rows) * columns // width
    m_in = jnp.concatenate([pack[n, :rows, :] for n in range(pack.shape[0])], axis=0)
    m_down = []
    for n in range(pack.shape[0]):
        starts = range(rows, pack.shape[1], down)
        m_down.append(jnp.concatenate([pack[n, p : p + down, :] for p in starts], axis=1))
    return m_in, jnp.concatenate(m_down, axis=0)


def feed_forward(blocks, pack):
    rows, width = blocks[0].shape
    count, hidden = len(blocks), pack.shape[2] // 2

    def kernel(*refs):
        m, ins, joined, outs = refs[0], refs[1 : count + 1], refs[count + 1], refs[count + 2 :]
        m_in, m_down = hidden_matrices(m, width)
        for n, (x, out) in enumerate(zip(ins, outs)):
            both = dot(x[...], m_in)
            joined[n * rows : (n + 1) * rows, :] = both.astype(BF)
            gate, up = both[:, :hidden], both[:, hidden:]
            gated = gate / (1.0 + jnp.exp(-gate)) * up
            out[...] = dot(gated.astype(BF), m_down).astype(BF)

    joined, *parts = on_chip(
        kernel,
        [((rows * count, 2 * hidden), BF)] + [((rows, width), BF)] * count,
        pack,
        *blocks,
        flops=2 * rows * count * pack.size,
        name="feed_forward",
    )
    return joined, parts


def feed_backward(blocks, joined, pack):
    rows, width = blocks[0].shape
    count, hidden = len(blocks), pack.shape[2] // 2

    def kernel(*refs):
        m, ins, (j, grad_joined, gated) = refs[0], refs[1 : count + 1], refs[count + 1 : count + 4]
        m_in, m_down = hidden_matrices(m, width)
        for n, (x, out) in enumerate(zip(ins, refs[count + 4 :])):
            part = slice(n * rows, (n + 1) * rows)
            gate = j[part, :hidden].astype(F32)
            up = j[part, hidden:].astype(F32)
            grad = lax.dot_general(x[...], m_down, NT, preferred_element_type=F32)
            sigmoid = 1.0 / (1.0 + jnp.exp(-gate))
            silu = gate * sigmoid
            gated[part, :] = (silu * up).astype(BF)
            grad_gate = grad * up * (sigmoid + silu * (1.0 - sigmoid))
            grad_joined[part, :hidden] = grad_gate.astype(BF)
            grad_joined[part, hidden:] = (grad * silu).astype(BF)
            total = lax.dot_general(grad_joined[part, :], m_in, NT, preferred_element_type=F32)
            out[...] = total.astype(BF)

    grad_joined, gated, *parts = on_chip(
        kernel,
        [((rows * count, 2 * hidden), BF), ((rows * count, hidden), BF)]
        + [((rows, width), BF)] * count,
        pack,
        *blocks,
        joined,
        flops=2 * rows * count * pack.size,
        name="feed_backward",
    )
    return grad_joined, gated, parts


def side_by_side(refs, scratch, sems, start=0):
    copies, column = [], 0
    for group in refs:
        row = 0
        for x in group:
            place = scratch.at[pl.ds(row, x.shape[0]), pl.ds(column, x.shape[1])]
            copies.append(pltpu.make_async_copy(x, place, sems.at[start + len(copies)]))
            row += x.shape[0]
        column += group[0].shape[1]
    return copies


def weight_call(kernel, outs, groups, shapes, at, flops, name):
    flat = [x for group in groups for column in group for x in column]
    outs = [jax.ShapeDtypeStruct(*out) for out in outs]
    moved = sum(math.prod(x.shape) * x.dtype.itemsize for x in flat + outs)

    def body(index, *refs):
        ins, refs = list(refs[: len(flat)]), refs[len(flat) :]
        results, scratch, sems = refs[: len(outs)], refs[len(outs) : -1], refs[-1]
        arrived, count = [], 0
        for group, target in zip(groups, scratch):
            taken = [[ins.pop(0) for x in column] for column in group]
            copies = side_by_side(taken, target, sems, count)
            count += len(copies)
            for copy in copies:
                copy.start()
            arrived.append(Arriving(copies, target))
        kernel(index, *arrived, *results)

    return pl.pallas_call(
        body,
        in_specs=[SMEM] + [pl.BlockSpec(memory_space=pl.ANY)] * len(flat),
        out_specs=[VMEM] * len(outs),
        out_shape=outs,
        scratch_shapes=[pltpu.VMEM(shape, BF) for shape in shapes]
        + [pltpu.SemaphoreType.DMA((len(flat),))],
        compiler_params=pltpu.CompilerParams(vmem_limit_bytes=WEIGHT_LIMIT),
        cost_estimate=pl.CostEstimate(flops=flops, bytes_accessed=moved, transcendentals=0),
        name=name,
    )(at.astype(jnp.int32).reshape(1), *flat)


class Arriving:
    def __init__(self, copies, ref):
        self.copies, self.ref = copies, ref

    def __getitem__(self, index):
        for copy in self.copies:
            copy.wait()
        self.copies = []
        return self.ref[index]


def hidden_weights(net, second, grad_joined, gated, grads):
    length = sum(x.shape[0] for x in second)
    width, columns, hidden = second[0].shape[1], grad_joined[0].shape[1], gated[0].shape[1]
    rows, down = width // net.dp_n, hidden // net.dp_n
    pieces = width // columns

    def kernel(index, a, b, c, d, out):
        for n in range(net.dp_n):
            left = a[:, n * rows : (n + 1) * rows]
            first = n * (rows + pieces * down)
            out[first : first + rows, :] = lax.dot_general(
                left, b[...], TN, preferred_element_type=F32
            ).astype(BF)
            left = c[:, n * down : (n + 1) * down]
            total = lax.dot_general(left, d[...], TN, preferred_element_type=F32).astype(BF)
            for p in range(pieces):
                start = first + rows + p * down
                out[start : start + down, :] = total[:, p * columns : (p + 1) * columns]

    return weight_call(
        kernel,
        [((net.dp_n * (rows + pieces * down), columns), BF)],
        [[second], [grad_joined], [gated], [grads]],
        [(length, width), (length, columns), (length, hidden), (length, width)],
        net.dp,
        2 * length * width * (columns + hidden),
        "hidden_weights",
    )[0]


def mixed_weights(net, normed, grads, shares, rows, kept):
    length, width = sum(x.shape[0] for x in normed), normed[0].shape[1]
    columns = sum(g.shape[1] for g in grads)
    chunk = width // net.dp_n // net.hi_n
    pieces = chunk // rows
    c = shares[0].shape[1] // pieces

    def kernel(index, a, b, *refs):
        *parts, mine, other = refs
        for n in range(net.dp_n * net.hi_n):
            left = a[:, n * chunk : (n + 1) * chunk]
            total = lax.dot_general(left, b[...], TN, preferred_element_type=F32)
            out = sum(part[n * rows : (n + 1) * rows, :].astype(F32) for part in parts)
            here = index[0] == n % net.hi_n

            def store(target, kind, n=n, total=total, out=out):
                target[n // net.hi_n, :, :columns] = total.astype(kind)
                for p in range(pieces):
                    cut = out[:, p * c : (p + 1) * c].astype(kind)
                    target[n // net.hi_n, p * rows : (p + 1) * rows, columns:] = cut

            pl.when(here)(lambda: store(mine, kept))
            pl.when(jnp.logical_not(here))(lambda: store(other, BF))

    shape = (net.dp_n, chunk, columns + c)
    flat = [x.astype(BF) for x in shares]
    return weight_call(
        kernel,
        [(shape, kept), (shape, BF)],
        [[normed], [[g] for g in grads]] + [[[x]] for x in flat],
        [(length, width), (length, columns)] + [x.shape for x in flat],
        net.hi,
        2 * length * width * columns,
        "mixed_weights",
    )


def split_pieces(own, columns, rows):
    pieces = own.shape[0] // rows
    return own[:, :columns], jnp.concatenate(jnp.split(own[:, columns:], pieces, axis=0), axis=1)


def out_backward(net, gradient, parts, middle, gain, matrix, arrived, rows_out):
    rows, width = gradient.shape
    count, heads = len(arrived), arrived[0].shape[1]
    groups = width // rows_out // count

    def kernel(index, g, mid, gn, *refs):
        sums, m, refs = refs[: len(parts)], refs[len(parts)], refs[len(parts) + 1 :]
        ins, (new, gain_out), refs = refs[:count], refs[count : count + 2], refs[count + 2 :]
        leaving, shares, scratch = refs[:count], refs[count : 2 * count], refs[2 * count]
        total = sum(part[...].astype(F32) for part in sums)
        grad, gain_out[...] = norm_adjoint(mid[...], gn[...], total)
        grad = g[...] + grad
        new[...] = grad
        branch = grad.astype(BF)
        for r in range(count):
            start = pl.multiple_of((index[0] ^ r) * heads, heads)
            leaving[r][...] = lax.dot_general(
                branch, m[pl.ds(start, heads), :], NT, preferred_element_type=F32
            ).astype(BF)
            block = lax.dot_general(ins[r][...], branch, TN, preferred_element_type=F32)
            scratch[pl.ds(pl.multiple_of(start // rows_out, heads // rows_out), heads // rows_out)] = (
                block.reshape(heads // rows_out, rows_out, width)
            )
        for r in range(count):
            for n in range(groups):
                shares[r][n] = scratch[n * count + (index[0] ^ r)].astype(BF)

    outs = on_chip(
        kernel,
        [((rows, width), F32), ((1, width), F32)]
        + [((rows, heads), BF)] * count
        + [((groups, rows_out, width), BF)] * count,
        gradient,
        middle,
        gain.reshape(1, width),
        *parts,
        matrix,
        *arrived,
        at=net.lo,
        scratch=[pltpu.VMEM((width // rows_out, rows_out, width), F32)],
        flops=4 * rows * matrix.size,
        name="out_backward",
    )
    return outs[0], outs[1][0], outs[2 : 2 + count], outs[2 + count :]


def mixed_backward(grads, matrix, rows):
    length = grads[0].shape[0]
    count = length // rows
    width = grads[0].shape[1]

    def kernel(q, k, v, m, *outs):
        for n, out in enumerate(outs):
            part = slice(n * rows, (n + 1) * rows)
            x = jnp.concatenate([q[part, :], k[part, :], v[part, :]], axis=1)
            out[...] = lax.dot_general(
                x, m[:, : 3 * width], NT, preferred_element_type=F32
            ).astype(BF)

    return on_chip(
        kernel,
        [((rows, matrix.shape[0]), BF)] * count,
        *grads,
        matrix,
        flops=2 * length * matrix.size,
        name="mixed_backward",
    )


def join_middle(blocks, index, rows):
    n, stacked, c = blocks[0].shape
    count, pieces = len(blocks), stacked // rows
    if rows % 16:
        full = in_order(blocks, index).reshape(count, n, pieces, rows, c)
        return full.transpose(1, 0, 3, 2, 4).reshape(-1, pieces * c)

    def kernel(at, *refs):
        for r, block in enumerate(refs[:-1]):
            for i in range(n):
                start = pl.multiple_of((i * count + (at[0] ^ r)) * rows, rows)
                for p in range(pieces):
                    refs[-1][pl.ds(start, rows), p * c : (p + 1) * c] = block[
                        i, p * rows : (p + 1) * rows, :
                    ]

    shape = (n * count * rows, pieces * c)
    return on_chip(kernel, [(shape, BF)], *blocks, at=index, name="join_middle")[0]


def lane_ids():
    return lax.broadcasted_iota(jnp.int32, (1, LANES), 1)


def three_parts(x):
    hi = x.astype(BF).astype(F32)
    mid = (x - hi).astype(BF).astype(F32)
    return hi, mid, x - hi - mid


def group_sum(x, width):
    rows = lax.broadcasted_iota(jnp.int32, (LANES, LANES), 0) // width
    columns = lax.broadcasted_iota(jnp.int32, (LANES, LANES), 1) // width
    ones = jnp.where(rows == columns, 1.0, 0.0).astype(BF)
    return sum(dot(part.astype(BF), ones) for part in three_parts(x))


def swap_halves(x, half):
    front = (lane_ids() // half) % 2 == 0
    return jnp.where(front, pltpu.roll(x, LANES - half, 1), pltpu.roll(x, half, 1))


def head_prep(raw, gain, cosine, sine, width):
    raw = raw.astype(F32)
    inverse = lax.rsqrt(group_sum(raw * raw, width) * (1.0 / width) + EPSILON)
    scaled = raw * inverse * gain
    return scaled * cosine + swap_halves(scaled, width // 2) * sine, inverse


def attend_kernel(
    rows, query_in, key_in, value_in, cosine, sine, marks, gains, bias, attended, kept, tops
):
    length = query_in.shape[0]
    width = LANES // 2
    low = lane_ids() < width
    query, unused = head_prep(query_in[...], gains[0:1, :], cosine[...], sine[...], width)
    keys, unused = head_prep(key_in[...], gains[1:2, :], cosine[...], sine[...], width)
    query = query * (1.0 / math.sqrt(width))
    mark = marks[...].astype(F32)
    value = value_in[...].astype(F32)
    heads = []
    for h in range(2):
        shift = (lambda x: pltpu.roll(x, width, 1)) if h else (lambda x: x)
        heads.append(
            (
                jnp.where(low, shift(query), mark * bias[0, h : h + 1, :]).astype(BF),
                jnp.where(low, shift(keys), mark).astype(BF),
                jnp.where(low, shift(value), 1.0).astype(BF),
            )
        )
    best = [None, None]
    for start in range(0, length, rows):
        part = slice(start, start + rows)
        outs = []
        for h, (head_query, head_keys, head_value) in enumerate(heads):
            scores = lax.dot_general(head_query[part], head_keys, NT, preferred_element_type=F32)
            top = jnp.max(scores, axis=0, keepdims=True)
            best[h] = top if best[h] is None else jnp.maximum(best[h], top)
            mixed = dot(jnp.exp(scores).astype(BF), head_value)
            out = jnp.where(low, mixed / pltpu.roll(mixed, width, 1), jnp.log(mixed))
            kept[h, part, :] = out
            outs.append(out)
        attended[part, :] = jnp.where(low, outs[0], pltpu.roll(outs[1], width, 1)).astype(BF)
    for h in range(2):
        tops[h, :, :] = jnp.broadcast_to(jnp.max(best[h], axis=1, keepdims=True), (8, LANES))


def attend_backward_kernel(
    columns,
    query_in,
    key_in,
    value_in,
    grad_in,
    cosine,
    sine,
    marks,
    gains,
    bias,
    kept,
    grad_query,
    grad_key,
    grad_value,
    grad_gains,
    grad_bias,
    keys_turned,
    sum_keys,
    sum_values,
):
    length = query_in.shape[0]
    width = LANES // 2
    lane = lane_ids()
    low = lane < width
    scale = 1.0 / math.sqrt(width)
    query, query_inverse = head_prep(query_in[...], gains[0:1, :], cosine[...], sine[...], width)
    keys, key_inverse = head_prep(key_in[...], gains[1:2, :], cosine[...], sine[...], width)
    query = query * scale
    mark = marks[...].astype(F32)
    value = value_in[...].astype(F32)
    grads = grad_in[...].astype(F32)

    def place(x, first, other):
        for offset, part in enumerate(three_parts(x)):
            other = jnp.where(lane == first + offset, part, other)
        return other

    all_query, all_keys, all_values = [], [], []
    for h in range(2):
        shift = (lambda x: pltpu.roll(x, width, 1)) if h else (lambda x: x)
        out = kept[h]
        query_marks = place(-out, width + 12, mark * bias[0, h : h + 1, :])
        head_query = jnp.where(low, shift(query), query_marks).astype(BF)
        head_keys = jnp.where(low, shift(keys), mark).astype(BF)
        ones = jnp.where(lane < width + 3, 1.0, 0.0)
        head_value = jnp.where(low, shift(value), ones).astype(BF)
        head_grad = jnp.where(low, shift(grads), 0.0)
        inner = pltpu.roll(-group_sum(head_grad * out, width), width, 1)
        head_grad = place(inner, width, head_grad).astype(BF)
        keys_turned[...] = head_keys.astype(F32).T.astype(BF)
        turned = []
        for start in range(0, length, columns):
            part = slice(start, start + columns)
            scores = lax.dot_general(head_keys, head_query[part], NT, preferred_element_type=F32)
            probability = jnp.exp(scores)
            grad_prob = lax.dot_general(
                head_value, head_grad[part], NT, preferred_element_type=F32
            )
            grad_scores = (probability * grad_prob).astype(BF)
            part_values = dot(probability.astype(BF), head_grad[part])
            part_keys = dot(grad_scores, head_query[part])
            if start:
                sum_values[...] += part_values
                sum_keys[...] += part_keys
            else:
                sum_values[...] = part_values
                sum_keys[...] = part_keys
            turned.append(dot(keys_turned[...], grad_scores).T)
        head_sum = jnp.concatenate(turned, axis=0)
        equal = jnp.where((lane >= width) & (lane < width + 4), mark, 0.0)
        match = jnp.sum(jnp.sum(head_sum * equal, axis=0, keepdims=True), axis=1, keepdims=True)
        total = jnp.sum(
            jnp.where(lane == width + 12, jnp.sum(head_sum, axis=0, keepdims=True), 0.0),
            axis=1,
            keepdims=True,
        )
        both = jnp.where(lane == 0, match, total - match)
        grad_bias[h, :, :] = jnp.broadcast_to(both, (8, LANES))
        all_query.append(head_sum * scale)
        all_keys.append(sum_keys[...])
        all_values.append(sum_values[...])

    def join(pair):
        return jnp.where(low, pair[0], pltpu.roll(pair[1], width, 1))

    grad_value[...] = join(all_values).astype(BF)
    for n, (pair, raw, inverse, out) in enumerate(
        (
            (all_query, query_in, query_inverse, grad_query),
            (all_keys, key_in, key_inverse, grad_key),
        )
    ):
        grad = join(pair)
        grad = grad * cosine[...] - swap_halves(grad, width // 2) * sine[...]
        normal = raw[...].astype(F32) * inverse
        grad_gains[0, n : n + 1, :] = jnp.sum(grad * normal, axis=0, keepdims=True)
        grad = grad * gains[n : n + 1, :]
        mean = group_sum(grad * normal, width) * (1.0 / width)
        out[...] = ((grad - normal * mean) * inverse).astype(BF)


def lane_block(length, offset):
    return pl.BlockSpec((length, LANES), lambda i: (0, offset + i))


def whole_block(shape):
    return pl.BlockSpec(shape, lambda i: (0,) * len(shape))


def attend(mixed, tables, gains, bias):
    length, heads = mixed.shape[0], bias.shape[0]
    pairs = heads // 2
    block = lane_block
    return pl.pallas_call(
        functools.partial(attend_kernel, min(256, length)),
        grid=(pairs,),
        in_specs=[
            block(length, 0),
            block(length, pairs),
            block(length, 2 * pairs),
            whole_block((length, LANES)),
            whole_block((length, LANES)),
            whole_block((length, LANES)),
            whole_block((2, LANES)),
            pl.BlockSpec((1, 2, LANES), lambda i: (i, 0, 0)),
        ],
        out_specs=[
            block(length, 0),
            pl.BlockSpec((2, length, LANES), lambda i: (i, 0, 0)),
            pl.BlockSpec((2, 8, LANES), lambda i: (i, 0, 0)),
        ],
        out_shape=[
            jax.ShapeDtypeStruct((length, pairs * LANES), BF),
            jax.ShapeDtypeStruct((heads, length, LANES), F32),
            jax.ShapeDtypeStruct((heads, 8, LANES), F32),
        ],
        compiler_params=pltpu.CompilerParams(vmem_limit_bytes=16 * 2**10 * max(1024, length)),
        cost_estimate=pl.CostEstimate(
            flops=8 * heads * length * length * LANES,
            bytes_accessed=16 * length * pairs * LANES,
            transcendentals=heads * length * length,
        ),
        name="attend",
    )(mixed, mixed, mixed, *tables, gains, bias.reshape(pairs, 2, LANES))


def attend_backward(mixed, grad, tables, gains, bias, kept):
    length, heads = mixed.shape[0], bias.shape[0]
    pairs = heads // 2
    block = lane_block
    flat = jax.ShapeDtypeStruct((length, pairs * LANES), BF)
    return pl.pallas_call(
        functools.partial(attend_backward_kernel, min(256, length)),
        grid=(pairs,),
        in_specs=[
            block(length, 0),
            block(length, pairs),
            block(length, 2 * pairs),
            block(length, 0),
            whole_block((length, LANES)),
            whole_block((length, LANES)),
            whole_block((length, LANES)),
            whole_block((2, LANES)),
            pl.BlockSpec((1, 2, LANES), lambda i: (i, 0, 0)),
            pl.BlockSpec((2, length, LANES), lambda i: (i, 0, 0)),
        ],
        out_specs=[
            block(length, 0),
            block(length, 0),
            block(length, 0),
            pl.BlockSpec((1, 2, LANES), lambda i: (i, 0, 0)),
            pl.BlockSpec((2, 8, LANES), lambda i: (i, 0, 0)),
        ],
        out_shape=[
            flat,
            flat,
            flat,
            jax.ShapeDtypeStruct((pairs, 2, LANES), F32),
            jax.ShapeDtypeStruct((heads, 8, LANES), F32),
        ],
        scratch_shapes=[
            pltpu.VMEM((LANES, length), BF),
            pltpu.VMEM((length, LANES), F32),
            pltpu.VMEM((length, LANES), F32),
        ],
        compiler_params=pltpu.CompilerParams(vmem_limit_bytes=16 * 2**10 * max(1024, length)),
        cost_estimate=pl.CostEstimate(
            flops=20 * heads * length * length * LANES,
            bytes_accessed=24 * length * pairs * LANES,
            transcendentals=heads * length * length,
        ),
        name="attend_backward",
    )(mixed, mixed, mixed, grad, *tables, gains, bias.reshape(pairs, 2, LANES), kept)


def head_tables(ids, places, width):
    frequency = jnp.exp(jnp.arange(width // 2, dtype=F32) * (-2.0 * math.log(10000.0) / width))
    angles = places.astype(F32)[:, None] * frequency
    cosine, sine = jnp.cos(angles), jnp.sin(angles)
    lane = jnp.arange(LANES)[None, :]
    equal = (ids[:, None] == (lane - width) % 4) & (lane >= width) & (lane < width + 12)
    plain = (lane >= width + 12) & (lane < width + 15)
    return (
        jnp.concatenate([cosine] * 4, axis=1),
        jnp.concatenate([-sine, sine, -sine, sine], axis=1),
        (equal | plain).astype(BF),
    )


def bias_marks(pair, width):
    gap = pair[0] - pair[1]
    hi = lax.reduce_precision(gap, 8, 7)
    mid = lax.reduce_precision(gap - hi, 8, 7)
    lane = jnp.arange(LANES)[None, :]
    marks = jnp.zeros((pair.shape[1], LANES), F32)
    for n, part in enumerate((hi, mid, gap - hi - mid)):
        inside = (lane >= width + 4 * n) & (lane < width + 4 * n + 4)
        marks = jnp.where(inside, part[:, None], marks)
    return marks


def wave(net, own, compute, held=None):
    bits = net.seq_bits
    if len(bits) != 3:
        blocks = net.gather(own, bits)
        cuts = (blocks[: len(blocks) // 2], blocks[len(blocks) // 2 :])
        return blocks, [compute(n, cut) for n, cut in enumerate(cuts)]
    core, first, second = bits
    half = own.shape[0] // 2
    if held is None:
        held = [net.swap(own, bit) for bit in (first, second)]
    by_core = net.swap(own, core)
    outs = [compute(0, [own, by_core])]
    by_first, by_second = (after(x, outs[0][0]) for x in held)
    corner = [net.swap(by_first[:half], second), net.swap(by_second[half:], first)]
    blocks = [own, by_core, by_first, net.swap(by_first, core)]
    blocks += [by_second, net.swap(by_second, core)]
    outs.append(compute(1, blocks[2:6]))
    corner = jnp.concatenate([after(x, outs[1][0]) for x in corner], axis=0)
    blocks += [corner, net.swap(corner, core)]
    outs.append(compute(2, blocks[6:]))
    return blocks, outs


def shards(
    tokens,
    variate_ids,
    time_ids,
    w_qkv,
    w_out,
    w_in,
    w_down,
    norm_gains,
    qk_gains,
    head_bias,
    cotangent,
):
    sequences, tok_dev, width = tokens.shape
    layers = w_qkv.shape[0]
    heads = head_bias.shape[2]
    head_size = qk_gains.shape[2]
    net = Net()
    lo_n, lo_bits, seq_bits = net.lo_n, net.lo_bits, net.seq_bits
    rows = sequences * tok_dev
    local_heads = heads // lo_n
    local_width = local_heads * head_size
    head_start = net.lo * local_heads
    unit = w_down.shape[1]
    rows_out = w_out.shape[1]

    def to_groups(x):
        return jnp.concatenate([pick(x, net.hi), net.swap_hi(pick(x, 1 - net.hi))], axis=0)

    def keep_own(x, came):
        return in_order([x[:tok_dev], came], net.hi)

    qkv_blocks = split_columns(w_qkv.reshape(-1, 3 * width), lo_n, local_width)
    qkv_came = lax.all_to_all(qkv_blocks, "lo", 0, 0, tiled=True)
    token_parts = after(tokens, qkv_blocks)
    tokens_came = net.swap_hi(pick(token_parts, 1 - net.hi))
    state = jnp.concatenate([pick(token_parts, net.hi), tokens_came], axis=0).astype(F32)
    flat_in = after(w_in.reshape(-1, w_in.shape[2]), qkv_blocks)
    in_blocks = split_columns(flat_in, net.seq_n, unit)
    in_came = lax.all_to_all(in_blocks, ("hi", "lo"), 0, 0, tiled=True)
    own_qkv = own_columns(qkv_came, layers)
    ring = GatherBoth(net, join_pieces(own_qkv[0], w_out[0], 1))
    normed = rms_scale(state, norm_gains[0, 0]).astype(BF)
    normed_held = net.swap(normed, lo_bits[-1])
    ring.step()
    first_full = ring.finish()
    own_in = own_columns(in_came, layers)
    own_packs = [join_pieces(own_in[n], w_down[n], 0) for n in range(layers)]
    pair = to_groups(jnp.stack([variate_ids, time_ids], axis=-1))
    pairs = net.gather(pair, lo_bits)
    early = (*ring.by_dp, ring.own_came, tokens_came, normed_held, pairs[-1])
    packs = [lax.all_gather(after(own_packs[0], *early), "dp", axis=0)]

    pair = jnp.concatenate(pairs, axis=0)
    tables = head_tables(pair[:, 0], pair[:, 1], head_size)

    def matrices(full):
        full = full.reshape((-1, own_qkv[0].shape[0]) + full.shape[2:])
        blocks = net.gather(full[:, :, 3 * local_width :], lo_bits)
        return full.reshape(-1, full.shape[2]), join_middle(blocks, net.lo, rows_out)

    saved, weights = [], []
    best_scores = jnp.full((layers, heads), FLOOR_VALUE, F32)
    for layer in range(layers):
        final = layer + 1 == layers
        weights.append(matrices(full_next if layer else first_full) + (packs[layer],))
        m_qkv, m_out, pack = weights[layer]
        ring = None
        layer_in = state
        blocks = net.gather(normed, lo_bits, None if layer else normed_held)
        taken = blocks
        if final:
            seed_grad = jnp.concatenate([pick(cotangent, net.hi), seed_came], axis=0)
            seed_held = [net.swap(after(seed_grad, blocks[0]), seq_bits[-1])]
            taken = [after(blocks[0], *seed_held)] + blocks[1:]
        mixed = project(taken, m_qkv, 3 * local_width)
        if not final:
            own_next = join_pieces(own_qkv[layer + 1], w_out[layer + 1], 1)
            came_next = net.swap_hi(after(own_next, first_full))
        if layer == 0:
            seed_came = net.swap_hi(pick(after(cotangent, came_next), 1 - net.hi))
        bias_pair = lax.dynamic_slice_in_dim(head_bias[layer], head_start, local_heads, 1)
        gains = jnp.concatenate([qk_gains[layer]] * 2, axis=1)
        bias = bias_marks(bias_pair, head_size)
        attended, kept, head_tops = attend(mixed, tables, gains, bias)
        head_tops = head_tops[:, 0, 0] + bias_pair[1]
        best_scores = lax.dynamic_update_slice(
            best_scores, head_tops[None, :], (jnp.int32(layer), head_start)
        )
        leaving = attended if final else after(attended, came_next)
        arrived = net.trade(jnp.split(leaving, lo_n, axis=0), lo_bits)
        if layer == 0:
            arrived[0] = after(arrived[0], seed_came)
        if not final:
            own_next = in_order([own_next, came_next], net.hi).reshape(-1, own_next.shape[1])
            full_next = lax.all_gather(own_next, "dp", axis=0, tiled=True)
            full_next = full_next.reshape((net.dp_n * 2, -1) + full_next.shape[1:])
        middle, second = out_project(layer_in, arrived, m_out, norm_gains[layer, 1], net.lo)
        if not final:
            packs.append(lax.all_gather(after(own_packs[layer + 1], second), "dp", axis=0))

        def forward(n, blocks, pack=pack):
            joined, parts = feed_forward(blocks, pack)
            return [joined] + parts

        second, outs = wave(net, second, forward)
        joined = [out[0] for out in outs]
        partial = [part for out in outs for part in out[1:]]
        if final:
            final_sum = SumAll(net, partial)
        else:
            parts = SumAll(net, partial).parts()
            state, normed = finish_layer(middle, parts, norm_gains[layer + 1, 0])
        saved.append((layer_in, blocks, mixed, gains, bias, kept, arrived, middle, second, joined))

    if len(seq_bits) == 3:
        seed_held = [net.swap(after(seed_grad, outs[0][0]), seq_bits[1])] + seed_held
    gradient = seed_grad.astype(F32)
    qkv_parts = [None] * layers
    out_parts = [None] * layers
    in_parts = [None] * layers
    down_parts = [None] * layers
    norm_parts = [None] * layers
    qk_parts = [None] * layers
    bias_parts = [None] * layers
    hidden_sums = [None] * layers
    attention_sums = [None] * layers
    sums, low = None, seed_grad
    for layer in reversed(range(layers)):
        final = layer + 1 == layers
        m_qkv, m_out, pack = weights[layer]
        layer_in, normed, mixed, gains, bias, kept, arrived, middle, second, joined = saved[layer]

        def backward(n, blocks, joined=joined, pack=pack, final=final, sums=sums):
            if n == 2 and not final:
                blocks = [after(blocks[0], hidden_sums[layer + 1])] + blocks[1:]
            grad_part, gated_part, parts = feed_backward(blocks, joined[n], pack)
            return [grad_part, gated_part] + parts

        held = seed_held if final and len(seq_bits) == 3 else None
        down_in, outs = wave(net, low, backward, held)
        grad_joined, gated = [out[0] for out in outs], [out[1] for out in outs]
        second_sum = SumAll(net, [part for out in outs for part in out[2:]])
        second_sum.step()
        moved = second_sum.moving
        second_sum.step()
        second_sum.step()
        parts = second_sum.parts()

        def weights_of(*earlier):
            first = after(grad_joined[0], *earlier)
            total = hidden_weights(net, second, [first] + grad_joined[1:], gated, down_in)
            hidden_sums[layer] = lax.psum_scatter(total, "dp", scatter_dimension=0, tiled=True)
            return total

        if final:
            final_sum.step(*moved)
            parts[0] = after(parts[0], *final_sum.moving)
        else:
            parts[0] = after(parts[0], weights_of(*second_sum.low))
        gradient, gain_second, leaving, shares = out_backward(
            net, gradient, parts, middle, norm_gains[layer, 1], m_out, arrived, rows_out
        )
        if final:
            final_sum.step(leaving[0])
        grad_heads = jnp.concatenate(net.trade(leaving, lo_bits), axis=0)
        share_sum = SumLo(net, [x.reshape(-1, width) for x in shares])
        share_sum.step()
        late = [weights_of(leaving[0])] if final else []
        grad_heads = after(grad_heads, *share_sum.moving, *late)
        out_sum = share_sum.parts()
        grad_query, grad_keys, grad_values, grad_gains, grad_pair = attend_backward(
            mixed, grad_heads, tables, gains, bias, kept
        )
        grad_query = after(grad_query, *share_sum.moving)
        grads = [grad_query, after(grad_keys, *final_sum.moving) if final else grad_keys, grad_values]
        if not final:
            other_sums = attention_sums[layer + 1]
            other_came = net.swap_hi(after(other_sums[1], leaving[0]))
            grads[2] = after(grad_values, other_came)
            total = other_sums[0].astype(F32) + other_came.astype(F32)
            qkv_parts[layer + 1], out_parts[layer + 1] = split_pieces(
                total, 3 * local_width, rows_out
            )
        last = layer == 0
        if not last:
            normed_sum = SumLo(net, mixed_backward(grads, m_qkv, rows))
            normed_sum.step()
            parts = normed_sum.parts()
            grads = [grads[0], after(grads[1], *normed_sum.low), grads[2]]
        mine, other = mixed_weights(net, normed, grads, out_sum, rows_out, F32 if last else BF)
        if last:
            sums = (mine, net.swap_hi(other))
        else:
            sent = [x.reshape(-1, x.shape[2]) for x in (mine, other)]
            attention_sums[layer] = [
                lax.psum_scatter(x, "dp", scatter_dimension=0, tiled=True) for x in sent
            ]
        if last:
            grads[0] = after(grads[0], other)
            normed_sum = SumLo(net, mixed_backward(grads, m_qkv, rows))
            normed_sum.step()
            parts = normed_sum.parts()
        else:
            parts[0] = after(parts[0], other)
        gradient, low, gain_first = norm_backward(
            gradient, parts, layer_in, norm_gains[layer, 0]
        )
        norm_parts[layer] = jnp.stack([gain_first, gain_second])
        qk_parts[layer] = grad_gains.reshape(-1, 2, 2, head_size).sum(axis=(0, 2))
        bias_parts[layer] = lax.dynamic_update_slice(
            jnp.zeros((2, heads), F32), grad_pair[:, 0, :2].T, (jnp.int32(0), head_start)
        )
    both = SumBoth(net, *sums)
    both.step()
    final_sum.step(low)
    qkv_parts[0], out_parts[0] = split_pieces(both.total(), 3 * local_width, rows_out)
    for layer in range(layers):
        in_parts[layer], down_parts[layer] = split_hidden(
            hidden_sums[layer], width // net.dp_n, width
        )
    qkv_parts = return_rows(qkv_parts, "lo", lo_n)
    in_parts = return_rows(in_parts, ("hi", "lo"), net.seq_n, qkv_parts)
    parts = final_sum.parts()
    low_state = (saved[-1][7] + sum(x.astype(F32) for x in parts)).astype(BF)
    layer_out = keep_own(low_state, net.swap_hi(low_state[tok_dev:]))
    input_grad = keep_own(low, net.swap_hi(low[tok_dev:])).astype(F32)
    tops = best_scores.size
    small = jnp.concatenate(
        [best_scores.reshape(-1)]
        + [jnp.stack(part).reshape(-1) for part in (norm_parts, qk_parts, bias_parts)]
    )
    small = after(small, *both.moving)
    is_top = jnp.arange(small.size) < tops
    small = net.all_small(small, lambda a, b: jnp.where(is_top, jnp.maximum(a, b), a + b))
    best_scores = small[:tops].reshape(best_scores.shape)
    small = small[tops:]
    cut_norm, cut_qk = norm_gains.size, norm_gains.size + qk_gains.size
    norm_sum = small[:cut_norm].reshape(norm_gains.shape)
    qk_sum = small[cut_norm:cut_qk].reshape(qk_gains.shape)
    bias_sum = small[cut_qk:].reshape(head_bias.shape)

    factor = jnp.sqrt(CLIP_LIMIT / jnp.maximum(best_scores, CLIP_LIMIT))
    spread = jnp.repeat(factor, head_size, axis=1)
    column_scale = jnp.concatenate([spread, spread, jnp.ones((layers, width), F32)], axis=1)
    clipped = (w_qkv.astype(F32) * column_scale[:, None, :]).astype(BF)
    return (
        layer_out,
        input_grad,
        merge_columns(qkv_parts, layers, local_width),
        jnp.stack(out_parts),
        merge_columns(in_parts, layers, unit),
        jnp.stack(down_parts),
        norm_sum,
        qk_sum,
        bias_sum,
        clipped,
        best_scores,
    )


def solution(mesh):
    def program(*arrays):
        dp_n = mesh.shape["dp"]
        sequences = arrays[0].shape[0] // dp_n
        split = Mesh(mesh.devices.reshape(dp_n, sequences, -1), ("dp", "hi", "lo"))
        seq = ("hi", "lo")
        tokens_spec = P("dp", seq, None)
        rows_spec = P(None, ("dp",) + seq, None)
        ids_spec = P("dp", seq)
        in_specs = (tokens_spec, ids_spec, ids_spec) + (rows_spec,) * 4 + (P(),) * 3
        in_specs += (tokens_spec,)
        out_specs = (tokens_spec,) * 2 + (rows_spec,) * 4 + (P(),) * 3 + (rows_spec, P())
        run = jax.shard_map(
            shards, mesh=split, in_specs=in_specs, out_specs=out_specs, check_vma=False
        )
        return run(*arrays)

    return program
```
